32 devices in a mesh: dp: 8 (over z, x), bn: 4 (over y, core).
Axes of the slice: x: 2, y: 2, z: 4, core: 2. Of those that a mesh axis runs over, the one named last changes fastest.
Arguments:
- images_coarse: bfloat16 [128, 10, 10, 1024], P(('dp', 'bn')), may hold values from -6 to 6
- images_medium: bfloat16 [64, 14, 14, 1024], P(('dp', 'bn')), may hold values from -6 to 6
- images_fine: bfloat16 [64, 18, 18, 1024], P(('dp', 'bn')), may hold values from -6 to 6
- live_coarse: int32 [128], replicated, may hold values from 0 to 1, as said below
- live_medium: int32 [64], replicated, may hold values from 0 to 1, as said below
- live_fine: int32 [64], replicated, may hold values from 0 to 1, as said below
- upstream_coarse: bfloat16 [128, 5, 5, 2048], P(('dp', 'bn')), may hold values from -6 to 6
- upstream_medium: bfloat16 [64, 7, 7, 2048], P(('dp', 'bn')), may hold values from -6 to 6
- upstream_fine: bfloat16 [64, 9, 9, 2048], P(('dp', 'bn')), may hold values from -6 to 6
- reduce_proj: float32 [1024, 512], P(('dp', 'bn')), may hold values from -0.1875 to 0.1875
- spatial_proj: float32 [4608, 512], P(('dp', 'bn')), may hold values from -0.09375 to 0.09375
- expand_proj: float32 [512, 2048], P(None, ('dp', 'bn')), may hold values from -0.25 to 0.25
- shortcut_proj: float32 [1024, 2048], P(None, ('dp', 'bn')), may hold values from -0.1875 to 0.1875
- reduce_ident: float32 [2048, 512], P(('dp', 'bn')), may hold values from -0.125 to 0.125
- spatial_ident: float32 [4608, 512], P(('dp', 'bn')), may hold values from -0.09375 to 0.09375
- expand_ident: float32 [512, 2048], P(None, ('dp', 'bn')), may hold values from -0.25 to 0.25
- norm_params: float32 [16384], P(('dp', 'bn')), may hold values from -0.6 to 1.4
- mean_reduce_proj: float32 [1024, 512], P(('dp', 'bn')), may hold values from -450.7913 to 450.7913
- mean_spatial_proj: float32 [4608, 512], P(('dp', 'bn')), may hold values from -418.59192 to 418.59192
- mean_expand_proj: float32 [512, 2048], P(None, ('dp', 'bn')), may hold values from -193.19627 to 193.19627
- mean_shortcut_proj: float32 [1024, 2048], P(None, ('dp', 'bn')), may hold values from -209.29596 to 209.29596
- mean_reduce_ident: float32 [2048, 512], P(('dp', 'bn')), may hold values from -386.39255 to 386.39255
- mean_spatial_ident: float32 [4608, 512], P(('dp', 'bn')), may hold values from -386.39255 to 386.39255
- mean_expand_ident: float32 [512, 2048], P(None, ('dp', 'bn')), may hold values from -193.19627 to 193.19627
- mean_norm_params: float32 [16384], P(('dp', 'bn')), may hold values from -321.99377 to 321.99377
- square_reduce_proj: float32 [1024, 512], P(('dp', 'bn')), may hold values from 22579.2 to 90316.8
- square_spatial_proj: float32 [4608, 512], P(('dp', 'bn')), may hold values from 19468.8 to 77875.2
- square_expand_proj: float32 [512, 2048], P(None, ('dp', 'bn')), may hold values from 4147.2 to 16588.8
- square_shortcut_proj: float32 [1024, 2048], P(None, ('dp', 'bn')), may hold values from 4838.4 to 19468.8
- square_reduce_ident: float32 [2048, 512], P(('dp', 'bn')), may hold values from 16588.8 to 66355.2
- square_spatial_ident: float32 [4608, 512], P(('dp', 'bn')), may hold values from 16588.8 to 66355.2
- square_expand_ident: float32 [512, 2048], P(None, ('dp', 'bn')), may hold values from 4147.2 to 16588.8
- square_norm_params: float32 [16384], P(('dp', 'bn')), may hold values from 11520 to 46080
Outputs:
- output_coarse: bfloat16 [128, 5, 5, 2048], P(('dp', 'bn'))
- output_medium: bfloat16 [64, 7, 7, 2048], P(('dp', 'bn'))
- output_fine: bfloat16 [64, 9, 9, 2048], P(('dp', 'bn'))
- grad_coarse: bfloat16 [128, 10, 10, 1024], P(('dp', 'bn'))
- grad_medium: bfloat16 [64, 14, 14, 1024], P(('dp', 'bn'))
- grad_fine: bfloat16 [64, 18, 18, 1024], P(('dp', 'bn'))
- next_reduce_proj: float32 [1024, 512], P(('dp', 'bn'))
- next_mean_reduce_proj: float32 [1024, 512], P(('dp', 'bn'))
- next_square_reduce_proj: float32 [1024, 512], P(('dp', 'bn'))
- next_spatial_proj: float32 [4608, 512], P(('dp', 'bn'))
- next_mean_spatial_proj: float32 [4608, 512], P(('dp', 'bn'))
- next_square_spatial_proj: float32 [4608, 512], P(('dp', 'bn'))
- next_expand_proj: float32 [512, 2048], P(None, ('dp', 'bn'))
- next_mean_expand_proj: float32 [512, 2048], P(None, ('dp', 'bn'))
- next_square_expand_proj: float32 [512, 2048], P(None, ('dp', 'bn'))
- next_shortcut_proj: float32 [1024, 2048], P(None, ('dp', 'bn'))
- next_mean_shortcut_proj: float32 [1024, 2048], P(None, ('dp', 'bn'))
- next_square_shortcut_proj: float32 [1024, 2048], P(None, ('dp', 'bn'))
- next_reduce_ident: float32 [2048, 512], P(('dp', 'bn'))
- next_mean_reduce_ident: float32 [2048, 512], P(('dp', 'bn'))
- next_square_reduce_ident: float32 [2048, 512], P(('dp', 'bn'))
- next_spatial_ident: float32 [4608, 512], P(('dp', 'bn'))
- next_mean_spatial_ident: float32 [4608, 512], P(('dp', 'bn'))
- next_square_spatial_ident: float32 [4608, 512], P(('dp', 'bn'))
- next_expand_ident: float32 [512, 2048], P(None, ('dp', 'bn'))
- next_mean_expand_ident: float32 [512, 2048], P(None, ('dp', 'bn'))
- next_square_expand_ident: float32 [512, 2048], P(None, ('dp', 'bn'))
- next_norm_params: float32 [16384], P(('dp', 'bn'))
- next_mean_norm_params: float32 [16384], P(('dp', 'bn'))
- next_square_norm_params: float32 [16384], P(('dp', 'bn'))
The draws below stay inside these ranges and needn't reach their ends.
Inputs may be any that keep to these rules, and one draw needn't show every extreme that they name: `live_coarse`: 1 marks a slot that holds an image. On every device the live slots come first and its first slot is always live; in every draw some device has all of its slots live. `live_medium`: 1 marks a slot that holds an image. On every device the live slots come first and its first slot is always live; in every draw some device has all of its slots live. `live_fine`: 1 marks a slot that holds an image. On every device the live slots come first and its first slot is always live; in every draw some device has all of its slots live.
All inputs are finite; a program needn't handle non-finite values.
Results may differ from the reference program's by a relative error of at most 0.017.
The reference program's roundings to bfloat16 on the way count: a program that leaves them out, or rounds other values in their place, can miss the bound.
Values may be sent and summed in bfloat16 or wider, within the bound.
No kernel may reach another device: no remote copies, remote signals or barrier semaphores. Data moves between devices by JAX's collectives and lax.ppermute only.
A program may use at most 192 MiB of HBM per device.

```python
import math
import jax
import jax.numpy as jnp
from jax import lax

C_IN = 1024
C_MID = 512
C_OUT = 2048
GA = 5
GB = 7
GC = 9
IMG_DEV = 2
STEP = 10
IMAGES_A = 128
IMAGES_B = 64
IMAGES_C = 64
NORM_ALL = 16384
PIX_DEV = 360
N_DP = 8
DEVICES = 32


def live_slots(key, overall, per_owner):
    owners = overall // per_owner
    keep_count = jax.random.randint(jax.random.fold_in(key, 1), (owners,), 1, per_owner + 1)
    chosen = jax.random.randint(jax.random.fold_in(key, 2), (), 0, owners)
    keep_count = jnp.where(jnp.arange(owners) == chosen, per_owner, keep_count)
    position = jnp.arange(overall) % per_owner
    holder = jnp.arange(overall) // per_owner
    return (position < keep_count[holder]).astype(jnp.int32)


def draw_live_coarse(key, part):
    return live_slots(jax.random.fold_in(key, 101), IMAGES_A, 2 * IMG_DEV)


def draw_live_medium(key, part):
    return live_slots(jax.random.fold_in(key, 202), IMAGES_B, IMG_DEV)


def draw_live_fine(key, part):
    return live_slots(jax.random.fold_in(key, 303), IMAGES_C, IMG_DEV)


def draw_norm_params(key, part):
    halfway = NORM_ALL // 2
    gain_part = jax.random.uniform(jax.random.fold_in(key, 7), (halfway,), jnp.float32, 0.6, 1.4)
    bias_part = jax.random.uniform(jax.random.fold_in(key, 8), (halfway,), jnp.float32, -0.6, 0.6)
    return jnp.concatenate([gain_part, bias_part])


def strengthened(values, rng, source, target, blocks, factor):
    def block_of(dim):
        return (jnp.arange(values.shape[dim]) // (values.shape[dim] // blocks)).reshape((-1,) + (1,) * (values.ndim - 1 - dim))

    first = jax.random.permutation(rng, blocks)[block_of(target)]
    second = (block_of(target) + blocks // 2) % blocks
    return jnp.where((block_of(source) == first) | (block_of(source) == second), factor * values, values)


def steps_of(stream_key, shape, cuts, least, high):
    level = 1.0
    for dim, shards_of in cuts:
        heights = jax.random.uniform(jax.random.fold_in(jax.random.fold_in(stream_key, 6), dim), (shards_of,), jnp.float32, least / len(cuts), high / len(cuts))
        level = level * jnp.repeat(jnp.exp(heights), shape[dim] // shards_of).reshape((-1,) + (1,) * (len(shape) - 1 - dim))
    return level


def noise(key, extent, deviation, bound, split=(), dtype=jnp.bfloat16):
    array = jax.random.normal(key, extent, jnp.float32) * deviation
    if len(split) > 0:
        array = steps_of(key, extent, split, -0.22, 0.18) * array
    return jnp.clip(array, min=-bound, max=bound).astype(dtype)


def gaussian_with(stream_key, shape, width, most, pieces, heavy, dtype=jnp.bfloat16):
    drawn = width * jax.random.normal(stream_key, shape, jnp.float32)
    if pieces:
        drawn = drawn * steps_of(stream_key, shape, pieces, -0.22, 0.18)
    return jnp.clip(strengthened(drawn, jax.random.fold_in(stream_key, 3), *heavy), -most, most).astype(dtype)


def setup_inputs(seed: int = 0) -> dict:
    streams_of = jax.random.split(jax.random.key(seed), 34)
    images_coarse = noise(streams_of[0], (IMAGES_A, 2 * GA, 2 * GA, C_IN), 1.0, 6.0, ((0, 32),))
    images_medium = noise(streams_of[1], (IMAGES_B, 2 * GB, 2 * GB, C_IN), 1.0, 6.0, ((0, 32),))
    images_fine = noise(streams_of[2], (IMAGES_C, 2 * GC, 2 * GC, C_IN), 1.0, 6.0, ((0, 32),))
    live_coarse = draw_live_coarse(jax.random.fold_in(streams_of[33], 71), 0)
    live_medium = draw_live_medium(jax.random.fold_in(streams_of[33], 71), 0)
    live_fine = draw_live_fine(jax.random.fold_in(streams_of[33], 71), 0)
    upstream_coarse = gaussian_with(streams_of[6], (IMAGES_A, GA, GA, C_OUT), 1.0, 6.0, ((0, 32),), (0, 3, 32, 2.75))
    upstream_medium = gaussian_with(streams_of[7], (IMAGES_B, GB, GB, C_OUT), 1.0, 6.0, ((0, 32),), (0, 3, 32, 2.75))
    upstream_fine = gaussian_with(streams_of[8], (IMAGES_C, GC, GC, C_OUT), 1.0, 6.0, ((0, 32),), (0, 3, 32, 2.75))
    reduce_proj = noise(streams_of[9], (C_IN, C_MID), C_IN ** -0.5, 0.1875, ((0, 32),), jnp.float32)
    spatial_proj = noise(streams_of[10], (9 * C_MID, C_MID), (9 * C_MID) ** -0.5, 0.09375, ((0, 32),), jnp.float32)
    expand_proj = noise(streams_of[11], (C_MID, C_OUT), C_MID ** -0.5, 0.25, ((1, 32),), jnp.float32)
    shortcut_proj = noise(streams_of[12], (C_IN, C_OUT), C_IN ** -0.5, 0.1875, ((1, 32),), jnp.float32)
    reduce_ident = noise(streams_of[13], (C_OUT, C_MID), C_OUT ** -0.5, 0.125, ((0, 32),), jnp.float32)
    spatial_ident = noise(streams_of[14], (9 * C_MID, C_MID), (9 * C_MID) ** -0.5, 0.09375, ((0, 32),), jnp.float32)
    expand_ident = noise(streams_of[15], (C_MID, C_OUT), C_MID ** -0.5, 0.25, ((1, 32),), jnp.float32)
    norm_params = draw_norm_params(jax.random.fold_in(streams_of[33], 71), 0)
    mean_reduce_proj = noise(streams_of[17], (C_IN, C_MID), (1.4 * (PIX_DEV * DEVICES) ** 0.5), 450.7913, ((0, 32),), jnp.float32)
    mean_spatial_proj = noise(streams_of[18], (9 * C_MID, C_MID), (1.3 * (PIX_DEV * DEVICES) ** 0.5), 418.59192, ((0, 32),), jnp.float32)
    mean_expand_proj = noise(streams_of[19], (C_MID, C_OUT), (0.6 * (PIX_DEV * DEVICES) ** 0.5), 193.19627, ((1, 32),), jnp.float32)
    mean_shortcut_proj = noise(streams_of[20], (C_IN, C_OUT), (0.65 * (PIX_DEV * DEVICES) ** 0.5), 209.29596, ((1, 32),), jnp.float32)
    mean_reduce_ident = noise(streams_of[21], (C_OUT, C_MID), (1.2 * (PIX_DEV * DEVICES) ** 0.5), 386.39255, ((0, 32),), jnp.float32)
    mean_spatial_ident = noise(streams_of[22], (9 * C_MID, C_MID), (1.2 * (PIX_DEV * DEVICES) ** 0.5), 386.39255, ((0, 32),), jnp.float32)
    mean_expand_ident = noise(streams_of[23], (C_MID, C_OUT), (0.6 * (PIX_DEV * DEVICES) ** 0.5), 193.19627, ((1, 32),), jnp.float32)
    mean_norm_params = noise(streams_of[24], (NORM_ALL,), ((PIX_DEV * DEVICES) ** 0.5), 321.99377, ((0, 32),), jnp.float32)
    square_reduce_proj = jnp.clip(jnp.exp(math.log(90316.8) - 1.3862944 * jax.random.uniform(streams_of[25], (C_IN, C_MID), jnp.float32) ** steps_of(streams_of[25], (C_IN, C_MID), ((0, 32),), -0.2, 0.2)), 22579.2, 90316.8)
    square_spatial_proj = jnp.clip(jnp.exp(math.log(77875.2) - 1.3862944 * jax.random.uniform(streams_of[26], (9 * C_MID, C_MID), jnp.float32) ** steps_of(streams_of[26], (9 * C_MID, C_MID), ((0, 32),), -0.2, 0.2)), 19468.8, 77875.2)
    square_expand_proj = jnp.clip(jnp.exp(math.log(16588.8) - 1.3862944 * jax.random.uniform(streams_of[27], (C_MID, C_OUT), jnp.float32) ** steps_of(streams_of[27], (C_MID, C_OUT), ((1, 32),), -0.2, 0.2)), 4147.2, 16588.8)
    square_shortcut_proj = jnp.clip(jnp.exp(math.log(19468.8) - 1.3922292 * jax.random.uniform(streams_of[28], (C_IN, C_OUT), jnp.float32) ** steps_of(streams_of[28], (C_IN, C_OUT), ((1, 32),), -0.2, 0.2)), 4838.4, 19468.8)
    square_reduce_ident = jnp.clip(jnp.exp(math.log(66355.2) - 1.3862944 * jax.random.uniform(streams_of[29], (C_OUT, C_MID), jnp.float32) ** steps_of(streams_of[29], (C_OUT, C_MID), ((0, 32),), -0.2, 0.2)), 16588.8, 66355.2)
    square_spatial_ident = jnp.clip(jnp.exp(math.log(66355.2) - 1.3862944 * jax.random.uniform(streams_of[30], (9 * C_MID, C_MID), jnp.float32) ** steps_of(streams_of[30], (9 * C_MID, C_MID), ((0, 32),), -0.2, 0.2)), 16588.8, 66355.2)
    square_expand_ident = jnp.clip(jnp.exp(math.log(16588.8) - 1.3862944 * jax.random.uniform(streams_of[31], (C_MID, C_OUT), jnp.float32) ** steps_of(streams_of[31], (C_MID, C_OUT), ((1, 32),), -0.2, 0.2)), 4147.2, 16588.8)
    square_norm_params = jnp.clip(jnp.exp(math.log(46080.0) - 1.3862944 * jax.random.uniform(streams_of[32], (NORM_ALL,), jnp.float32) ** steps_of(streams_of[32], (NORM_ALL,), ((0, 32),), -0.2, 0.2)), 11520.0, 46080.0)
    return dict(images_coarse=images_coarse, images_medium=images_medium, images_fine=images_fine, live_coarse=live_coarse, live_medium=live_medium, live_fine=live_fine, upstream_coarse=upstream_coarse, upstream_medium=upstream_medium, upstream_fine=upstream_fine, reduce_proj=reduce_proj, spatial_proj=spatial_proj, expand_proj=expand_proj, shortcut_proj=shortcut_proj, reduce_ident=reduce_ident, spatial_ident=spatial_ident, expand_ident=expand_ident, norm_params=norm_params, mean_reduce_proj=mean_reduce_proj, mean_spatial_proj=mean_spatial_proj, mean_expand_proj=mean_expand_proj, mean_shortcut_proj=mean_shortcut_proj, mean_reduce_ident=mean_reduce_ident, mean_spatial_ident=mean_spatial_ident, mean_expand_ident=mean_expand_ident, mean_norm_params=mean_norm_params, square_reduce_proj=square_reduce_proj, square_spatial_proj=square_spatial_proj, square_expand_proj=square_expand_proj, square_shortcut_proj=square_shortcut_proj, square_reduce_ident=square_reduce_ident, square_spatial_ident=square_spatial_ident, square_expand_ident=square_expand_ident, square_norm_params=square_norm_params)


EPSILON = 1e-05
PRECISE = lax.Precision.HIGHEST
RATE_CONV = 0.03
RATE_NORM = 0.4
DECAY_CONV = 0.05

@jax.custom_vjp
def low(v):
    return lax.optimization_barrier(v.astype(jnp.bfloat16)).astype(jnp.float32)

@jax.custom_vjp
def low_back(v):
    return v

def low_keep(v):
    return (low(v), None)

def low_pass(kept, grad):
    return (grad,)

def back_keep(v):
    return (v, None)

def back_low(kept, grad):
    return (low(grad),)
low.defvjp(low_keep, low_pass)
low_back.defvjp(back_keep, back_low)

def split_norm(vector):
    widths = [C_MID, C_MID, C_OUT, C_OUT, C_MID, C_MID, C_OUT]
    halfway = NORM_ALL // 2
    paired = []
    offset = 0
    for section in widths:
        paired.append((vector[offset:offset + section], vector[halfway + offset:halfway + offset + section]))
        offset = offset + section
    return paired

def normalize(values, weight, counted, gain_bias):
    average = lax.optimization_barrier(jnp.sum(values * weight, axis=0)) / counted
    centred = values - average
    variance = lax.optimization_barrier(jnp.sum(centred * centred * weight, axis=0)) / counted
    return gain_bias[0] * centred * lax.rsqrt(variance + EPSILON) + gain_bias[1]

def matmul(left_side, right_side):
    return jnp.dot(left_side, right_side, precision=PRECISE, preferred_element_type=jnp.float32)

def conv_three(pictures, kernel, stride):
    shaped = kernel.reshape(3, 3, pictures.shape[3], kernel.shape[1])
    return lax.conv_general_dilated(pictures, shaped, (stride, stride), ((1, 1), (1, 1)), dimension_numbers=('NHWC', 'HWIO', 'NHWC'), precision=PRECISE, preferred_element_type=jnp.float32)

def blocks(params, pictures, alive_slots):
    lowered = [low(member) for member in params]
    w_reduce, w_spatial, w_expand, w_short, w_narrow, w_middle, w_widen, norm_vector = lowered
    paired = split_norm(norm_vector)
    number, in_side = (pictures.shape[0], pictures.shape[1])
    out_side = in_side // 2
    alive_mask = alive_slots.astype(jnp.float32)
    weight_in = jnp.repeat(alive_mask, in_side * in_side)[:, None]
    weight_out = jnp.repeat(alive_mask, out_side * out_side)[:, None]
    count_in = jnp.sum(alive_mask) * (in_side * in_side)
    count_out = jnp.sum(alive_mask) * (out_side * out_side)
    flat_input = pictures.reshape(-1, C_IN)
    conv_one = low_back(matmul(flat_input, w_reduce))
    act_one = low(jax.nn.silu(normalize(conv_one, weight_in, count_in, paired[0])))
    conv_two = low_back(conv_three(act_one.reshape(number, in_side, in_side, C_MID), w_spatial, 2).reshape(-1, C_MID))
    act_two = low(jax.nn.silu(normalize(conv_two, weight_out, count_out, paired[1])))
    conv_expand = low_back(matmul(act_two, w_expand))
    sub_flat = pictures[:, ::2, ::2, :].reshape(-1, C_IN)
    conv_short = low_back(matmul(sub_flat, w_short))
    hidden = jax.nn.silu(normalize(conv_expand, weight_out, count_out, paired[2]) + normalize(conv_short, weight_out, count_out, paired[3]))
    conv_four = low_back(matmul(low(hidden), w_narrow))
    act_four = low(jax.nn.silu(normalize(conv_four, weight_out, count_out, paired[4])))
    conv_five = low_back(conv_three(act_four.reshape(number, out_side, out_side, C_MID), w_middle, 1).reshape(-1, C_MID))
    act_five = low(jax.nn.silu(normalize(conv_five, weight_out, count_out, paired[5])))
    conv_six = low_back(matmul(act_five, w_widen))
    result = weight_out * jax.nn.silu(normalize(conv_six, weight_out, count_out, paired[6]) + hidden)
    return result.reshape(number, out_side, out_side, C_OUT)

def adam_step(weight, moment_one, moment_two, gradient, step_rate, decay_rate):
    first_new = 0.5 * moment_one + 0.5 * gradient
    second_new = 0.5 * moment_two + 0.5 * gradient * gradient
    correct = 1.0 - 0.5 ** STEP
    update = first_new / correct / (jnp.sqrt(second_new / correct) + 1e-08) + decay_rate * weight
    return (weight - step_rate * update, first_new, second_new)

def reference(images_coarse, images_medium, images_fine, live_coarse, live_medium, live_fine, upstream_coarse, upstream_medium, upstream_fine, reduce_proj, spatial_proj, expand_proj, shortcut_proj, reduce_ident, spatial_ident, expand_ident, norm_params, mean_reduce_proj, mean_spatial_proj, mean_expand_proj, mean_shortcut_proj, mean_reduce_ident, mean_spatial_ident, mean_expand_ident, mean_norm_params, square_reduce_proj, square_spatial_proj, square_expand_proj, square_shortcut_proj, square_reduce_ident, square_spatial_ident, square_expand_ident, square_norm_params):
    params = (reduce_proj, spatial_proj, expand_proj, shortcut_proj, reduce_ident, spatial_ident, expand_ident, norm_params)
    totals = tuple((jnp.zeros(member.shape, jnp.float32) for member in params))
    results = []
    back_list = []
    for pictures, alive_slots, upstream in ((images_coarse, live_coarse, upstream_coarse), (images_medium, live_medium, upstream_medium), (images_fine, live_fine, upstream_fine)):
        per_group = pictures.shape[0] // N_DP
        grouped = (pictures.reshape((N_DP, per_group) + pictures.shape[1:]), alive_slots.reshape(N_DP, per_group), upstream.reshape((N_DP, per_group) + upstream.shape[1:]))

        def one_group(running, group_item):
            group_pictures, group_alive, group_upstream = group_item

            def local_blocks(weights, inputs):
                return blocks(weights, inputs, group_alive)
            result, pullback = jax.vjp(local_blocks, params, group_pictures.astype(jnp.float32))
            grad_params, grad_input = pullback(group_upstream.astype(jnp.float32))
            running = tuple((previous + increment for previous, increment in zip(running, grad_params)))
            return (running, (result.astype(jnp.bfloat16), grad_input.astype(jnp.bfloat16)))
        totals, (result, backed) = lax.scan(one_group, totals, grouped)
        results.append(result.reshape(upstream.shape))
        back_list.append(backed.reshape(pictures.shape))
    firsts = (mean_reduce_proj, mean_spatial_proj, mean_expand_proj, mean_shortcut_proj, mean_reduce_ident, mean_spatial_ident, mean_expand_ident, mean_norm_params)
    seconds = (square_reduce_proj, square_spatial_proj, square_expand_proj, square_shortcut_proj, square_reduce_ident, square_spatial_ident, square_expand_ident, square_norm_params)
    stepped = []
    for position in range(8):
        if position < 7:
            stepped.append(adam_step(params[position], firsts[position], seconds[position], totals[position], RATE_CONV, DECAY_CONV))
        else:
            stepped.append(adam_step(params[position], firsts[position], seconds[position], totals[position], RATE_NORM, 0.0))
    return (results[0], results[1], results[2], back_list[0], back_list[1], back_list[2], stepped[0][0], stepped[0][1], stepped[0][2], stepped[1][0], stepped[1][1], stepped[1][2], stepped[2][0], stepped[2][1], stepped[2][2], stepped[3][0], stepped[3][1], stepped[3][2], stepped[4][0], stepped[4][1], stepped[4][2], stepped[5][0], stepped[5][1], stepped[5][2], stepped[6][0], stepped[6][1], stepped[6][2], stepped[7][0], stepped[7][1], stepped[7][2])
```

```python
import jax
import jax.numpy as jnp
import numpy as np
from jax import lax
from jax.experimental import pallas as pl
from jax.experimental.pallas import tpu as pltpu
from jax.sharding import PartitionSpec as P

STEP = 10
EPSILON = 1e-05
RATE_CONV = 0.03
RATE_NORM = 0.4
DECAY_CONV = 0.05
BF = jnp.bfloat16
F32 = jnp.float32
MID = 512
HALO = 32
NORM_ROW = {"1": 0, "2": 1, "3": 2, "S": 6, "4": 10, "5": 11, "6": 12}


class Grid:
    def __init__(self, counts, sides):
        self.counts, self.sides = counts, sides
        self.seg, self.size = [], []
        at = 0
        for number, side in zip(counts, sides):
            rows = -(-number * (side + 1) ** 2 // 16) * 16
            self.seg.append(at)
            self.size.append(rows)
            at += rows
        self.rows = at

    def lines(self):
        for which, (number, side) in enumerate(zip(self.counts, self.sides)):
            for line in range(side):
                for column in range(side):
                    yield which, line, column, self.seg[which] + (line * (side + 1) + column) * number


def silu(v):
    return v * jax.nn.sigmoid(v)


def slope(v):
    s = jax.nn.sigmoid(v)
    return s * (1.0 + v * (1.0 - s))


def dot_nn(a, b):
    return lax.dot_general(a, b, (((1,), (0,)), ((), ())), preferred_element_type=F32)


def dot_nt(a, b):
    return lax.dot_general(a, b, (((1,), (1,)), ((), ())), preferred_element_type=F32)


def dot_tn(a, b):
    return lax.dot_general(a, b, (((0,), (0,)), ((), ())), preferred_element_type=F32)


def aligned(row):
    return pl.multiple_of(row, 16)


def wide(mask):
    return jnp.concatenate([mask] * (MID // 128), axis=1)


VM = pl.BlockSpec(memory_space=pltpu.VMEM)
SM = pl.BlockSpec(memory_space=pltpu.SMEM)
HB = pl.BlockSpec(memory_space=pl.ANY)


def call(body, ins, outs, scratch=(), flops=0, moved=0, aliases=None):
    return pl.pallas_call(
        body,
        out_shape=[jax.ShapeDtypeStruct(shape, dtype) for shape, dtype, _ in outs],
        in_specs=[spec for _, spec in ins],
        out_specs=[spec for _, _, spec in outs],
        scratch_shapes=list(scratch),
        input_output_aliases=aliases or {},
        compiler_params=pltpu.CompilerParams(vmem_limit_bytes=58 * 1024 * 1024),
        cost_estimate=pl.CostEstimate(flops=flops, bytes_accessed=moved, transcendentals=0),
    )(*[array for array, _ in ins])


class Device:
    def __init__(self, grid, blocks, members):
        self.g = grid
        self.blocks = blocks
        self.members = members
        self.R = grid.rows


    def chunks(self, body):
        for which in range(3):
            start = self.g.seg[which]

            def step(i, _, which=which, start=start):
                body(which, aligned(start + i * 16))
                return 0

            lax.fori_loop(0, self.g.size[which] // 16, step, 0)

    def load_start(self, layout, ids, refs, off, rows, dst, sem):
        for ref, (base, places) in zip(refs, layout):
            low, high = max(base, off), min(base + ref.shape[1], off + rows)
            if high <= low:
                continue
            for pos, rel in enumerate(places):
                block = rel ^ ids[0]
                pltpu.make_async_copy(
                    ref.at[pos, pl.ds(low - base, high - low), :],
                    dst.at[pl.ds(pl.multiple_of(block * rows + (low - off), 16), high - low), :],
                    sem,
                ).start()

    def load_wait(self, dst, sem):
        pltpu.make_async_copy(dst, dst, sem).wait()

    def store_start(self, chains, ids, src, rows, split, offs, refs, sems):
        at, lo = 0, 0
        for places_list, take, off in zip(chains, split, offs):
            for places in places_list:
                for pos, rel in enumerate(places):
                    block = rel ^ ids[0]
                    pltpu.make_async_copy(
                        src.at[pl.ds(pl.multiple_of(block * rows + lo, 16), take), :],
                        refs[at].at[pos, pl.ds(off, take), :],
                        sems.at[at],
                    ).start()
                at += 1
            lo += take

    def store_wait(self, refs, sems, spans):
        for which, (ref, (off, size)) in enumerate(zip(refs, spans)):
            view = ref.at[:, pl.ds(off, size), :]
            pltpu.make_async_copy(view, view, sems.at[which]).wait()

    def local_stats(self, c_ref, m_ref, sc, out_ref, at, area, phases=1):
        cols = c_ref.shape[1]
        out_ref[pl.ds(at, 8), :] = jnp.zeros((8, cols), F32)
        for which in range(3):
            start, size = self.g.seg[which], self.g.size[which]
            held = sc[0, which] * float(area[which])
            for q in range(cols // MID):
                lane = slice(q * MID, (q + 1) * MID)

                def first(i, acc, start=start, lane=lane):
                    row = aligned(start + i * 16)
                    m = wide(m_ref[pl.ds(row, 16), :])
                    for phase in range(phases):
                        v = c_ref[pl.ds(aligned(row + phase * self.R), 16), lane] * m
                        acc = acc + v[:8] + v[8:]
                    return acc

                acc = lax.fori_loop(0, size // 16, first, jnp.zeros((8, MID), F32))
                total = jnp.sum(acc, axis=0, keepdims=True)
                mean = total / held

                def second(i, acc, start=start, lane=lane, mean=mean):
                    row = aligned(start + i * 16)
                    m = wide(m_ref[pl.ds(row, 16), :])
                    for phase in range(phases):
                        v = c_ref[pl.ds(aligned(row + phase * self.R), 16), lane] - mean
                        v = v * v * m
                        acc = acc + v[:8] + v[8:]
                    return acc

                acc = lax.fori_loop(0, size // 16, second, jnp.zeros((8, MID), F32))
                out_ref[at + which : at + which + 1, lane] = total
                out_ref[at + 3 + which : at + 4 + which, lane] = jnp.sum(acc, axis=0, keepdims=True)

    def group_norm(self, st_refs, at, sc, area, out_ref):
        cols = out_ref.shape[1]
        out_ref[...] = jnp.zeros(out_ref.shape, F32)
        for which in range(3):
            count = sc[self.members, which] * float(area[which])
            sums = [ref[at + which : at + which + 1, :] for ref in st_refs]
            mean = sum(sums[1:], sums[0]) / count
            spread = jnp.zeros((1, cols), F32)
            for k, ref in enumerate(st_refs):
                held = sc[k, which] * float(area[which])
                apart = sums[k] / held - mean
                spread = spread + (ref[at + 3 + which : at + 4 + which, :] + held * apart * apart)
            out_ref[which : which + 1, :] = mean
            out_ref[3 + which : 4 + which, :] = lax.rsqrt(spread / count + EPSILON)

    def group_sums(self, st_refs, at, sc, area, out_ref):
        out_ref[...] = jnp.zeros(out_ref.shape, F32)
        for which in range(3):
            count = sc[self.members, which] * float(area[which])
            for row in (which, 3 + which):
                rows = [ref[at + row : at + row + 1, :] for ref in st_refs]
                out_ref[row : row + 1, :] = sum(rows[1:], rows[0]) / count

    def xhat(self, c_ref, nrm, which, row, lane=slice(0, MID)):
        return (c_ref[pl.ds(row, 16), lane] - nrm[which : which + 1, lane]) * nrm[3 + which : 4 + which, lane]

    def affine(self, normp, name, q, xh):
        at = NORM_ROW[name] + q
        return normp[at : at + 1, :] * xh + normp[16 + at : 17 + at, :]

    def norm_back(self, normp, name, q, nrm, sums, which, lane, dz, xh, m):
        at = NORM_ROW[name] + q
        a = sums[which : which + 1, lane]
        b = sums[3 + which : 4 + which, lane]
        scale = normp[at : at + 1, :] * nrm[3 + which : 4 + which, lane]
        return scale * (dz - m * (a + xh * b))

    def add_rows(self, out_ref, row, value, lane=slice(0, MID)):
        out_ref[row : row + 1, lane] = out_ref[row : row + 1, lane] + jnp.sum(value, axis=0, keepdims=True)

    def shifted(self, hs_ref, dst_ref, col, sign_r, sign_c):
        for which in range(3):
            off = (sign_r * (self.g.sides[which] + 1) + sign_c) * self.g.counts[which]
            for i in range(self.g.size[which] // 16):
                row = self.g.seg[which] + i * 16
                dst_ref[row : row + 16, col : col + MID] = hs_ref[HALO + row + off : HALO + row + off + 16, :].astype(BF)

    def clear_halo(self, hs_ref):
        hs_ref[0:HALO, :] = jnp.zeros((HALO, MID), F32)
        hs_ref[HALO + self.R : 2 * HALO + self.R, :] = jnp.zeros((HALO, MID), F32)

    def area(self, side_scale):
        return [(side_scale * side) ** 2 for side in self.g.sides]


    def prepare(self, spot, lives, pictures):
        R = self.R
        g = self.g
        width = pictures[0].shape[3]
        members = self.members

        def body(spot, la, lb, lc, xa, xb, xc, xp, msk, sc, big):
            x_refs, l_refs = (xa, xb, xc), (la, lb, lc)
            own = []
            for which in range(3):
                per = g.counts[which]
                whole = jnp.zeros((), jnp.int32)
                for k in range(members):
                    first = (spot[0] * members + (spot[1] ^ k)) * per
                    flags = [l_refs[which][first + i] for i in range(per)]
                    held = sum(flags[1:], flags[0])
                    sc[k, which] = held.astype(F32)
                    whole = whole + held
                    if k == 0:
                        own.append(flags)
                sc[members, which] = whole.astype(F32)
            big[...] = jnp.zeros(big.shape, F32)
            msk[...] = jnp.zeros(msk.shape, F32)
            alive = []
            for which in range(3):
                per = g.counts[which]
                slot = lax.broadcasted_iota(jnp.int32, (per, 128), 0)
                mask = jnp.zeros((per, 128), F32)
                for i in range(per):
                    mask = jnp.where(slot == i, own[which][i].astype(F32), mask)
                alive.append(mask)
            for which, line, column, row in g.lines():
                per = g.counts[which]
                msk[row : row + per, :] = alive[which]
                for phase in range(4):
                    odd, second = divmod(phase, 2)
                    base = phase * R + row
                    big[base : base + per, :] = x_refs[which][2 * line + odd, 2 * column + second].astype(F32)

            def cast(i, _):
                row = aligned(i * 16)
                xp[pl.ds(row, 16), :] = big[pl.ds(row, 16), :].astype(BF)
                return 0

            lax.fori_loop(0, 4 * R // 16, cast, 0)

        return call(
            body,
            [(spot, SM)] + [(l, SM) for l in lives] + [(p, VM) for p in pictures],
            [((4 * R, width), BF, VM), ((R, 128), F32, VM), ((members + 1, 3), F32, SM)],
            [pltpu.VMEM((4 * R, width), F32)],
        )

    def conv_one(self, ids, sc, xp, msk, w, off, rows, norm_off):
        R = self.R
        width = xp.shape[1]
        layout, arrays = w
        with_norm = norm_off is not None

        def body(ids, sc, xp, msk, *rest):
            refs = rest[: len(arrays)]
            rest = rest[len(arrays) :]
            if with_norm:
                c, st, normp, ws, ns, sem, sem2 = rest
                self.load_start(layout, ids, refs, norm_off, 16, ns, sem2)
            else:
                c, st, ws, sem = rest
            self.load_start(layout, ids, refs, off, rows, ws, sem)
            if with_norm:
                self.load_wait(ns, sem2)
                for b in range(self.blocks):
                    normp[b : b + 1, :] = ns[b * 16 : b * 16 + 16, :].astype(F32)[0:1, :]
            self.load_wait(ws, sem)
            for phase in range(4):
                c[phase * R : (phase + 1) * R, :] = dot_nn(xp[phase * R : (phase + 1) * R, :], ws[...])
            self.local_stats(c, msk, sc, st, 0, self.area(2), 4)

        outs = [((4 * R, MID), F32, VM), ((8, MID), F32, VM)]
        scratch = [pltpu.VMEM((width, MID), BF)]
        if with_norm:
            outs.append(((32, MID), F32, VM))
            scratch.append(pltpu.VMEM((self.blocks * 16, MID), BF))
            scratch.append(pltpu.SemaphoreType.DMA)
        scratch.append(pltpu.SemaphoreType.DMA)
        return call(
            body,
            [(ids, SM), (sc, SM), (xp, VM), (msk, VM)] + [(a, HB) for a in arrays],
            outs,
            scratch,
            flops=2 * 4 * R * width * MID,
        )

    @staticmethod
    def tap_two(tap):
        i, j = divmod(tap, 3)
        return (0 if i == 1 else 2) + (0 if j == 1 else 1), (1 if i == 0 else 0), (1 if j == 0 else 0)

    def conv_two(self, ids, sc, c1, sts, normp, msk, w, off, rows):
        R = self.R
        layout, arrays = w
        nst, nw = len(sts), len(arrays)

        def body(ids, sc, c1, normp, msk, *rest):
            st_refs, refs = rest[:nst], rest[nst : nst + nw]
            a1, nrm, c2, st, ws, hs, patches, sem = rest[nst + nw :]
            self.load_start(layout, ids, refs, off, rows, ws, sem)
            self.group_norm(st_refs, 0, sc, self.area(2), nrm)
            self.clear_halo(hs)
            for phase in range(4):

                def act(which, row, phase=phase):
                    at = aligned(row + phase * R)
                    m = wide(msk[pl.ds(row, 16), :])
                    v = silu(self.affine(normp, "1", 0, self.xhat(c1, nrm, which, at))) * m
                    hs[pl.ds(aligned(row + HALO), 16), :] = v
                    a1[pl.ds(at, 16), :] = v.astype(BF)

                self.chunks(act)
                for tap in range(9):
                    source, back_r, back_c = self.tap_two(tap)
                    if source == phase:
                        self.shifted(hs, patches, tap * MID, -back_r, -back_c)
            self.load_wait(ws, sem)
            c2[...] = dot_nn(patches[...], ws[...])
            self.local_stats(c2, msk, sc, st, 0, self.area(1))

        return call(
            body,
            [(ids, SM), (sc, SM), (c1, VM), (normp, VM), (msk, VM)] + [(s, VM) for s in sts] + [(a, HB) for a in arrays],
            [((4 * R, MID), BF, VM), ((8, MID), F32, VM), ((R, MID), F32, VM), ((8, MID), F32, VM)],
            [
                pltpu.VMEM((9 * MID, MID), BF),
                pltpu.VMEM((R + 2 * HALO, MID), F32),
                pltpu.VMEM((R, 9 * MID), BF),
                pltpu.SemaphoreType.DMA,
            ],
            flops=2 * 9 * R * MID * MID,
        )

    def conv_short(self, ids, sc, xp, msk, w, off, rows):
        R = self.R
        layout, arrays = w
        nw = len(arrays)
        out_width = self.blocks * rows if self.blocks > 1 else rows

        def body(ids, sc, xp, msk, *rest):
            refs = rest[:nw]
            c, st, wa, wb, sem = rest[nw:]
            self.load_start(layout, ids, refs, off, rows, wa, sem.at[0])
            self.load_start(layout, ids, refs, off + rows, rows, wb, sem.at[1])
            self.load_wait(wa, sem.at[0])
            self.load_wait(wb, sem.at[1])
            for q in range(out_width // MID):
                lane = slice(q * MID, (q + 1) * MID)
                c[:, lane] = dot_nt(xp[0:R, 0:MID], wa[lane, :]) + dot_nt(xp[0:R, MID : 2 * MID], wb[lane, :])
            self.local_stats(c, msk, sc, st, 0, self.area(1))

        return call(
            body,
            [(ids, SM), (sc, SM), (xp, VM), (msk, VM)] + [(a, HB) for a in arrays],
            [((R, out_width), F32, VM), ((8, out_width), F32, VM)],
            [pltpu.VMEM((out_width, MID), BF), pltpu.VMEM((out_width, MID), BF), pltpu.SemaphoreType.DMA((2,))],
            flops=2 * R * 2 * MID * out_width,
        )

    def conv_expand(self, ids, sc, c, sts, normp, msk, w, off, rows, name, more=None):
        R = self.R
        layout, arrays = w
        nst, nw = len(sts), len(arrays)
        out_width = self.blocks * rows if self.blocks > 1 else rows
        stat_rows = 8 if more is None else 16

        def body(ids, sc, c, normp, msk, *rest):
            st_refs, refs = rest[:nst], rest[nst : nst + nw]
            rest = rest[nst + nw :]
            if more is not None:
                more_ref, rest = rest[0], rest[1:]
            act, nrm, prod, st, ws, sem = rest
            self.load_start(layout, ids, refs, off, rows, ws, sem)
            self.group_norm(st_refs, 0, sc, self.area(1), nrm)

            def one(which, row):
                m = wide(msk[pl.ds(row, 16), :])
                v = silu(self.affine(normp, name, 0, self.xhat(c, nrm, which, row))) * m
                act[pl.ds(row, 16), :] = v.astype(BF)

            self.chunks(one)
            self.load_wait(ws, sem)
            for q in range(out_width // MID):
                lane = slice(q * MID, (q + 1) * MID)
                prod[:, lane] = dot_nt(act[...], ws[lane, :])
            self.local_stats(prod, msk, sc, st, 0, self.area(1))
            if more is not None:
                st[8:16, :] = more_ref[...]

        ins = [(ids, SM), (sc, SM), (c, VM), (normp, VM), (msk, VM)] + [(s, VM) for s in sts] + [(a, HB) for a in arrays]
        if more is not None:
            ins.append((more, VM))
        return call(
            body,
            ins,
            [((R, MID), BF, VM), ((8, MID), F32, VM), ((R, out_width), F32, VM), ((stat_rows, out_width), F32, VM)],
            [pltpu.VMEM((out_width, MID), BF), pltpu.SemaphoreType.DMA],
            flops=2 * R * MID * out_width,
        )

    def conv_four(self, ids, sc, c3, cs, sts, normp, msk, w, off, rows):
        R = self.R
        layout, arrays = w
        nst, nw = len(sts), len(arrays)
        out_width = c3.shape[1]

        def body(ids, sc, c3, cs, normp, msk, *rest):
            st_refs, refs = rest[:nst], rest[nst : nst + nw]
            h, hb, nrm3, nrms, c4, st, ws, sem = rest[nst + nw :]
            self.load_start(layout, ids, refs, off, rows, ws, sem)
            self.group_norm(st_refs, 0, sc, self.area(1), nrm3)
            self.group_norm(st_refs, 8, sc, self.area(1), nrms)

            def one(which, row):
                m = wide(msk[pl.ds(row, 16), :])
                for q in range(out_width // MID):
                    lane = slice(q * MID, (q + 1) * MID)
                    pre = self.affine(normp, "3", q, self.xhat(c3, nrm3, which, row, lane)) + self.affine(
                        normp, "S", q, self.xhat(cs, nrms, which, row, lane)
                    )
                    v = silu(pre) * m
                    h[pl.ds(row, 16), lane] = v
                    hb[pl.ds(row, 16), lane] = v.astype(BF)

            self.chunks(one)
            self.load_wait(ws, sem)
            c4[...] = dot_nn(hb[...], ws[...])
            self.local_stats(c4, msk, sc, st, 0, self.area(1))

        return call(
            body,
            [(ids, SM), (sc, SM), (c3, VM), (cs, VM), (normp, VM), (msk, VM)]
            + [(s, VM) for s in sts]
            + [(a, HB) for a in arrays],
            [
                ((R, out_width), F32, VM),
                ((R, out_width), BF, VM),
                ((8, out_width), F32, VM),
                ((8, out_width), F32, VM),
                ((R, MID), F32, VM),
                ((8, MID), F32, VM),
            ],
            [pltpu.VMEM((out_width, MID), BF), pltpu.SemaphoreType.DMA],
            flops=2 * R * MID * out_width,
        )

    def conv_five(self, ids, sc, c4, sts, normp, msk, w, off, rows):
        R = self.R
        layout, arrays = w
        nst, nw = len(sts), len(arrays)

        def body(ids, sc, c4, normp, msk, *rest):
            st_refs, refs = rest[:nst], rest[nst : nst + nw]
            a4, nrm, c5, st, ws, hs, patches, sem = rest[nst + nw :]
            self.load_start(layout, ids, refs, off, rows, ws, sem)
            self.group_norm(st_refs, 0, sc, self.area(1), nrm)
            self.clear_halo(hs)

            def act(which, row):
                m = wide(msk[pl.ds(row, 16), :])
                v = silu(self.affine(normp, "4", 0, self.xhat(c4, nrm, which, row))) * m
                hs[pl.ds(aligned(row + HALO), 16), :] = v
                a4[pl.ds(row, 16), :] = v.astype(BF)

            self.chunks(act)
            for tap in range(9):
                i, j = divmod(tap, 3)
                self.shifted(hs, patches, tap * MID, i - 1, j - 1)
            self.load_wait(ws, sem)
            c5[...] = dot_nn(patches[...], ws[...])
            self.local_stats(c5, msk, sc, st, 0, self.area(1))

        return call(
            body,
            [(ids, SM), (sc, SM), (c4, VM), (normp, VM), (msk, VM)] + [(s, VM) for s in sts] + [(a, HB) for a in arrays],
            [((R, MID), BF, VM), ((8, MID), F32, VM), ((R, MID), F32, VM), ((8, MID), F32, VM)],
            [
                pltpu.VMEM((9 * MID, MID), BF),
                pltpu.VMEM((R + 2 * HALO, MID), F32),
                pltpu.VMEM((R, 9 * MID), BF),
                pltpu.SemaphoreType.DMA,
            ],
            flops=2 * 9 * R * MID * MID,
        )

    def finish(self, sc, c6, h, sts, normp, msk, ups):
        R = self.R
        g = self.g
        nst = len(sts)
        out_width = c6.shape[1]

        def body(sc, c6, h, normp, msk, ua, ub, uc, *rest):
            st_refs = rest[:nst]
            oa, ob, oc, dz, nrm, st, up, res = rest[nst:]
            u_refs, o_refs = (ua, ub, uc), (oa, ob, oc)
            self.group_norm(st_refs, 0, sc, self.area(1), nrm)
            up[...] = jnp.zeros(up.shape, F32)
            st[...] = jnp.zeros(st.shape, F32)
            for which, line, column, row in g.lines():
                up[row : row + g.counts[which], :] = u_refs[which][line, column].astype(F32)

            def one(which, row):
                m = wide(msk[pl.ds(row, 16), :])
                for q in range(out_width // MID):
                    lane = slice(q * MID, (q + 1) * MID)
                    xh = self.xhat(c6, nrm, which, row, lane)
                    pre = self.affine(normp, "6", q, xh) + h[pl.ds(row, 16), lane]
                    s = jax.nn.sigmoid(pre)
                    res[pl.ds(row, 16), lane] = m * (pre * s)
                    d = up[pl.ds(row, 16), lane] * m * (s * (1.0 + pre * (1.0 - s)))
                    dz[pl.ds(row, 16), lane] = d
                    self.add_rows(st, which, d, lane)
                    self.add_rows(st, 3 + which, d * xh, lane)

            self.chunks(one)
            for which, line, column, row in g.lines():
                o_refs[which][line, column] = res[row : row + g.counts[which], :].astype(BF)

        return call(
            body,
            [(sc, SM), (c6, VM), (h, VM), (normp, VM), (msk, VM)] + [(u, VM) for u in ups] + [(s, VM) for s in sts],
            [(u.shape, BF, VM) for u in ups]
            + [((R, out_width), F32, VM), ((8, out_width), F32, VM), ((8, out_width), F32, VM)],
            [pltpu.VMEM((R, out_width), F32), pltpu.VMEM((R, out_width), F32)],
        )

    def back_six(self, ids, sc, dz, c6, nrm6, sts, normp, msk, c5, nrm5, w, off, rows):
        R = self.R
        layout, arrays = w
        nst, nw = len(sts), len(arrays)
        out_width = c6.shape[1]

        def body(ids, sc, dz, c6, nrm6, normp, msk, c5, nrm5, *rest):
            st_refs, refs = rest[:nst], rest[nst : nst + nw]
            dc, dz5, st, sums, ws, sem = rest[nst + nw :]
            self.load_start(layout, ids, refs, off, rows, ws, sem)
            self.group_sums(st_refs, 0, sc, self.area(1), sums)
            st[...] = jnp.zeros(st.shape, F32)

            def one(which, row):
                m = wide(msk[pl.ds(row, 16), :])
                for q in range(out_width // MID):
                    lane = slice(q * MID, (q + 1) * MID)
                    xh = self.xhat(c6, nrm6, which, row, lane)
                    v = self.norm_back(normp, "6", q, nrm6, sums, which, lane, dz[pl.ds(row, 16), lane], xh, m)
                    dc[pl.ds(row, 16), lane] = v.astype(BF)

            self.chunks(one)
            self.load_wait(ws, sem)
            dz5[...] = dot_nn(dc[...], ws[...])
            self.through(dz5, c5, nrm5, normp, "5", msk, st)

        return call(
            body,
            [(ids, SM), (sc, SM), (dz, VM), (c6, VM), (nrm6, VM), (normp, VM), (msk, VM), (c5, VM), (nrm5, VM)]
            + [(s, VM) for s in sts]
            + [(a, HB) for a in arrays],
            [((R, out_width), BF, VM), ((R, MID), F32, VM), ((8, MID), F32, VM)],
            [pltpu.VMEM((8, out_width), F32), pltpu.VMEM((out_width, MID), BF), pltpu.SemaphoreType.DMA],
            flops=2 * R * MID * out_width,
        )

    def through(self, dz, c, nrm, normp, name, msk, st, phases=1):
        def one(which, row):
            m = wide(msk[pl.ds(row, 16), :])
            for phase in range(phases):
                at = aligned(row + phase * self.R)
                xh = self.xhat(c, nrm, which, at)
                d = dz[pl.ds(at, 16), :] * slope(self.affine(normp, name, 0, xh)) * m
                dz[pl.ds(at, 16), :] = d
                self.add_rows(st, which, d)
                self.add_rows(st, 3 + which, d * xh)

        self.chunks(one)

    def back_five(self, ids, sc, dz5, c5, nrm5, sts, normp, msk, c4, nrm4, w, off, rows):
        R = self.R
        layout, arrays = w
        nst, nw = len(sts), len(arrays)

        def body(ids, sc, dz5, c5, nrm5, normp, msk, c4, nrm4, *rest):
            st_refs, refs = rest[:nst], rest[nst : nst + nw]
            dc, dz4, st, sums, ws, hs, patches, sem = rest[nst + nw :]
            self.load_start(layout, ids, refs, off, rows, ws, sem)
            self.group_sums(st_refs, 0, sc, self.area(1), sums)
            self.clear_halo(hs)
            st[...] = jnp.zeros(st.shape, F32)
            self.own_dc(dz5, c5, nrm5, sums, normp, "5", msk, dc, hs)
            for tap in range(9):
                i, j = divmod(tap, 3)
                self.shifted(hs, patches, tap * MID, 1 - i, 1 - j)
            self.load_wait(ws, sem)
            for tap in range(9):
                part = dot_nt(patches[:, tap * MID : (tap + 1) * MID], ws[tap * MID : (tap + 1) * MID, :])
                if tap == 0:
                    dz4[...] = part
                else:
                    dz4[...] += part
            self.through(dz4, c4, nrm4, normp, "4", msk, st)

        return call(
            body,
            [(ids, SM), (sc, SM), (dz5, VM), (c5, VM), (nrm5, VM), (normp, VM), (msk, VM), (c4, VM), (nrm4, VM)]
            + [(s, VM) for s in sts]
            + [(a, HB) for a in arrays],
            [((R, MID), BF, VM), ((R, MID), F32, VM), ((8, MID), F32, VM)],
            [
                pltpu.VMEM((8, MID), F32),
                pltpu.VMEM((9 * MID, MID), BF),
                pltpu.VMEM((R + 2 * HALO, MID), F32),
                pltpu.VMEM((R, 9 * MID), BF),
                pltpu.SemaphoreType.DMA,
            ],
            flops=2 * 9 * R * MID * MID,
        )

    def own_dc(self, dz, c, nrm, sums, normp, name, msk, dc, hs=None, phases=1):
        def one(which, row):
            m = wide(msk[pl.ds(row, 16), :])
            for phase in range(phases):
                at = aligned(row + phase * self.R)
                xh = self.xhat(c, nrm, which, at)
                v = self.norm_back(normp, name, 0, nrm, sums, which, slice(0, MID), dz[pl.ds(at, 16), :], xh, m)
                dc[pl.ds(at, 16), :] = v.astype(BF)
                if hs is not None:
                    hs[pl.ds(aligned(row + HALO), 16), :] = v

        self.chunks(one)

    def back_four(self, ids, sc, dz4, c4, nrm4, sts, normp, msk, dz6, c3, nrm3, cs, nrms, w, off, rows):
        R = self.R
        layout, arrays = w
        nst, nw = len(sts), len(arrays)
        out_width = c3.shape[1]

        def body(ids, sc, dz4, c4, nrm4, normp, msk, dz6, c3, nrm3, cs, nrms, *rest):
            st_refs, refs = rest[:nst], rest[nst : nst + nw]
            dc, dz3, st, sums, ws, sem = rest[nst + nw :]
            self.load_start(layout, ids, refs, off, rows, ws, sem)
            self.group_sums(st_refs, 0, sc, self.area(1), sums)
            st[...] = jnp.zeros(st.shape, F32)
            self.own_dc(dz4, c4, nrm4, sums, normp, "4", msk, dc)
            self.load_wait(ws, sem)
            for q in range(out_width // MID):
                lane = slice(q * MID, (q + 1) * MID)
                dz3[:, lane] = dot_nt(dc[...], ws[lane, :])

            def one(which, row):
                m = wide(msk[pl.ds(row, 16), :])
                for q in range(out_width // MID):
                    lane = slice(q * MID, (q + 1) * MID)
                    xh3 = self.xhat(c3, nrm3, which, row, lane)
                    xhs = self.xhat(cs, nrms, which, row, lane)
                    pre = self.affine(normp, "3", q, xh3) + self.affine(normp, "S", q, xhs)
                    d = (dz6[pl.ds(row, 16), lane] + dz3[pl.ds(row, 16), lane]) * slope(pre) * m
                    dz3[pl.ds(row, 16), lane] = d
                    self.add_rows(st, which, d, lane)
                    self.add_rows(st, 3 + which, d * xh3, lane)
                    self.add_rows(st, 8 + 3 + which, d * xhs, lane)

            self.chunks(one)
            st[8:11, :] = st[0:3, :]

        return call(
            body,
            [(ids, SM), (sc, SM), (dz4, VM), (c4, VM), (nrm4, VM), (normp, VM), (msk, VM)]
            + [(dz6, VM), (c3, VM), (nrm3, VM), (cs, VM), (nrms, VM)]
            + [(s, VM) for s in sts]
            + [(a, HB) for a in arrays],
            [((R, MID), BF, VM), ((R, out_width), F32, VM), ((16, out_width), F32, VM)],
            [pltpu.VMEM((8, MID), F32), pltpu.VMEM((out_width, MID), BF), pltpu.SemaphoreType.DMA],
            flops=2 * R * MID * out_width,
        )

    def back_three(self, ids, sc, dz3, c3, nrm3, cs, nrms, sts, normp, msk, c2, nrm2, w, off, rows):
        R = self.R
        layout, arrays = w
        nst, nw = len(sts), len(arrays)
        out_width = c3.shape[1]

        def body(ids, sc, dz3, c3, nrm3, cs, nrms, normp, msk, c2, nrm2, *rest):
            st_refs, refs = rest[:nst], rest[nst : nst + nw]
            dc3, dcs, dz2, st, sums3, sumss, ws, sem = rest[nst + nw :]
            self.load_start(layout, ids, refs, off, rows, ws, sem)
            self.group_sums(st_refs, 0, sc, self.area(1), sums3)
            self.group_sums(st_refs, 8, sc, self.area(1), sumss)
            st[...] = jnp.zeros(st.shape, F32)

            def one(which, row):
                m = wide(msk[pl.ds(row, 16), :])
                for q in range(out_width // MID):
                    lane = slice(q * MID, (q + 1) * MID)
                    d = dz3[pl.ds(row, 16), lane]
                    xh = self.xhat(c3, nrm3, which, row, lane)
                    dc3[pl.ds(row, 16), lane] = self.norm_back(
                        normp, "3", q, nrm3, sums3, which, lane, d, xh, m
                    ).astype(BF)
                    xh = self.xhat(cs, nrms, which, row, lane)
                    dcs[pl.ds(row, 16), lane] = self.norm_back(
                        normp, "S", q, nrms, sumss, which, lane, d, xh, m
                    ).astype(BF)

            self.chunks(one)
            self.load_wait(ws, sem)
            dz2[...] = dot_nn(dc3[...], ws[...])
            self.through(dz2, c2, nrm2, normp, "2", msk, st)

        return call(
            body,
            [(ids, SM), (sc, SM), (dz3, VM), (c3, VM), (nrm3, VM), (cs, VM), (nrms, VM), (normp, VM), (msk, VM)]
            + [(c2, VM), (nrm2, VM)]
            + [(s, VM) for s in sts]
            + [(a, HB) for a in arrays],
            [((R, out_width), BF, VM), ((R, out_width), BF, VM), ((R, MID), F32, VM), ((8, MID), F32, VM)],
            [
                pltpu.VMEM((8, out_width), F32),
                pltpu.VMEM((8, out_width), F32),
                pltpu.VMEM((out_width, MID), BF),
                pltpu.SemaphoreType.DMA,
            ],
            flops=2 * R * MID * out_width,
        )

    SHIFTS = ((0, 0), (0, 1), (1, 0), (1, 1))

    def back_two(self, ids, sc, dz2, c2, nrm2, sts, normp, msk, c1, nrm1, w, off, rows):
        R = self.R
        layout, arrays = w
        nst, nw = len(sts), len(arrays)

        def body(ids, sc, dz2, c2, nrm2, normp, msk, c1, nrm1, *rest):
            st_refs, refs = rest[:nst], rest[nst : nst + nw]
            dc, dz1, st, sums, ws, hs, patches, sem = rest[nst + nw :]
            self.load_start(layout, ids, refs, off, rows, ws, sem)
            self.group_sums(st_refs, 0, sc, self.area(1), sums)
            self.clear_halo(hs)
            st[...] = jnp.zeros(st.shape, F32)
            self.own_dc(dz2, c2, nrm2, sums, normp, "2", msk, dc, hs)
            for k, (fwd_r, fwd_c) in enumerate(self.SHIFTS):
                self.shifted(hs, patches, k * MID, fwd_r, fwd_c)
            self.load_wait(ws, sem)
            seen = set()
            for tap in range(9):
                phase, back_r, back_c = self.tap_two(tap)
                k = self.SHIFTS.index((back_r, back_c))
                part = dot_nt(patches[:, k * MID : (k + 1) * MID], ws[tap * MID : (tap + 1) * MID, :])
                if phase in seen:
                    dz1[phase * R : (phase + 1) * R, :] += part
                else:
                    dz1[phase * R : (phase + 1) * R, :] = part
                seen.add(phase)
            self.through(dz1, c1, nrm1, normp, "1", msk, st, 4)

        return call(
            body,
            [(ids, SM), (sc, SM), (dz2, VM), (c2, VM), (nrm2, VM), (normp, VM), (msk, VM), (c1, VM), (nrm1, VM)]
            + [(s, VM) for s in sts]
            + [(a, HB) for a in arrays],
            [((R, MID), BF, VM), ((4 * R, MID), F32, VM), ((8, MID), F32, VM)],
            [
                pltpu.VMEM((8, MID), F32),
                pltpu.VMEM((9 * MID, MID), BF),
                pltpu.VMEM((R + 2 * HALO, MID), F32),
                pltpu.VMEM((R, 4 * MID), BF),
                pltpu.SemaphoreType.DMA,
            ],
            flops=2 * 9 * R * MID * MID,
        )

    def back_one(self, sc, dz1, c1, nrm1, sts, normp, msk):
        R = self.R
        nst = len(sts)

        def body(sc, dz1, c1, nrm1, normp, msk, *rest):
            st_refs = rest[:nst]
            dc, sums = rest[nst:]
            self.group_sums(st_refs, 0, sc, self.area(2), sums)
            self.own_dc(dz1, c1, nrm1, sums, normp, "1", msk, dc, None, 4)

        return call(
            body,
            [(sc, SM), (dz1, VM), (c1, VM), (nrm1, VM), (normp, VM), (msk, VM)] + [(s, VM) for s in sts],
            [((4 * R, MID), BF, VM)],
            [pltpu.VMEM((8, MID), F32)],
        )[0]

    def input_grad(self, ids, dc1, dcs, w1, off1, rows1, ids_s, ws, offs, rowss, pictures):
        R = self.R
        g = self.g
        lay1, arr1 = w1
        lays, arrs = ws
        n1, ns = len(arr1), len(arrs)
        width = pictures[0].shape[3]
        out_width = dcs.shape[1]

        def body(ids, ids_s, dc1, dcs, *rest):
            r1, rs = rest[:n1], rest[n1 : n1 + ns]
            ga, gb, gc, k1, ka, kb, dx, sem = rest[n1 + ns :]
            g_refs = (ga, gb, gc)
            self.load_start(lay1, ids, r1, off1, rows1, k1, sem.at[0])
            self.load_start(lays, ids_s, rs, offs, rowss, ka, sem.at[1])
            self.load_start(lays, ids_s, rs, offs + rowss, rowss, kb, sem.at[2])
            self.load_wait(k1, sem.at[0])
            self.load_wait(ka, sem.at[1])
            self.load_wait(kb, sem.at[2])
            for phase in range(4):
                for q in range(width // MID):
                    lane = slice(q * MID, (q + 1) * MID)
                    part = dot_nt(dc1[phase * R : (phase + 1) * R, :], k1[lane, :])
                    if phase == 0:
                        part = part + dot_nn(dcs[...], (ka, kb)[q][...])
                    dx[phase * R : (phase + 1) * R, lane] = part
            for which, line, column, row in g.lines():
                for phase in range(4):
                    odd, second = divmod(phase, 2)
                    base = phase * R + row
                    g_refs[which][2 * line + odd, 2 * column + second] = dx[base : base + g.counts[which], :].astype(BF)

        return call(
            body,
            [(ids, SM), (ids_s, SM), (dc1, VM), (dcs, VM)] + [(a, HB) for a in arr1] + [(a, HB) for a in arrs],
            [(p.shape, BF, VM) for p in pictures],
            [
                pltpu.VMEM((width, MID), BF),
                pltpu.VMEM((out_width, MID), BF),
                pltpu.VMEM((out_width, MID), BF),
                pltpu.VMEM((4 * R, width), F32),
                pltpu.SemaphoreType.DMA((3,)),
            ],
            flops=2 * (4 * R * width * MID + R * width * out_width),
        )


    def gradient(self, ids, chains, kind, ins, parts, heights, held=None, extra=None):
        fresh = held is None
        arrays, start = ([], [0] * len(chains)) if fresh else held
        outs, spans = [], []
        for c, places_list in enumerate(chains):
            size = sum(split[c] for _, split in parts)
            for places in places_list:
                outs.append(((len(places), heights[c], MID), BF, HB))
                spans.append((start[c], size))
        count, pieces = len(ins), len(outs)

        def body(ids, *rest):
            refs, rest = rest[:count], rest[count + len(arrays) :]
            out_refs, rest = rest[:pieces], rest[pieces:]
            bufs, rest = rest[: len(parts)], rest[len(parts) :]
            sems, tail = rest[0], rest[1:]
            offs = list(start)
            for part, (buf, (rows, split)) in enumerate(zip(bufs, parts)):
                kind(part, refs, buf, tail)
                self.store_start(chains, ids, buf, rows, split, offs, out_refs, sems)
                offs = [o + t for o, t in zip(offs, split)]
            self.store_wait(out_refs, sems, spans)

        tall = [rows * self.blocks if self.blocks > 1 else rows for rows, _ in parts]
        scratch = [pltpu.VMEM((t, MID), BF) for t in tall]
        scratch.append(pltpu.SemaphoreType.DMA((pieces,)))
        scratch.extend(extra or [])
        made = call(
            body,
            [(ids, SM)] + [(a, VM) for a in ins] + [(a, HB) for a in arrays],
            outs,
            scratch,
            flops=2 * self.R * sum(tall) * MID,
            aliases={1 + count + i: i for i in range(len(arrays))},
        )
        ends = [at + sum(split[c] for _, split in parts) for c, at in enumerate(start)]
        return list(made), ends

    def grad_outer(self, ids, chains, pairs, parts, heights, held=None):
        ins = []
        for left, right in pairs:
            ins += [left, right]

        def kind(part, refs, buf, tail):
            left, right = refs[2 * part], refs[2 * part + 1]
            for q in range(left.shape[1] // MID):
                buf[q * MID : (q + 1) * MID, :] = dot_tn(left[:, q * MID : (q + 1) * MID], right[...]).astype(BF)

        return self.gradient(ids, chains, kind, ins, parts, heights, held)

    def grad_short(self, ids, chains, a2, dc3, dcs, xp, parts, heights, held=None):
        R = self.R

        def kind(part, refs, buf, tail):
            a2, dc3, dcs, xp = refs
            left = dc3 if part == 0 else dcs
            for q in range(left.shape[1] // MID):
                cols = left[:, q * MID : (q + 1) * MID]
                right = a2[...] if part == 0 else xp[0:R, (part - 1) * MID : part * MID]
                buf[q * MID : (q + 1) * MID, :] = dot_tn(cols, right).astype(BF)

        return self.gradient(ids, chains, kind, [a2, dc3, dcs, xp], parts, heights, held)

    def grad_taps(self, ids, chains, act, dc, parts, heights, stride, held=None):
        R = self.R

        def kind(part, refs, buf, tail):
            act, dc = refs
            hs, patches = tail
            self.clear_halo(hs)

            def spread(which, row):
                hs[pl.ds(aligned(row + HALO), 16), :] = dc[pl.ds(row, 16), :].astype(F32)

            self.chunks(spread)
            if stride == 1:
                shifts = [(1 - tap // 3, 1 - tap % 3) for tap in range(9)]
            else:
                shifts = list(self.SHIFTS)
            for k, (sr, sc_) in enumerate(shifts):
                self.shifted(hs, patches, k * MID, sr, sc_)
            for tap in range(9):
                if stride == 1:
                    left, k = act[...], tap
                else:
                    phase, back_r, back_c = self.tap_two(tap)
                    left, k = act[phase * R : (phase + 1) * R, :], self.SHIFTS.index((back_r, back_c))
                buf[tap * MID : (tap + 1) * MID, :] = dot_tn(left, patches[:, k * MID : (k + 1) * MID]).astype(BF)

        wide_cols = 9 if stride == 1 else 4
        extra = [pltpu.VMEM((R + 2 * HALO, MID), F32), pltpu.VMEM((R, wide_cols * MID), BF)]
        return self.gradient(ids, chains, kind, [act, dc], parts, heights, held, extra)

    def grad_first(self, ids, chains, xp, dc1, sums, parts, heights):
        def kind(part, refs, buf, tail):
            if part == 0:
                xp, dc1 = refs[0], refs[1]
                for q in range(xp.shape[1] // MID):
                    buf[q * MID : (q + 1) * MID, :] = dot_tn(xp[:, q * MID : (q + 1) * MID], dc1[...]).astype(BF)
            else:
                row = 0
                for first in (3, 0):
                    for name in ("1", "2", "3", "S", "4", "5", "6"):
                        ref = refs[2 + ("1", "2", "3", "4", "5", "6").index("3" if name == "S" else name)]
                        at = first + (8 if name == "S" else 0)
                        total = ref[at : at + 1, :] + ref[at + 1 : at + 2, :] + ref[at + 2 : at + 3, :]
                        for q in range(ref.shape[1] // MID):
                            piece = total[:, q * MID : (q + 1) * MID]
                            buf[row * 16 : row * 16 + 16, :] = jnp.broadcast_to(piece, (16, MID)).astype(BF)
                            row += 1

        return self.gradient(ids, chains, kind, [xp, dc1] + list(sums), parts, heights)


def adam_step(weight, moment_one, moment_two, gradient, step_rate, decay_rate):
    first_new = 0.5 * moment_one + 0.5 * gradient
    second_new = 0.5 * moment_two + 0.5 * gradient * gradient
    correct = 1.0 - 0.5**STEP
    update = first_new / correct / (jnp.sqrt(second_new / correct) + 1e-08) + decay_rate * weight
    return (weight - step_rate * update, first_new, second_new)


BOTH = ("dp", "bn")


def orders(total):
    count = total.bit_length() - 1
    if count == 5:
        return [4, 2, 3, 1, 0], [4, 1, 3, 2, 0], [2, 1, 4, 3, 0]
    return (list(range(count))[::-1],) * 3


def on_device(*args):
    slots_inside = (1, 2, 0, 3)
    images = [jnp.transpose(args[k], slots_inside) for k in (0, 2, 1)]
    lives = (args[3], args[5], args[4])
    ups = [jnp.transpose(args[k], slots_inside) for k in (6, 8, 7)]
    params, firsts, seconds = args[9:17], args[17:25], args[25:33]
    groups, members = lax.axis_size("dp"), lax.axis_size("bn")
    total = groups * members
    pos_dp, pos_bn = lax.axis_index("dp"), lax.axis_index("bn")
    me = pos_dp * members + pos_bn
    grid = Grid([p.shape[2] for p in images], [u.shape[1] for u in ups])

    low = [p.astype(BF) for p in params]
    short_t = low[3].T
    shards = {
        "1": low[0],
        "2": low[1],
        "3": low[2].T,
        "S": jnp.concatenate([short_t[:, :MID], short_t[:, MID:]], axis=0),
        "4": low[4],
        "5": low[5],
        "6": low[6].T,
    }
    unit = {"1": 1, "2": 1, "3": 1, "S": 2, "4": 1, "5": 1, "6": 1}
    rows = {k: v.shape[0] // unit[k] for k, v in shards.items()}
    direct = all(r % 16 == 0 for r in rows.values()) and params[7].shape[0] == MID
    blocks = total if direct else 1
    if not direct:
        rows = {k: r * total for k, r in rows.items()}
    dev = Device(grid, blocks, members)

    spot = jnp.stack([pos_dp, pos_bn]).astype(jnp.int32)
    far = jnp.zeros((1,), jnp.int32)
    near = me.reshape(1).astype(jnp.int32) if direct else far

    def offsets(names):
        where, at = {}, 0
        for k in names:
            where[k] = at
            at += rows[k] * unit[k]
        return where, at

    def packed(names, with_norm=False):
        parts = [shards[k] for k in names]
        if with_norm:
            parts.append(jnp.broadcast_to(low[7].reshape(1, MID), (16, MID)))
        return jnp.concatenate(parts, axis=0) if len(parts) > 1 else parts[0]

    def gather(names):
        buf = packed(names)
        full = lax.all_gather(buf, BOTH, axis=0, tiled=True).reshape(total, buf.shape[0], MID)
        if direct:
            return ([(0, list(range(total)))], [full]), offsets(names)[0]
        pieces, spot_row = [], 0
        for k in names:
            for _ in range(unit[k]):
                r = rows[k] // total
                pieces.append(full[:, spot_row : spot_row + r, :].reshape(rows[k], MID))
                spot_row += r
        return ([(0, [0])], [jnp.concatenate(pieces, axis=0)[None]]), offsets(names)[0]

    def swap(array, bit):
        return lax.ppermute(array, BOTH, [(i, i ^ (1 << bit)) for i in range(total)])

    def butterfly_gather(buf, order):
        held, places, steps = buf[None], [0], []
        for step, bit in enumerate(order):
            got = swap(held, bit)
            steps.append(got)
            there = [r ^ (1 << bit) for r in places]
            if step == len(order) - 1:
                return [places, there], [held, got], steps
            held, places = jnp.concatenate([held, got]), places + there

    def gather_near(names, chains, with_norm=False, after=None):
        if not direct:
            made, where = gather(names)
            return made, where, None
        buf = packed(names, with_norm)
        if after is not None:
            buf = lax.optimization_barrier((buf, after))[0]
        layout, arrays, at, steps = [], [], 0, None
        for height, order in chains:
            places, got, steps = butterfly_gather(buf[at : at + height], order)
            for p, a in zip(places, got):
                layout.append((at, p))
                arrays.append(a)
            at += height
        return (layout, arrays), offsets(names)[0], steps

    def exchange(stat):
        return [stat] + [
            lax.ppermute(stat, "bn", [(i, i ^ k) for i in range(members)]) for k in range(1, members)
        ]

    first, second, third = orders(total)
    r2 = rows["2"] // 48 * 16
    w1, at_1, steps = gather_near(["1"], [(rows["1"] + 16, first)], True)
    w2, at_2, _ = gather_near(
        ["2"],
        [(r2, first), (r2, second), (rows["2"] - 2 * r2, third)],
        after=steps[1] if direct else None,
    )
    wb, at_b = gather(["3", "S", "4", "5", "6"])

    xp, msk, sc = dev.prepare(spot, lives, images)
    if direct:
        c1, st1, normp = dev.conv_one(near, sc, xp, msk, w1, at_1["1"], rows["1"], rows["1"])
    else:
        c1, st1 = dev.conv_one(near, sc, xp, msk, w1, at_1["1"], rows["1"], None)
        normp = lax.all_gather(low[7], BOTH, axis=0, tiled=True).astype(F32).reshape(32, MID)
    a1, nrm1, c2, st2 = dev.conv_two(near, sc, c1, exchange(st1), normp, msk, w2, at_2["2"], rows["2"])
    cs, sts = dev.conv_short(far, sc, xp, msk, wb, at_b["S"], rows["S"])
    a2, nrm2, c3, st3 = dev.conv_expand(
        far, sc, c2, exchange(st2), normp, msk, wb, at_b["3"], rows["3"], "2", sts
    )
    h, hb, nrm3, nrms, c4, st4 = dev.conv_four(
        far, sc, c3, cs, exchange(st3), normp, msk, wb, at_b["4"], rows["4"]
    )
    a4, nrm4, c5, st5 = dev.conv_five(far, sc, c4, exchange(st4), normp, msk, wb, at_b["5"], rows["5"])
    a5, nrm5, c6, st6 = dev.conv_expand(far, sc, c5, exchange(st5), normp, msk, wb, at_b["6"], rows["6"], "5")
    oc, oa, ob, dz6, nrm6, su6 = dev.finish(sc, c6, h, exchange(st6), normp, msk, ups)

    def split_places(order):
        places = [0]
        for bit in reversed(order[1:]):
            places = places + [r ^ (1 << bit) for r in places]
        return [places, [r ^ (1 << order[0]) for r in places]]

    def butterfly_scatter(pieces, order):
        kept, sent = [pieces[0]], pieces[1]
        for step, bit in enumerate(order):
            kept.append(swap(sent, bit))
            if step < len(order) - 1:
                half = kept[0].shape[0] // 2
                sent = sum([k[half:].astype(F32) for k in kept[1:]], kept[0][half:].astype(F32)).astype(BF)
                kept = [k[:half] for k in kept]
        return sum([k[0].astype(F32) for k in kept[1:]], kept[0][0].astype(F32))

    def scatter(piece, heights):
        if not direct:
            parts, spot_row = [], 0
            for height in heights:
                parts.append(piece[0, spot_row : spot_row + height].reshape(total, height // total, MID))
                spot_row += height
            piece = jnp.concatenate(parts, axis=1)
        owned = lax.psum_scatter(piece.reshape(-1, MID), BOTH, scatter_dimension=0, tiled=True)
        return owned.astype(F32)

    def scatter_near(pieces, used, heights):
        if not direct:
            return [scatter(pieces[0], heights)]
        return [butterfly_scatter(pieces[2 * c : 2 * c + 2], order) for c, order in enumerate(used)]

    def cut(owned, heights):
        parts, spot_row = [], 0
        for height in heights:
            height = height if direct else height // total
            parts.append(owned[spot_row : spot_row + height])
            spot_row += height
        return parts

    whole = [[list(range(total)) if direct else [0]]]
    back_first, back_second = first[::-1], second[::-1]

    def halves(k):
        if not direct:
            return [rows[k]]
        one = rows[k] // 32 * 16
        return [rows[k] - one, one]

    pair = [back_first, back_second] if direct else [None]
    pair_places = [split_places(order) for order in pair] if direct else whole
    single = [back_first] if direct else [None]
    single_places = [split_places(back_first)] if direct else whole

    dc6, dz5, su5 = dev.back_six(
        far, sc, dz6, c6, nrm6, exchange(su6), normp, msk, c5, nrm5, wb, at_b["6"], rows["6"]
    )
    high = [rows["6"] + rows["5"]]
    g65 = dev.grad_outer(far, whole, [(dc6, a5)], [(rows["6"], [rows["6"]])], high)
    dc5, dz4, su4 = dev.back_five(
        far, sc, dz5, c5, nrm5, exchange(su5), normp, msk, c4, nrm4, wb, at_b["5"], rows["5"]
    )
    g65 = dev.grad_taps(far, whole, a4, dc5, [(rows["5"], [rows["5"]])], high, 1, g65)
    hts65 = [rows["6"], rows["5"]]
    o6, o5 = cut(scatter(g65[0][0], hts65), hts65)

    dc4, dz3, su3 = dev.back_four(
        far, sc, dz4, c4, nrm4, exchange(su4), normp, msk, dz6, c3, nrm3, cs, nrms, wb, at_b["4"], rows["4"]
    )
    part4, part3 = (rows["4"], halves("4")), (rows["3"], halves("3"))
    mid = [a + 3 * b for a, b in zip(part4[1], part3[1])]
    g43 = dev.grad_outer(near, pair_places, [(hb, dc4)], [part4], mid)
    dc3, dcs, dz2, su2 = dev.back_three(
        far, sc, dz3, c3, nrm3, cs, nrms, exchange(su3), normp, msk, c2, nrm2, wb, at_b["3"], rows["3"]
    )
    g43 = dev.grad_short(near, pair_places, a2, dc3, dcs, xp, [part3] * 3, mid, g43)
    got = scatter_near(g43[0], pair, [rows["4"]] + [rows["3"]] * 3)
    cuts = [cut(owned, [part4[1][c]] + [part3[1][c]] * 3) for c, owned in enumerate(got)]
    o4, o3, osa, osb = [jnp.concatenate(p, axis=0) if len(p) > 1 else p[0] for p in zip(*cuts)]

    dc2, dz1, su1 = dev.back_two(
        near, sc, dz2, c2, nrm2, exchange(su2), normp, msk, c1, nrm1, w2, at_2["2"], rows["2"]
    )
    g2 = dev.grad_taps(near, pair_places, a1, dc2, [(rows["2"], halves("2"))], halves("2"), 2)
    got = scatter_near(g2[0], pair, [rows["2"]])
    o2 = jnp.concatenate(got, axis=0) if len(got) > 1 else got[0]
    dc1 = dev.back_one(sc, dz1, c1, nrm1, exchange(su1), normp, msk)
    sums = (su1, su2, su3, su4, su5, su6)
    parts = [(rows["1"], [rows["1"]])] + ([(16, [16])] if direct else [])
    g1 = dev.grad_first(near, single_places, xp, dc1, sums, parts, [sum(p for p, _ in parts)])
    grads = dev.input_grad(near, dc1, dcs, w1, at_1["1"], rows["1"], far, wb, at_b["S"], rows["S"], images)
    gc_, ga_, gb_ = grads
    last = scatter_near(g1[0], single, [rows["1"]])[0]
    o1 = last[: rows["1"]] if direct else last
    if direct:
        onorm = last[rows["1"]]
    else:

        def three(stat, at):
            return jnp.sum(stat[at : at + 3], axis=0)

        vec = [three(su1, 3), three(su2, 3), three(su3, 3), three(su3, 11), three(su4, 3), three(su5, 3), three(su6, 3)]
        vec += [three(su1, 0), three(su2, 0), three(su3, 0), three(su3, 8), three(su4, 0), three(su5, 0), three(su6, 0)]
        onorm = lax.psum_scatter(jnp.concatenate(vec), BOTH, scatter_dimension=0, tiled=True)
    owned = (o1, o2, o3.T, jnp.concatenate([osa, osb], axis=1).T, o4, o5, o6.T, onorm)
    stepped = []
    for k in range(8):
        rate, decay = (RATE_CONV, DECAY_CONV) if k < 7 else (RATE_NORM, 0.0)
        stepped.extend(adam_step(params[k], firsts[k], seconds[k], owned[k], rate, decay))
    images_out = [jnp.transpose(a, (2, 0, 1, 3)) for a in (oc, oa, ob, gc_, ga_, gb_)]
    order_out = [images_out[k] for k in (0, 2, 1, 3, 5, 4)]
    return (*order_out, *stepped)


def solution(mesh):
    batch = P(BOTH, None, None, None)
    by_row, by_col, flat = P(BOTH, None), P(None, BOTH), P(BOTH)
    weights = (by_row, by_row, by_col, by_col, by_row, by_row, by_col, flat)
    triple = tuple(spec for spec in weights for _ in range(3))
    return jax.shard_map(
        on_device,
        mesh=mesh,
        in_specs=(batch,) * 3 + (P(),) * 3 + (batch,) * 3 + weights * 3,
        out_specs=(batch,) * 6 + triple,
        check_vma=False,
    )
```

```python
import jax
import jax.numpy as jnp
import numpy as np
from jax import lax
from jax.experimental import pallas as pl
from jax.experimental.pallas import tpu as pltpu
from jax.sharding import PartitionSpec as P

STEP = 10
EPSILON = 1e-05
RATE_CONV = 0.03
RATE_NORM = 0.4
DECAY_CONV = 0.05
BF = jnp.bfloat16
F32 = jnp.float32
MID = 512
HALO = 32
UNROLL = 4
NORM_ROW = {"1": 0, "2": 1, "3": 2, "S": 6, "4": 10, "5": 11, "6": 12}


class Grid:
    def __init__(self, counts, sides):
        self.counts, self.sides = counts, sides
        self.seg, self.size = [], []
        at = 0
        for number, side in zip(counts, sides):
            rows = -(-number * (side + 1) ** 2 // 16) * 16
            self.seg.append(at)
            self.size.append(rows)
            at += rows
        self.rows = at

    def lines(self):
        for which, (number, side) in enumerate(zip(self.counts, self.sides)):
            for line in range(side):
                for column in range(side):
                    yield which, line, column, self.seg[which] + (line * (side + 1) + column) * number


def silu(v):
    return v * jax.nn.sigmoid(v)


def slope(v):
    s = jax.nn.sigmoid(v)
    return s * (1.0 + v * (1.0 - s))


def dot_nn(a, b):
    return lax.dot_general(a, b, (((1,), (0,)), ((), ())), preferred_element_type=F32)


def dot_nt(a, b):
    return lax.dot_general(a, b, (((1,), (1,)), ((), ())), preferred_element_type=F32)


def dot_tn(a, b):
    return lax.dot_general(a, b, (((0,), (0,)), ((), ())), preferred_element_type=F32)


def aligned(row):
    return row if isinstance(row, int) else pl.multiple_of(row, 16)


def wide(mask):
    return jnp.concatenate([mask] * (MID // 128), axis=1)


VM = pl.BlockSpec(memory_space=pltpu.VMEM)
SM = pl.BlockSpec(memory_space=pltpu.SMEM)
HB = pl.BlockSpec(memory_space=pl.ANY)


def call(body, ins, outs, scratch=(), flops=0, moved=0, aliases=None):
    return pl.pallas_call(
        body,
        out_shape=[jax.ShapeDtypeStruct(shape, dtype) for shape, dtype, _ in outs],
        in_specs=[spec for _, spec in ins],
        out_specs=[spec for _, _, spec in outs],
        scratch_shapes=list(scratch),
        input_output_aliases=aliases or {},
        compiler_params=pltpu.CompilerParams(vmem_limit_bytes=58 * 1024 * 1024),
        cost_estimate=pl.CostEstimate(flops=flops, bytes_accessed=moved, transcendentals=0),
    )(*[array for array, _ in ins])


class Device:
    def __init__(self, grid, blocks, members):
        self.g = grid
        self.blocks = blocks
        self.members = members
        self.R = grid.rows


    def sweep(self, cols, make, st=None, sums=()):
        for which in range(3):
            start, count = self.g.seg[which], self.g.size[which] // 16
            for q in range(cols // MID):
                lane = slice(q * MID, (q + 1) * MID)
                work = make(which, q, lane)

                def add(acc, row, work=work):
                    terms = work(aligned(row)) or ()
                    return tuple(a + t[:8] + t[8:] for a, t in zip(acc, terms))

                def trip(i, acc, start=start, add=add):
                    for j in range(UNROLL):
                        acc = add(acc, start + (i * UNROLL + j) * 16)
                    return acc

                acc = tuple(jnp.zeros((8, MID), F32) for _ in sums)
                trips = count // UNROLL
                acc = lax.fori_loop(0, trips, trip, acc)
                for j in range(trips * UNROLL, count):
                    acc = add(acc, start + j * 16)
                for row, a in zip(sums, acc):
                    st[row + which : row + which + 1, lane] = jnp.sum(a, axis=0, keepdims=True)

    def normal(self, c, nrm, which, lane=slice(0, MID)):
        mean, rstd = nrm[which : which + 1, lane], nrm[3 + which : 4 + which, lane]
        return lambda row: (c[pl.ds(row, 16), lane] - mean) * rstd

    def scaled(self, normp, name, q):
        at = NORM_ROW[name] + q
        gain, bias = normp[at : at + 1, :], normp[16 + at : 17 + at, :]
        return lambda xh: gain * xh + bias

    def backed(self, normp, name, q, nrm, sums, which, lane=slice(0, MID)):
        at = NORM_ROW[name] + q
        a, b = sums[which : which + 1, lane], sums[3 + which : 4 + which, lane]
        scale = normp[at : at + 1, :] * nrm[3 + which : 4 + which, lane]
        return lambda dz, xh, m: scale * (dz - m * (a + xh * b))

    def load_start(self, layout, ids, refs, off, rows, dst, sem):
        for ref, (base, places) in zip(refs, layout):
            low, high = max(base, off), min(base + ref.shape[1], off + rows)
            if high <= low:
                continue
            for pos, rel in enumerate(places):
                block = rel ^ ids[0]
                pltpu.make_async_copy(
                    ref.at[pos, pl.ds(low - base, high - low), :],
                    dst.at[pl.ds(pl.multiple_of(block * rows + (low - off), 16), high - low), :],
                    sem,
                ).start()

    def load_wait(self, dst, sem):
        pltpu.make_async_copy(dst, dst, sem).wait()

    def store_start(self, chains, ids, src, rows, split, offs, refs, sems):
        at, lo = 0, 0
        for places_list, take, off in zip(chains, split, offs):
            for places in places_list:
                for pos, rel in enumerate(places):
                    block = rel ^ ids[0]
                    pltpu.make_async_copy(
                        src.at[pl.ds(pl.multiple_of(block * rows + lo, 16), take), :],
                        refs[at].at[pos, pl.ds(off, take), :],
                        sems.at[at],
                    ).start()
                at += 1
            lo += take

    def store_wait(self, refs, sems, spans):
        for which, (ref, (off, size)) in enumerate(zip(refs, spans)):
            view = ref.at[:, pl.ds(off, size), :]
            pltpu.make_async_copy(view, view, sems.at[which]).wait()

    def local_stats(self, c_ref, m_ref, sc, out_ref, at, area, phases=1):
        cols = c_ref.shape[1]
        out_ref[pl.ds(at, 8), :] = jnp.zeros((8, cols), F32)
        def make(which, q, lane):
            start = self.g.seg[which]
            base = c_ref[start : start + 1, lane]

            def work(row):
                m = wide(m_ref[pl.ds(row, 16), :])
                total = square = None
                for phase in range(phases):
                    d = c_ref[pl.ds(aligned(row + phase * self.R), 16), lane] - base
                    v = d * m
                    total = v if total is None else total + v
                    square = v * d if square is None else square + v * d
                return total, square

            return work

        self.sweep(cols, make, out_ref, (at, at + 3))
        for which in range(3):
            held = sc[0, which] * float(area[which])
            base = c_ref[self.g.seg[which] : self.g.seg[which] + 1, :]
            total = out_ref[at + which : at + which + 1, :]
            out_ref[at + which : at + which + 1, :] = total + held * base
            square = out_ref[at + 3 + which : at + 4 + which, :]
            out_ref[at + 3 + which : at + 4 + which, :] = square - total * (total / held)

    def group_norm(self, st_refs, at, sc, area, out_ref):
        cols = out_ref.shape[1]
        out_ref[...] = jnp.zeros(out_ref.shape, F32)
        for which in range(3):
            count = sc[self.members, which] * float(area[which])
            sums = [ref[at + which : at + which + 1, :] for ref in st_refs]
            mean = sum(sums[1:], sums[0]) / count
            spread = jnp.zeros((1, cols), F32)
            for k, ref in enumerate(st_refs):
                held = sc[k, which] * float(area[which])
                apart = sums[k] / held - mean
                spread = spread + (ref[at + 3 + which : at + 4 + which, :] + held * apart * apart)
            out_ref[which : which + 1, :] = mean
            out_ref[3 + which : 4 + which, :] = lax.rsqrt(spread / count + EPSILON)

    def group_sums(self, st_refs, at, sc, area, out_ref):
        out_ref[...] = jnp.zeros(out_ref.shape, F32)
        for which in range(3):
            count = sc[self.members, which] * float(area[which])
            for row in (which, 3 + which):
                rows = [ref[at + row : at + row + 1, :] for ref in st_refs]
                out_ref[row : row + 1, :] = sum(rows[1:], rows[0]) / count

    def shifted(self, hs_ref, dst_ref, col, sign_r, sign_c):
        for which in range(3):
            off = (sign_r * (self.g.sides[which] + 1) + sign_c) * self.g.counts[which]
            for i in range(self.g.size[which] // 16):
                row = self.g.seg[which] + i * 16
                dst_ref[row : row + 16, col : col + MID] = hs_ref[HALO + row + off : HALO + row + off + 16, :].astype(BF)

    def clear_halo(self, hs_ref):
        hs_ref[0:HALO, :] = jnp.zeros((HALO, MID), F32)
        hs_ref[HALO + self.R : 2 * HALO + self.R, :] = jnp.zeros((HALO, MID), F32)

    def area(self, side_scale):
        return [(side_scale * side) ** 2 for side in self.g.sides]


    def prepare(self, spot, lives, pictures):
        R = self.R
        g = self.g
        width = pictures[0].shape[3]
        members = self.members

        def body(spot, la, lb, lc, xa, xb, xc, xp, msk, sc, big):
            x_refs, l_refs = (xa, xb, xc), (la, lb, lc)
            own = []
            for which in range(3):
                per = g.counts[which]
                whole = jnp.zeros((), jnp.int32)
                for k in range(members):
                    first = (spot[0] * members + (spot[1] ^ k)) * per
                    flags = [l_refs[which][first + i] for i in range(per)]
                    held = sum(flags[1:], flags[0])
                    sc[k, which] = held.astype(F32)
                    whole = whole + held
                    if k == 0:
                        own.append(flags)
                sc[members, which] = whole.astype(F32)
            big[...] = jnp.zeros(big.shape, F32)
            msk[...] = jnp.zeros(msk.shape, F32)
            alive = []
            for which in range(3):
                per = g.counts[which]
                slot = lax.broadcasted_iota(jnp.int32, (per, 128), 0)
                mask = jnp.zeros((per, 128), F32)
                for i in range(per):
                    mask = jnp.where(slot == i, own[which][i].astype(F32), mask)
                alive.append(mask)
            for which, line, column, row in g.lines():
                per = g.counts[which]
                msk[row : row + per, :] = alive[which]
                for phase in range(4):
                    odd, second = divmod(phase, 2)
                    base = phase * R + row
                    big[base : base + per, :] = x_refs[which][2 * line + odd, 2 * column + second].astype(F32)

            def cast(i, _):
                row = aligned(i * 16)
                xp[pl.ds(row, 16), :] = big[pl.ds(row, 16), :].astype(BF)
                return 0

            lax.fori_loop(0, 4 * R // 16, cast, 0)

        return call(
            body,
            [(spot, SM)] + [(l, SM) for l in lives] + [(p, VM) for p in pictures],
            [((4 * R, width), BF, VM), ((R, 128), F32, VM), ((members + 1, 3), F32, SM)],
            [pltpu.VMEM((4 * R, width), F32)],
        )

    def conv_one(self, ids, sc, xp, msk, w, off, rows):
        R = self.R
        width = xp.shape[1]
        layout, arrays = w

        def body(ids, sc, xp, msk, *rest):
            refs = rest[: len(arrays)]
            c, st, ws, sem = rest[len(arrays) :]
            self.load_start(layout, ids, refs, off, rows, ws, sem)
            self.load_wait(ws, sem)
            for phase in range(4):
                c[phase * R : (phase + 1) * R, :] = dot_nn(xp[phase * R : (phase + 1) * R, :], ws[...])
            self.local_stats(c, msk, sc, st, 0, self.area(2), 4)

        return call(
            body,
            [(ids, SM), (sc, SM), (xp, VM), (msk, VM)] + [(a, HB) for a in arrays],
            [((4 * R, MID), F32, VM), ((8, MID), F32, VM)],
            [pltpu.VMEM((width, MID), BF), pltpu.SemaphoreType.DMA],
            flops=2 * 4 * R * width * MID,
        )

    @staticmethod
    def tap_two(tap):
        i, j = divmod(tap, 3)
        return (0 if i == 1 else 2) + (0 if j == 1 else 1), (1 if i == 0 else 0), (1 if j == 0 else 0)

    def conv_two(self, ids, sc, c1, sts, normp, msk, w, off, rows, norm_off=None):
        R = self.R
        layout, arrays = w
        nst, nw = len(sts), len(arrays)
        with_norm = norm_off is not None

        def body(ids, sc, c1, msk, *rest):
            st_refs, refs, rest = rest[:nst], rest[nst : nst + nw], rest[nst + nw :]
            if with_norm:
                a1, nrm, c2, st, normp, ws, hs, patches, sem, ns, sem2 = rest
                self.load_start(layout, ids, refs, norm_off, 16, ns, sem2)
            else:
                normp, a1, nrm, c2, st, ws, hs, patches, sem = rest
            self.load_start(layout, ids, refs, off, rows, ws, sem)
            self.group_norm(st_refs, 0, sc, self.area(2), nrm)
            self.clear_halo(hs)
            if with_norm:
                self.load_wait(ns, sem2)
                for b in range(self.blocks):
                    normp[b : b + 1, :] = ns[b * 16 : b * 16 + 16, :].astype(F32)[0:1, :]
            for phase in range(4):

                def make(which, q, lane, phase=phase):
                    xh, put = self.normal(c1, nrm, which), self.scaled(normp, "1", 0)

                    def work(row):
                        at = aligned(row + phase * R)
                        v = silu(put(xh(at))) * wide(msk[pl.ds(row, 16), :])
                        hs[pl.ds(aligned(row + HALO), 16), :] = v
                        a1[pl.ds(at, 16), :] = v.astype(BF)

                    return work

                self.sweep(MID, make)
                for tap in range(9):
                    source, back_r, back_c = self.tap_two(tap)
                    if source == phase:
                        self.shifted(hs, patches, tap * MID, -back_r, -back_c)
            self.load_wait(ws, sem)
            c2[...] = dot_nn(patches[...], ws[...])
            self.local_stats(c2, msk, sc, st, 0, self.area(1))

        ins = [(ids, SM), (sc, SM), (c1, VM), (msk, VM)] + [(s, VM) for s in sts] + [(a, HB) for a in arrays]
        outs = [((4 * R, MID), BF, VM), ((8, MID), F32, VM), ((R, MID), F32, VM), ((8, MID), F32, VM)]
        scratch = [
            pltpu.VMEM((9 * MID, MID), BF),
            pltpu.VMEM((R + 2 * HALO, MID), F32),
            pltpu.VMEM((R, 9 * MID), BF),
            pltpu.SemaphoreType.DMA,
        ]
        if with_norm:
            outs.append(((self.blocks, MID), F32, VM))
            scratch += [pltpu.VMEM((self.blocks * 16, MID), BF), pltpu.SemaphoreType.DMA]
        else:
            ins.append((normp, VM))
        return call(body, ins, outs, scratch, flops=2 * 9 * R * MID * MID)

    def conv_short(self, ids, sc, xp, msk, w, off, rows):
        R = self.R
        layout, arrays = w
        nw = len(arrays)
        out_width = self.blocks * rows if self.blocks > 1 else rows

        def body(ids, sc, xp, msk, *rest):
            refs = rest[:nw]
            c, st, wa, wb, sem = rest[nw:]
            self.load_start(layout, ids, refs, off, rows, wa, sem.at[0])
            self.load_start(layout, ids, refs, off + rows, rows, wb, sem.at[1])
            self.load_wait(wa, sem.at[0])
            self.load_wait(wb, sem.at[1])
            for q in range(out_width // MID):
                lane = slice(q * MID, (q + 1) * MID)
                c[:, lane] = dot_nt(xp[0:R, 0:MID], wa[lane, :]) + dot_nt(xp[0:R, MID : 2 * MID], wb[lane, :])
            self.local_stats(c, msk, sc, st, 0, self.area(1))

        return call(
            body,
            [(ids, SM), (sc, SM), (xp, VM), (msk, VM)] + [(a, HB) for a in arrays],
            [((R, out_width), F32, VM), ((8, out_width), F32, VM)],
            [pltpu.VMEM((out_width, MID), BF), pltpu.VMEM((out_width, MID), BF), pltpu.SemaphoreType.DMA((2,))],
            flops=2 * R * 2 * MID * out_width,
        )

    def conv_expand(self, ids, sc, c, sts, normp, msk, w, off, rows, name, more=None):
        R = self.R
        layout, arrays = w
        nst, nw = len(sts), len(arrays)
        out_width = self.blocks * rows if self.blocks > 1 else rows
        stat_rows = 8 if more is None else 16

        def body(ids, sc, c, normp, msk, *rest):
            st_refs, refs = rest[:nst], rest[nst : nst + nw]
            rest = rest[nst + nw :]
            if more is not None:
                more_ref, rest = rest[0], rest[1:]
            act, nrm, prod, st, ws, sem = rest
            self.load_start(layout, ids, refs, off, rows, ws, sem)
            self.group_norm(st_refs, 0, sc, self.area(1), nrm)

            def make(which, q, lane):
                xh, put = self.normal(c, nrm, which), self.scaled(normp, name, 0)

                def work(row):
                    v = silu(put(xh(row))) * wide(msk[pl.ds(row, 16), :])
                    act[pl.ds(row, 16), :] = v.astype(BF)

                return work

            self.sweep(MID, make)
            self.load_wait(ws, sem)
            for q in range(out_width // MID):
                lane = slice(q * MID, (q + 1) * MID)
                prod[:, lane] = dot_nt(act[...], ws[lane, :])
            self.local_stats(prod, msk, sc, st, 0, self.area(1))
            if more is not None:
                st[8:16, :] = more_ref[...]

        ins = [(ids, SM), (sc, SM), (c, VM), (normp, VM), (msk, VM)] + [(s, VM) for s in sts] + [(a, HB) for a in arrays]
        if more is not None:
            ins.append((more, VM))
        return call(
            body,
            ins,
            [((R, MID), BF, VM), ((8, MID), F32, VM), ((R, out_width), F32, VM), ((stat_rows, out_width), F32, VM)],
            [pltpu.VMEM((out_width, MID), BF), pltpu.SemaphoreType.DMA],
            flops=2 * R * MID * out_width,
        )

    def conv_four(self, ids, sc, c3, cs, sts, normp, msk, w, off, rows):
        R = self.R
        layout, arrays = w
        nst, nw = len(sts), len(arrays)
        out_width = c3.shape[1]

        def body(ids, sc, c3, cs, normp, msk, *rest):
            st_refs, refs = rest[:nst], rest[nst : nst + nw]
            h_far, hb_far, nrm3, nrms, c4, st, ws, h, hb, sem, sems = rest[nst + nw :]
            self.load_start(layout, ids, refs, off, rows, ws, sem)
            self.group_norm(st_refs, 0, sc, self.area(1), nrm3)
            self.group_norm(st_refs, 8, sc, self.area(1), nrms)

            def make(which, q, lane):
                xh3, put3 = self.normal(c3, nrm3, which, lane), self.scaled(normp, "3", q)
                xhs, puts = self.normal(cs, nrms, which, lane), self.scaled(normp, "S", q)

                def work(row):
                    v = silu(put3(xh3(row)) + puts(xhs(row))) * wide(msk[pl.ds(row, 16), :])
                    h[pl.ds(row, 16), lane] = v
                    hb[pl.ds(row, 16), lane] = v.astype(BF)

                return work

            self.sweep(out_width, make)
            out = [pltpu.make_async_copy(h, h_far, sems.at[0]), pltpu.make_async_copy(hb, hb_far, sems.at[1])]
            for copy in out:
                copy.start()
            self.load_wait(ws, sem)
            c4[...] = dot_nn(hb[...], ws[...])
            self.local_stats(c4, msk, sc, st, 0, self.area(1))
            for copy in out:
                copy.wait()

        return call(
            body,
            [(ids, SM), (sc, SM), (c3, VM), (cs, VM), (normp, VM), (msk, VM)]
            + [(s, VM) for s in sts]
            + [(a, HB) for a in arrays],
            [
                ((R, out_width), F32, HB),
                ((R, out_width), BF, HB),
                ((8, out_width), F32, VM),
                ((8, out_width), F32, VM),
                ((R, MID), F32, VM),
                ((8, MID), F32, VM),
            ],
            [
                pltpu.VMEM((out_width, MID), BF),
                pltpu.VMEM((R, out_width), F32),
                pltpu.VMEM((R, out_width), BF),
                pltpu.SemaphoreType.DMA,
                pltpu.SemaphoreType.DMA((2,)),
            ],
            flops=2 * R * MID * out_width,
        )

    def conv_five(self, ids, sc, c4, sts, normp, msk, w, off, rows):
        R = self.R
        layout, arrays = w
        nst, nw = len(sts), len(arrays)

        def body(ids, sc, c4, normp, msk, *rest):
            st_refs, refs = rest[:nst], rest[nst : nst + nw]
            a4, nrm, c5, st, ws, hs, patches, sem = rest[nst + nw :]
            self.load_start(layout, ids, refs, off, rows, ws, sem)
            self.group_norm(st_refs, 0, sc, self.area(1), nrm)
            self.clear_halo(hs)

            def make(which, q, lane):
                xh, put = self.normal(c4, nrm, which), self.scaled(normp, "4", 0)

                def work(row):
                    v = silu(put(xh(row))) * wide(msk[pl.ds(row, 16), :])
                    hs[pl.ds(aligned(row + HALO), 16), :] = v
                    a4[pl.ds(row, 16), :] = v.astype(BF)

                return work

            self.sweep(MID, make)
            for tap in range(9):
                i, j = divmod(tap, 3)
                self.shifted(hs, patches, tap * MID, i - 1, j - 1)
            self.load_wait(ws, sem)
            c5[...] = dot_nn(patches[...], ws[...])
            self.local_stats(c5, msk, sc, st, 0, self.area(1))

        return call(
            body,
            [(ids, SM), (sc, SM), (c4, VM), (normp, VM), (msk, VM)] + [(s, VM) for s in sts] + [(a, HB) for a in arrays],
            [((R, MID), BF, VM), ((8, MID), F32, VM), ((R, MID), F32, VM), ((8, MID), F32, VM)],
            [
                pltpu.VMEM((9 * MID, MID), BF),
                pltpu.VMEM((R + 2 * HALO, MID), F32),
                pltpu.VMEM((R, 9 * MID), BF),
                pltpu.SemaphoreType.DMA,
            ],
            flops=2 * 9 * R * MID * MID,
        )

    def finish(self, sc, c6, h, sts, normp, msk, ups):
        R = self.R
        g = self.g
        nst = len(sts)
        out_width = c6.shape[1]

        def body(sc, c6, h, normp, msk, ua, ub, uc, *rest):
            st_refs = rest[:nst]
            oa, ob, oc, dz, nrm, st, up, res = rest[nst:]
            u_refs, o_refs = (ua, ub, uc), (oa, ob, oc)
            self.group_norm(st_refs, 0, sc, self.area(1), nrm)
            up[...] = jnp.zeros(up.shape, F32)
            st[...] = jnp.zeros(st.shape, F32)
            for which, line, column, row in g.lines():
                up[row : row + g.counts[which], :] = u_refs[which][line, column].astype(F32)

            def make(which, q, lane):
                xh6, put = self.normal(c6, nrm, which, lane), self.scaled(normp, "6", q)

                def work(row):
                    m = wide(msk[pl.ds(row, 16), :])
                    xh = xh6(row)
                    pre = put(xh) + h[pl.ds(row, 16), lane]
                    s = jax.nn.sigmoid(pre)
                    res[pl.ds(row, 16), lane] = m * (pre * s)
                    d = up[pl.ds(row, 16), lane] * m * (s * (1.0 + pre * (1.0 - s)))
                    dz[pl.ds(row, 16), lane] = d
                    return d, d * xh

                return work

            self.sweep(out_width, make, st, (0, 3))
            for which, line, column, row in g.lines():
                o_refs[which][line, column] = res[row : row + g.counts[which], :].astype(BF)

        return call(
            body,
            [(sc, SM), (c6, VM), (h, VM), (normp, VM), (msk, VM)] + [(u, VM) for u in ups] + [(s, VM) for s in sts],
            [(u.shape, BF, VM) for u in ups]
            + [((R, out_width), F32, VM), ((8, out_width), F32, VM), ((8, out_width), F32, VM)],
            [pltpu.VMEM((R, out_width), F32), pltpu.VMEM((R, out_width), F32)],
        )

    def back_six(self, ids, sc, dz, c6, nrm6, sts, normp, msk, c5, nrm5, w, off, rows):
        R = self.R
        layout, arrays = w
        nst, nw = len(sts), len(arrays)
        out_width = c6.shape[1]

        def body(ids, sc, dz, c6, nrm6, normp, msk, c5, nrm5, *rest):
            st_refs, refs = rest[:nst], rest[nst : nst + nw]
            dc, dz5, st, sums, ws, sem = rest[nst + nw :]
            self.load_start(layout, ids, refs, off, rows, ws, sem)
            self.group_sums(st_refs, 0, sc, self.area(1), sums)
            st[...] = jnp.zeros(st.shape, F32)

            def make(which, q, lane):
                xh, back = self.normal(c6, nrm6, which, lane), self.backed(normp, "6", q, nrm6, sums, which, lane)

                def work(row):
                    m = wide(msk[pl.ds(row, 16), :])
                    dc[pl.ds(row, 16), lane] = back(dz[pl.ds(row, 16), lane], xh(row), m).astype(BF)

                return work

            self.sweep(out_width, make)
            self.load_wait(ws, sem)
            dz5[...] = dot_nn(dc[...], ws[...])
            self.through(dz5, c5, nrm5, normp, "5", msk, st)

        return call(
            body,
            [(ids, SM), (sc, SM), (dz, VM), (c6, VM), (nrm6, VM), (normp, VM), (msk, VM), (c5, VM), (nrm5, VM)]
            + [(s, VM) for s in sts]
            + [(a, HB) for a in arrays],
            [((R, out_width), BF, VM), ((R, MID), F32, VM), ((8, MID), F32, VM)],
            [pltpu.VMEM((8, out_width), F32), pltpu.VMEM((out_width, MID), BF), pltpu.SemaphoreType.DMA],
            flops=2 * R * MID * out_width,
        )

    def through(self, dz, c, nrm, normp, name, msk, st, phases=1):
        def make(which, q, lane):
            xhat, put = self.normal(c, nrm, which), self.scaled(normp, name, 0)

            def work(row):
                m = wide(msk[pl.ds(row, 16), :])
                one = two = None
                for phase in range(phases):
                    at = aligned(row + phase * self.R)
                    xh = xhat(at)
                    d = dz[pl.ds(at, 16), :] * slope(put(xh)) * m
                    dz[pl.ds(at, 16), :] = d
                    one = d if one is None else one + d
                    two = d * xh if two is None else two + d * xh
                return one, two

            return work

        self.sweep(MID, make, st, (0, 3))

    def back_five(self, ids, sc, dz5, c5, nrm5, sts, normp, msk, c4, nrm4, w, off, rows):
        R = self.R
        layout, arrays = w
        nst, nw = len(sts), len(arrays)

        def body(ids, sc, dz5, c5, nrm5, normp, msk, c4, nrm4, *rest):
            st_refs, refs = rest[:nst], rest[nst : nst + nw]
            dc, dz4, st, sums, ws, hs, patches, sem = rest[nst + nw :]
            self.load_start(layout, ids, refs, off, rows, ws, sem)
            self.group_sums(st_refs, 0, sc, self.area(1), sums)
            self.clear_halo(hs)
            st[...] = jnp.zeros(st.shape, F32)
            self.own_dc(dz5, c5, nrm5, sums, normp, "5", msk, dc, hs)
            for tap in range(9):
                i, j = divmod(tap, 3)
                self.shifted(hs, patches, tap * MID, 1 - i, 1 - j)
            self.load_wait(ws, sem)
            for tap in range(9):
                part = dot_nt(patches[:, tap * MID : (tap + 1) * MID], ws[tap * MID : (tap + 1) * MID, :])
                if tap == 0:
                    dz4[...] = part
                else:
                    dz4[...] += part
            self.through(dz4, c4, nrm4, normp, "4", msk, st)

        return call(
            body,
            [(ids, SM), (sc, SM), (dz5, VM), (c5, VM), (nrm5, VM), (normp, VM), (msk, VM), (c4, VM), (nrm4, VM)]
            + [(s, VM) for s in sts]
            + [(a, HB) for a in arrays],
            [((R, MID), BF, VM), ((R, MID), F32, VM), ((8, MID), F32, VM)],
            [
                pltpu.VMEM((8, MID), F32),
                pltpu.VMEM((9 * MID, MID), BF),
                pltpu.VMEM((R + 2 * HALO, MID), F32),
                pltpu.VMEM((R, 9 * MID), BF),
                pltpu.SemaphoreType.DMA,
            ],
            flops=2 * 9 * R * MID * MID,
        )

    def own_dc(self, dz, c, nrm, sums, normp, name, msk, dc, hs=None, phases=1):
        def make(which, q, lane):
            xh, back = self.normal(c, nrm, which), self.backed(normp, name, 0, nrm, sums, which)

            def work(row):
                m = wide(msk[pl.ds(row, 16), :])
                for phase in range(phases):
                    at = aligned(row + phase * self.R)
                    v = back(dz[pl.ds(at, 16), :], xh(at), m)
                    dc[pl.ds(at, 16), :] = v.astype(BF)
                    if hs is not None:
                        hs[pl.ds(aligned(row + HALO), 16), :] = v

            return work

        self.sweep(MID, make)

    def back_four(self, ids, sc, dz4, c4, nrm4, sts, normp, msk, dz6, c3, nrm3, cs, nrms, w, off, rows):
        R = self.R
        layout, arrays = w
        nst, nw = len(sts), len(arrays)
        out_width = c3.shape[1]

        def body(ids, sc, dz4, c4, nrm4, normp, msk, dz6_far, c3_far, nrm3, cs_far, nrms, *rest):
            st_refs, refs = rest[:nst], rest[nst : nst + nw]
            dc, dz3, st, sums, ws, dz6, c3, cs, sem, sems = rest[nst + nw :]
            self.load_start(layout, ids, refs, off, rows, ws, sem)
            late = [
                pltpu.make_async_copy(far, held, sems.at[k])
                for k, (far, held) in enumerate(((dz6_far, dz6), (c3_far, c3), (cs_far, cs)))
            ]
            for copy in late:
                copy.start()
            self.group_sums(st_refs, 0, sc, self.area(1), sums)
            st[...] = jnp.zeros(st.shape, F32)
            self.own_dc(dz4, c4, nrm4, sums, normp, "4", msk, dc)
            self.load_wait(ws, sem)
            for q in range(out_width // MID):
                lane = slice(q * MID, (q + 1) * MID)
                dz3[:, lane] = dot_nt(dc[...], ws[lane, :])
            for copy in late:
                copy.wait()

            def make(which, q, lane):
                xhat3, put3 = self.normal(c3, nrm3, which, lane), self.scaled(normp, "3", q)
                xhats, puts = self.normal(cs, nrms, which, lane), self.scaled(normp, "S", q)

                def work(row):
                    xh3, xhs = xhat3(row), xhats(row)
                    d = (dz6[pl.ds(row, 16), lane] + dz3[pl.ds(row, 16), lane]) * slope(put3(xh3) + puts(xhs))
                    d = d * wide(msk[pl.ds(row, 16), :])
                    dz3[pl.ds(row, 16), lane] = d
                    return d, d * xh3, d * xhs

                return work

            self.sweep(out_width, make, st, (0, 3, 11))
            st[8:11, :] = st[0:3, :]

        return call(
            body,
            [(ids, SM), (sc, SM), (dz4, VM), (c4, VM), (nrm4, VM), (normp, VM), (msk, VM)]
            + [(dz6, HB), (c3, HB), (nrm3, VM), (cs, HB), (nrms, VM)]
            + [(s, VM) for s in sts]
            + [(a, HB) for a in arrays],
            [((R, MID), BF, VM), ((R, out_width), F32, VM), ((16, out_width), F32, VM)],
            [pltpu.VMEM((8, MID), F32), pltpu.VMEM((out_width, MID), BF)]
            + [pltpu.VMEM((R, out_width), F32)] * 3
            + [pltpu.SemaphoreType.DMA, pltpu.SemaphoreType.DMA((3,))],
            flops=2 * R * MID * out_width,
        )

    def back_three(self, ids, sc, dz3, c3, nrm3, cs, nrms, sts, normp, msk, c2, nrm2, w, off, rows):
        R = self.R
        layout, arrays = w
        nst, nw = len(sts), len(arrays)
        out_width = c3.shape[1]

        def body(ids, sc, dz3, c3, nrm3, cs, nrms, normp, msk, c2, nrm2, *rest):
            st_refs, refs = rest[:nst], rest[nst : nst + nw]
            dc3_far, dcs_far, dz2, st, sums3, sumss, ws, dc3, dcs, sem, sems = rest[nst + nw :]
            self.load_start(layout, ids, refs, off, rows, ws, sem)
            self.group_sums(st_refs, 0, sc, self.area(1), sums3)
            self.group_sums(st_refs, 8, sc, self.area(1), sumss)
            st[...] = jnp.zeros(st.shape, F32)

            def make(which, q, lane):
                xh3, back3 = self.normal(c3, nrm3, which, lane), self.backed(normp, "3", q, nrm3, sums3, which, lane)
                xhs, backs = self.normal(cs, nrms, which, lane), self.backed(normp, "S", q, nrms, sumss, which, lane)

                def work(row):
                    m = wide(msk[pl.ds(row, 16), :])
                    d = dz3[pl.ds(row, 16), lane]
                    dc3[pl.ds(row, 16), lane] = back3(d, xh3(row), m).astype(BF)
                    dcs[pl.ds(row, 16), lane] = backs(d, xhs(row), m).astype(BF)

                return work

            self.sweep(out_width, make)
            out = [pltpu.make_async_copy(dc3, dc3_far, sems.at[0]), pltpu.make_async_copy(dcs, dcs_far, sems.at[1])]
            for copy in out:
                copy.start()
            self.load_wait(ws, sem)
            dz2[...] = dot_nn(dc3[...], ws[...])
            self.through(dz2, c2, nrm2, normp, "2", msk, st)
            for copy in out:
                copy.wait()

        return call(
            body,
            [(ids, SM), (sc, SM), (dz3, VM), (c3, VM), (nrm3, VM), (cs, VM), (nrms, VM), (normp, VM), (msk, VM)]
            + [(c2, VM), (nrm2, VM)]
            + [(s, VM) for s in sts]
            + [(a, HB) for a in arrays],
            [((R, out_width), BF, HB), ((R, out_width), BF, HB), ((R, MID), F32, VM), ((8, MID), F32, VM)],
            [
                pltpu.VMEM((8, out_width), F32),
                pltpu.VMEM((8, out_width), F32),
                pltpu.VMEM((out_width, MID), BF),
                pltpu.VMEM((R, out_width), BF),
                pltpu.VMEM((R, out_width), BF),
                pltpu.SemaphoreType.DMA,
                pltpu.SemaphoreType.DMA((2,)),
            ],
            flops=2 * R * MID * out_width,
        )

    SHIFTS = ((0, 0), (0, 1), (1, 0), (1, 1))

    def back_two(self, ids, sc, dz2, c2, nrm2, sts, normp, msk, c1, nrm1, w, off, rows):
        R = self.R
        layout, arrays = w
        nst, nw = len(sts), len(arrays)

        def body(ids, sc, dz2, c2, nrm2, normp, msk, c1, nrm1, *rest):
            st_refs, refs = rest[:nst], rest[nst : nst + nw]
            dc, dz1, st, sums, ws, hs, patches, sem = rest[nst + nw :]
            self.load_start(layout, ids, refs, off, rows, ws, sem)
            self.group_sums(st_refs, 0, sc, self.area(1), sums)
            self.clear_halo(hs)
            st[...] = jnp.zeros(st.shape, F32)
            self.own_dc(dz2, c2, nrm2, sums, normp, "2", msk, dc, hs)
            for k, (fwd_r, fwd_c) in enumerate(self.SHIFTS):
                self.shifted(hs, patches, k * MID, fwd_r, fwd_c)
            self.load_wait(ws, sem)
            seen = set()
            for tap in range(9):
                phase, back_r, back_c = self.tap_two(tap)
                k = self.SHIFTS.index((back_r, back_c))
                part = dot_nt(patches[:, k * MID : (k + 1) * MID], ws[tap * MID : (tap + 1) * MID, :])
                if phase in seen:
                    dz1[phase * R : (phase + 1) * R, :] += part
                else:
                    dz1[phase * R : (phase + 1) * R, :] = part
                seen.add(phase)
            self.through(dz1, c1, nrm1, normp, "1", msk, st, 4)

        return call(
            body,
            [(ids, SM), (sc, SM), (dz2, VM), (c2, VM), (nrm2, VM), (normp, VM), (msk, VM), (c1, VM), (nrm1, VM)]
            + [(s, VM) for s in sts]
            + [(a, HB) for a in arrays],
            [((R, MID), BF, VM), ((4 * R, MID), F32, VM), ((8, MID), F32, VM)],
            [
                pltpu.VMEM((8, MID), F32),
                pltpu.VMEM((9 * MID, MID), BF),
                pltpu.VMEM((R + 2 * HALO, MID), F32),
                pltpu.VMEM((R, 4 * MID), BF),
                pltpu.SemaphoreType.DMA,
            ],
            flops=2 * 9 * R * MID * MID,
        )

    def back_one(self, sc, dz1, c1, nrm1, sts, normp, msk):
        R = self.R
        nst = len(sts)

        def body(sc, dz1, c1, nrm1, normp, msk, *rest):
            st_refs = rest[:nst]
            dc, sums = rest[nst:]
            self.group_sums(st_refs, 0, sc, self.area(2), sums)
            self.own_dc(dz1, c1, nrm1, sums, normp, "1", msk, dc, None, 4)

        return call(
            body,
            [(sc, SM), (dz1, VM), (c1, VM), (nrm1, VM), (normp, VM), (msk, VM)] + [(s, VM) for s in sts],
            [((4 * R, MID), BF, VM)],
            [pltpu.VMEM((8, MID), F32)],
        )[0]

    def input_grad(self, ids, dc1, dcs, w1, off1, rows1, ids_s, ws, offs, rowss, pictures):
        R = self.R
        g = self.g
        lay1, arr1 = w1
        lays, arrs = ws
        n1, ns = len(arr1), len(arrs)
        width = pictures[0].shape[3]
        out_width = dcs.shape[1]

        def body(ids, ids_s, dc1, dcs, *rest):
            r1, rs = rest[:n1], rest[n1 : n1 + ns]
            ga, gb, gc, k1, ka, kb, dx, sem = rest[n1 + ns :]
            g_refs = (ga, gb, gc)
            self.load_start(lay1, ids, r1, off1, rows1, k1, sem.at[0])
            self.load_start(lays, ids_s, rs, offs, rowss, ka, sem.at[1])
            self.load_start(lays, ids_s, rs, offs + rowss, rowss, kb, sem.at[2])
            self.load_wait(k1, sem.at[0])
            self.load_wait(ka, sem.at[1])
            self.load_wait(kb, sem.at[2])
            for phase in range(4):
                for q in range(width // MID):
                    lane = slice(q * MID, (q + 1) * MID)
                    part = dot_nt(dc1[phase * R : (phase + 1) * R, :], k1[lane, :])
                    if phase == 0:
                        part = part + dot_nn(dcs[...], (ka, kb)[q][...])
                    dx[phase * R : (phase + 1) * R, lane] = part
            for which, line, column, row in g.lines():
                for phase in range(4):
                    odd, second = divmod(phase, 2)
                    base = phase * R + row
                    g_refs[which][2 * line + odd, 2 * column + second] = dx[base : base + g.counts[which], :].astype(BF)

        return call(
            body,
            [(ids, SM), (ids_s, SM), (dc1, VM), (dcs, VM)] + [(a, HB) for a in arr1] + [(a, HB) for a in arrs],
            [(p.shape, BF, VM) for p in pictures],
            [
                pltpu.VMEM((width, MID), BF),
                pltpu.VMEM((out_width, MID), BF),
                pltpu.VMEM((out_width, MID), BF),
                pltpu.VMEM((4 * R, width), F32),
                pltpu.SemaphoreType.DMA((3,)),
            ],
            flops=2 * (4 * R * width * MID + R * width * out_width),
        )


    def gradient(self, ids, chains, kind, ins, parts, heights, held=None, extra=None):
        fresh = held is None
        arrays, start = ([], [0] * len(chains)) if fresh else held
        outs, spans = [], []
        for c, places_list in enumerate(chains):
            size = sum(split[c] for _, split in parts)
            for places in places_list:
                outs.append(((len(places), heights[c], MID), BF, HB))
                spans.append((start[c], size))
        count, pieces = len(ins), len(outs)

        def body(ids, *rest):
            refs, rest = rest[:count], rest[count + len(arrays) :]
            out_refs, rest = rest[:pieces], rest[pieces:]
            bufs, rest = rest[: len(parts)], rest[len(parts) :]
            sems, tail = rest[0], rest[1:]
            offs = list(start)
            for part, (buf, (rows, split)) in enumerate(zip(bufs, parts)):
                kind(part, refs, buf, tail)
                self.store_start(chains, ids, buf, rows, split, offs, out_refs, sems)
                offs = [o + t for o, t in zip(offs, split)]
            self.store_wait(out_refs, sems, spans)

        tall = [rows * self.blocks if self.blocks > 1 else rows for rows, _ in parts]
        scratch = [pltpu.VMEM((t, MID), BF) for t in tall]
        scratch.append(pltpu.SemaphoreType.DMA((pieces,)))
        scratch.extend(extra or [])
        made = call(
            body,
            [(ids, SM)] + [(a, VM) for a in ins] + [(a, HB) for a in arrays],
            outs,
            scratch,
            flops=2 * self.R * sum(tall) * MID,
            aliases={1 + count + i: i for i in range(len(arrays))},
        )
        ends = [at + sum(split[c] for _, split in parts) for c, at in enumerate(start)]
        return list(made), ends

    def grad_outer(self, ids, chains, pairs, parts, heights, held=None):
        ins = []
        for left, right in pairs:
            ins += [left, right]

        def kind(part, refs, buf, tail):
            left, right = refs[2 * part], refs[2 * part + 1]
            for q in range(left.shape[1] // MID):
                buf[q * MID : (q + 1) * MID, :] = dot_tn(left[:, q * MID : (q + 1) * MID], right[...]).astype(BF)

        return self.gradient(ids, chains, kind, ins, parts, heights, held)

    def grad_short(self, ids, chains, a2, dc3, dcs, xp, parts, heights, held=None):
        R = self.R

        def kind(part, refs, buf, tail):
            a2, dc3, dcs, xp = refs
            left = dc3 if part == 0 else dcs
            for q in range(left.shape[1] // MID):
                cols = left[:, q * MID : (q + 1) * MID]
                right = a2[...] if part == 0 else xp[0:R, (part - 1) * MID : part * MID]
                buf[q * MID : (q + 1) * MID, :] = dot_tn(cols, right).astype(BF)

        return self.gradient(ids, chains, kind, [a2, dc3, dcs, xp], parts, heights, held)

    def grad_taps(self, ids, chains, act, dc, parts, heights, stride, held=None):
        R = self.R

        def kind(part, refs, buf, tail):
            act, dc = refs
            hs, patches = tail
            self.clear_halo(hs)

            for row in range(0, R, 16):
                hs[HALO + row : HALO + row + 16, :] = dc[row : row + 16, :].astype(F32)
            if stride == 1:
                shifts = [(1 - tap // 3, 1 - tap % 3) for tap in range(9)]
            else:
                shifts = list(self.SHIFTS)
            for k, (sr, sc_) in enumerate(shifts):
                self.shifted(hs, patches, k * MID, sr, sc_)
            for tap in range(9):
                if stride == 1:
                    left, k = act[...], tap
                else:
                    phase, back_r, back_c = self.tap_two(tap)
                    left, k = act[phase * R : (phase + 1) * R, :], self.SHIFTS.index((back_r, back_c))
                buf[tap * MID : (tap + 1) * MID, :] = dot_tn(left, patches[:, k * MID : (k + 1) * MID]).astype(BF)

        wide_cols = 9 if stride == 1 else 4
        extra = [pltpu.VMEM((R + 2 * HALO, MID), F32), pltpu.VMEM((R, wide_cols * MID), BF)]
        return self.gradient(ids, chains, kind, [act, dc], parts, heights, held, extra)

    def grad_first(self, ids, chains, xp, dc1, sums, parts, heights):
        def kind(part, refs, buf, tail):
            if part == 0:
                xp, dc1 = refs[0], refs[1]
                for q in range(xp.shape[1] // MID):
                    buf[q * MID : (q + 1) * MID, :] = dot_tn(xp[:, q * MID : (q + 1) * MID], dc1[...]).astype(BF)
            else:
                row = 0
                for first in (3, 0):
                    for name in ("1", "2", "3", "S", "4", "5", "6"):
                        ref = refs[2 + ("1", "2", "3", "4", "5", "6").index("3" if name == "S" else name)]
                        at = first + (8 if name == "S" else 0)
                        total = ref[at : at + 1, :] + ref[at + 1 : at + 2, :] + ref[at + 2 : at + 3, :]
                        for q in range(ref.shape[1] // MID):
                            piece = total[:, q * MID : (q + 1) * MID]
                            buf[row * 16 : row * 16 + 16, :] = jnp.broadcast_to(piece, (16, MID)).astype(BF)
                            row += 1

        return self.gradient(ids, chains, kind, [xp, dc1] + list(sums), parts, heights)


def adam_step(weight, moment_one, moment_two, gradient, step_rate, decay_rate):
    first_new = 0.5 * moment_one + 0.5 * gradient
    second_new = 0.5 * moment_two + 0.5 * gradient * gradient
    correct = 1.0 - 0.5**STEP
    update = first_new / correct / (jnp.sqrt(second_new / correct) + 1e-08) + decay_rate * weight
    return (weight - step_rate * update, first_new, second_new)


BOTH = ("dp", "bn")


def orders(total):
    count = total.bit_length() - 1
    if count == 5:
        return [4, 2, 3, 1, 0], [4, 1, 3, 2, 0], [2, 1, 4, 3, 0]
    return (list(range(count))[::-1],) * 3


class Order:
    def __init__(self, free=False):
        self.last, self.free = None, free

    def hold(self, value):
        if self.last is None:
            return value
        return lax.optimization_barrier((value, self.last))[0]

    def mark(self, value):
        self.last = None if self.free else value


class Gather:
    def __init__(self, seq, swap, buf, order):
        self.seq, self.swap, self.bits = seq, swap, list(order)
        self.held, self.places = buf[None], [0]
        self.go()

    def go(self):
        bit = self.bits.pop(0)
        self.got = self.swap(self.held, bit)
        self.there = [r ^ (1 << bit) for r in self.places]

    def step(self):
        self.held = jnp.concatenate([self.held, self.seq.hold(self.got)])
        self.places = self.places + self.there
        self.seq.mark(self.held)
        self.go()

    def result(self):
        return [self.places, self.there], [self.held, self.got]


class Scatter:
    def __init__(self, seq, swap, pieces, order):
        self.seq, self.swap, self.bits = seq, swap, list(order)
        self.kept = [pieces[0]]
        self.got = swap(pieces[1], self.bits.pop(0))

    @staticmethod
    def places(order):
        kept = [0]
        for bit in reversed(order[1:]):
            kept = kept + [r ^ (1 << bit) for r in kept]
        return [kept, [r ^ (1 << order[0]) for r in kept]]

    def step(self):
        kept = self.kept + [self.seq.hold(self.got)]
        half = kept[0].shape[0] // 2
        sent = sum([k[half:].astype(F32) for k in kept[1:]], kept[0][half:].astype(F32)).astype(BF)
        self.kept = [k[:half] for k in kept]
        self.seq.mark(sent)
        self.got = self.swap(sent, self.bits.pop(0))

    def result(self):
        kept = self.kept + [self.seq.hold(self.got)]
        return sum([k[0].astype(F32) for k in kept[1:]], kept[0][0].astype(F32))


def gentle(total):
    if total == 32:
        return [1, 4, 3, 2, 0], [1, 2, 4, 3, 0]
    return orders(total)[:2]


def backward_orders(total):
    if total == 32:
        return [0, 2, 3, 4, 1], [0, 3, 2, 1, 4], [0, 1, 2, 3, 4], [0, 3, 1, 2, 4]
    return [orders(total)[0][::-1]] * 4


def on_device(*args):
    slots_inside = (1, 2, 0, 3)
    images = [jnp.transpose(args[k], slots_inside) for k in (0, 2, 1)]
    lives = (args[3], args[5], args[4])
    ups = [jnp.transpose(args[k], slots_inside) for k in (6, 8, 7)]
    params, firsts, seconds = args[9:17], args[17:25], args[25:33]
    groups, members = lax.axis_size("dp"), lax.axis_size("bn")
    total = groups * members
    pos_dp, pos_bn = lax.axis_index("dp"), lax.axis_index("bn")
    me = pos_dp * members + pos_bn
    grid = Grid([p.shape[2] for p in images], [u.shape[1] for u in ups])

    seq = Order()
    low = [params[0].astype(BF)]
    seq.mark(low[0])
    low += [seq.hold(p).astype(BF) for p in params[1:]]
    short_t = low[3].T
    shards = {
        "1": low[0],
        "2": low[1],
        "3": low[2].T,
        "S": jnp.concatenate([short_t[:, :MID], short_t[:, MID:]], axis=0),
        "4": low[4],
        "5": low[5],
        "6": low[6].T,
    }
    unit = {"1": 1, "2": 1, "3": 1, "S": 2, "4": 1, "5": 1, "6": 1}
    rows = {k: v.shape[0] // unit[k] for k, v in shards.items()}
    direct = all(r % 16 == 0 for r in rows.values()) and params[7].shape[0] == MID
    blocks = total if direct else 1
    if not direct:
        rows = {k: r * total for k, r in rows.items()}
    dev = Device(grid, blocks, members)

    spot = jnp.stack([pos_dp, pos_bn]).astype(jnp.int32)
    far = jnp.zeros((1,), jnp.int32)
    near = me.reshape(1).astype(jnp.int32) if direct else far

    def offsets(names):
        where, at = {}, 0
        for k in names:
            where[k] = at
            at += rows[k] * unit[k]
        return where, at

    def packed(names, with_norm=False):
        parts = [shards[k] for k in names]
        if with_norm:
            parts.append(jnp.broadcast_to(low[7].reshape(1, MID), (16, MID)))
        return jnp.concatenate(parts, axis=0) if len(parts) > 1 else parts[0]

    def gather(names):
        buf = packed(names)
        full = lax.all_gather(buf, BOTH, axis=0, tiled=True).reshape(total, buf.shape[0], MID)
        if direct:
            return ([(0, list(range(total)))], [full]), offsets(names)[0]
        pieces, spot_row = [], 0
        for k in names:
            for _ in range(unit[k]):
                r = rows[k] // total
                pieces.append(full[:, spot_row : spot_row + r, :].reshape(rows[k], MID))
                spot_row += r
        return ([(0, [0])], [jnp.concatenate(pieces, axis=0)[None]]), offsets(names)[0]

    def swap(array, bit):
        return lax.ppermute(array, BOTH, [(i, i ^ (1 << bit)) for i in range(total)])

    def exchange(stat):
        return [stat] + [
            lax.ppermute(stat, "bn", [(i, i ^ k) for i in range(members)]) for k in range(1, members)
        ]

    first, second, third = orders(total)

    def chains(buf, cuts, seq):
        made, at = [], 0
        for height, order in cuts:
            made.append((at, Gather(seq, swap, buf[at : at + height], order)))
            at += height
        return made

    def steps(made):
        for _, chain in made:
            chain.step()

    def results(made):
        layout, arrays = [], []
        for at, chain in made:
            for places, array in zip(*chain.result()):
                layout.append((at, places))
                arrays.append(array)
        return layout, arrays

    if direct:
        r2 = rows["2"] // 48 * 16
        quiet_x, _ = gentle(total)
        free = Order(True)
        g_one = chains(packed(["1"]), [(rows["1"], first)], free)
        buf2, buf5 = packed(["2"], True), packed(["5"])
        wb, at_b = gather(["3", "S", "4", "6"])
        steps(g_one)
        later = lax.optimization_barrier((buf2, g_one[0][1].held))[0]
        g_two = chains(later, [(r2, first), (r2, second), (rows["2"] - 2 * r2 + 16, third)], free)
        for _ in range(3):
            steps(g_one)
        for _ in range(4):
            steps(g_two)
        xp, msk, sc = dev.prepare(spot, lives, images)
        c1, st1 = dev.conv_one(near, sc, xp, msk, results(g_one), 0, rows["1"])
        seq.mark(st1)
        st1 = exchange(st1)
        g_five = chains(seq.hold(buf5), [(rows["5"], quiet_x)], seq)
        a1, nrm1, c2, st2, normp = dev.conv_two(
            near, sc, c1, st1, None, seq.hold(msk), results(g_two), 0, rows["2"], rows["2"]
        )
        seq.mark(st2)
        st2 = exchange(st2)
        steps(g_five)
        steps(g_five)
        cs, sts = dev.conv_short(far, sc, xp, seq.hold(msk), wb, at_b["S"], rows["S"])
        seq.mark(sts)
        steps(g_five)
        a2, nrm2, c3, st3 = dev.conv_expand(
            far, sc, c2, st2, normp, seq.hold(msk), wb, at_b["3"], rows["3"], "2", sts
        )
        seq.mark(st3)
        st3 = exchange(st3)
        w1, w2 = results(g_one), results(g_two)
        w3 = w4 = w6 = wb
        at_3 = at_b
    else:
        w1, w2, w4, w5, w6 = [gather([k])[0] for k in ("1", "2", "4", "5", "6")]
        w3, at_3 = gather(["3", "S"])
        xp, msk, sc = dev.prepare(spot, lives, images)
        c1, st1 = dev.conv_one(near, sc, xp, msk, w1, 0, rows["1"])
        normp = lax.all_gather(low[7], BOTH, axis=0, tiled=True).astype(F32).reshape(32, MID)
        a1, nrm1, c2, st2 = dev.conv_two(near, sc, c1, exchange(st1), normp, msk, w2, 0, rows["2"])
        cs, sts = dev.conv_short(far, sc, xp, msk, w3, at_3["S"], rows["S"])
        a2, nrm2, c3, st3 = dev.conv_expand(
            far, sc, c2, exchange(st2), normp, msk, w3, at_3["3"], rows["3"], "2", sts
        )
        st3 = exchange(st3)
        at_b = {"4": 0, "6": 0}
    h, hb, nrm3, nrms, c4, st4 = dev.conv_four(
        far, sc, c3, cs, st3, normp, msk, w4, at_b["4"], rows["4"]
    )
    if direct:
        seq.mark(st4)
        steps(g_five)
        w5 = results(g_five)
    a4, nrm4, c5, st5 = dev.conv_five(near, sc, c4, exchange(st4), normp, msk, w5, 0, rows["5"])
    a5, nrm5, c6, st6 = dev.conv_expand(far, sc, c5, exchange(st5), normp, msk, w6, at_b["6"], rows["6"], "5")
    oc, oa, ob, dz6, nrm6, su6 = dev.finish(sc, c6, h, exchange(st6), normp, msk, ups)

    def scatter(piece, heights):
        if not direct:
            parts, spot_row = [], 0
            for height in heights:
                parts.append(piece[0, spot_row : spot_row + height].reshape(total, height // total, MID))
                spot_row += height
            piece = jnp.concatenate(parts, axis=1)
        owned = lax.psum_scatter(piece.reshape(-1, MID), BOTH, scatter_dimension=0, tiled=True)
        return owned.astype(F32)

    def cut(owned, heights):
        parts, spot_row = [], 0
        for height in heights:
            height = height if direct else height // total
            parts.append(owned[spot_row : spot_row + height])
            spot_row += height
        return parts

    whole = [[list(range(total)) if direct else [0]]]
    order_a, order_b, order_two, order_one = backward_orders(total)

    def halves(k):
        if not direct:
            return [rows[k]]
        one = rows[k] // 32 * 16
        return [rows[k] - one, one]

    pair = [order_a, order_b] if direct else [None]
    pair_places = [Scatter.places(order) for order in pair] if direct else whole
    two_places = [Scatter.places(order_two)] if direct else whole
    single_places = [Scatter.places(order_one)] if direct else whole

    def sums(made, orders_used):
        if not direct:
            return []
        return [Scatter(seq, swap, made[0][2 * c : 2 * c + 2], order) for c, order in enumerate(orders_used)]

    def advance(made):
        for chain in made:
            chain.step()

    dc6, dz5, su5 = dev.back_six(
        far, sc, dz6, c6, nrm6, exchange(su6), normp, msk, c5, nrm5, w6, at_b["6"], rows["6"]
    )
    seq.mark(su5)
    high = [rows["6"] + rows["5"]]
    g65 = dev.grad_outer(seq.hold(far), whole, [(dc6, a5)], [(rows["6"], [rows["6"]])], high)
    seq.mark(g65[0][0])
    dc5, dz4, su4 = dev.back_five(
        near, sc, dz5, c5, nrm5, exchange(su5), normp, seq.hold(msk), c4, nrm4, w5, 0, rows["5"]
    )
    seq.mark(su4)
    g65 = dev.grad_taps(seq.hold(far), whole, a4, dc5, [(rows["5"], [rows["5"]])], high, 1, g65)
    seq.mark(g65[0][0])
    hts65 = [rows["6"], rows["5"]]
    owned65 = scatter(g65[0][0], hts65)

    dc4, dz3, su3 = dev.back_four(
        far, sc, dz4, c4, nrm4, exchange(su4), normp, seq.hold(msk), dz6, c3, nrm3, cs, nrms, w4, at_b["4"], rows["4"]
    )
    seq.mark(su3)
    part4, part3 = (rows["4"], halves("4")), (rows["3"], halves("3"))
    mid = [a + 3 * b for a, b in zip(part4[1], part3[1])]
    g43 = dev.grad_outer(seq.hold(near), pair_places, [(hb, dc4)], [part4], mid)
    seq.mark(g43[0][0])
    dc3, dcs, dz2, su2 = dev.back_three(
        far, sc, dz3, c3, nrm3, cs, nrms, exchange(su3), normp, seq.hold(msk), c2, nrm2, w3, at_3["3"], rows["3"]
    )
    seq.mark(su2)
    g43 = dev.grad_short(seq.hold(near), pair_places, a2, dc3, dcs, xp, [part3] * 3, mid, g43)
    seq.mark(g43[0][0])
    s43 = sums(g43, pair)
    dc2, dz1, su1 = dev.back_two(
        near, sc, dz2, c2, nrm2, exchange(su2), normp, seq.hold(msk), c1, nrm1, w2, 0, rows["2"]
    )
    seq.mark(su1)
    advance(s43)
    g2 = dev.grad_taps(seq.hold(near), two_places, a1, dc2, [(rows["2"], [rows["2"]])], [rows["2"]], 2)
    seq.mark(g2[0][0])
    s2 = sums(g2, [order_two])
    dc1 = dev.back_one(sc, dz1, c1, nrm1, exchange(su1), normp, seq.hold(msk))
    seq.mark(dc1)
    advance(s2)
    advance(s43)
    parts = [(rows["1"], [rows["1"]])] + ([(16, [16])] if direct else [])
    g1 = dev.grad_first(
        seq.hold(near), single_places, xp, dc1, (su1, su2, su3, su4, su5, su6), parts, [sum(p for p, _ in parts)]
    )
    seq.mark(g1[0][0])
    s1 = sums(g1, [order_one])
    grads = dev.input_grad(seq.hold(near), dc1, dcs, w1, 0, rows["1"], far, w3, at_3["S"], rows["S"], images)
    seq.mark(grads[0])
    gc_, ga_, gb_ = grads
    if direct:
        advance(s1)
        advance(s43)
        advance(s2)
        advance(s1)
        advance(s43)
        advance(s2)
        advance(s1)
        advance(s2)
        advance(s1)
        got43 = [chain.result() for chain in s43]
        got2 = [chain.result() for chain in s2]
        last = s1[0].result()
    else:
        got43 = [scatter(g43[0][0], [rows["4"]] + [rows["3"]] * 3)]
        got2 = [scatter(g2[0][0], [rows["2"]])]
        last = scatter(g1[0][0], [rows["1"]])
    cuts = [cut(owned, [part4[1][c]] + [part3[1][c]] * 3) for c, owned in enumerate(got43)]
    o4, o3, osa, osb = [jnp.concatenate(p, axis=0) if len(p) > 1 else p[0] for p in zip(*cuts)]
    o2 = jnp.concatenate(got2, axis=0) if len(got2) > 1 else got2[0]
    o6, o5 = cut(owned65, hts65)
    o1 = last[: rows["1"]] if direct else last
    if direct:
        onorm = last[rows["1"]]
    else:

        def three(stat, at):
            return jnp.sum(stat[at : at + 3], axis=0)

        vec = [three(su1, 3), three(su2, 3), three(su3, 3), three(su3, 11), three(su4, 3), three(su5, 3), three(su6, 3)]
        vec += [three(su1, 0), three(su2, 0), three(su3, 0), three(su3, 8), three(su4, 0), three(su5, 0), three(su6, 0)]
        onorm = lax.psum_scatter(jnp.concatenate(vec), BOTH, scatter_dimension=0, tiled=True)
    owned = (o1, o2, o3.T, jnp.concatenate([osa, osb], axis=1).T, o4, o5, o6.T, onorm)
    stepped = []
    for k in range(8):
        rate, decay = (RATE_CONV, DECAY_CONV) if k < 7 else (RATE_NORM, 0.0)
        stepped.extend(adam_step(params[k], firsts[k], seconds[k], owned[k], rate, decay))
    images_out = [jnp.transpose(a, (2, 0, 1, 3)) for a in (oc, oa, ob, gc_, ga_, gb_)]
    order_out = [images_out[k] for k in (0, 2, 1, 3, 5, 4)]
    return (*order_out, *stepped)


def solution(mesh):
    batch = P(BOTH, None, None, None)
    by_row, by_col, flat = P(BOTH, None), P(None, BOTH), P(BOTH)
    weights = (by_row, by_row, by_col, by_col, by_row, by_row, by_col, flat)
    triple = tuple(spec for spec in weights for _ in range(3))
    return jax.shard_map(
        on_device,
        mesh=mesh,
        in_specs=(batch,) * 3 + (P(),) * 3 + (batch,) * 3 + weights * 3,
        out_specs=(batch,) * 6 + triple,
        check_vma=False,
    )
```

```python
import jax
import jax.numpy as jnp
import numpy as np
from jax import lax
from jax.experimental import pallas as pl
from jax.experimental.pallas import tpu as pltpu
from jax.sharding import PartitionSpec as P

STEP = 10
EPSILON = 1e-05
RATE_CONV = 0.03
RATE_NORM = 0.4
DECAY_CONV = 0.05
BF = jnp.bfloat16
F32 = jnp.float32
MID = 512
HALO = 32
UNROLL = 4
NORM_ROW = {"1": 0, "2": 1, "3": 2, "S": 6, "4": 10, "5": 11, "6": 12}


class Grid:
    def __init__(self, counts, sides):
        self.counts, self.sides = counts, sides
        self.seg, self.size = [], []
        at = 0
        for number, side in zip(counts, sides):
            rows = -(-number * (side + 1) ** 2 // 16) * 16
            self.seg.append(at)
            self.size.append(rows)
            at += rows
        self.rows = at

    def lines(self):
        for which, (number, side) in enumerate(zip(self.counts, self.sides)):
            for line in range(side):
                for column in range(side):
                    yield which, line, column, self.seg[which] + (line * (side + 1) + column) * number


def silu(v):
    return v * jax.nn.sigmoid(v)


def slope(v):
    s = jax.nn.sigmoid(v)
    return s * (1.0 + v * (1.0 - s))


def dot_nn(a, b):
    return lax.dot_general(a, b, (((1,), (0,)), ((), ())), preferred_element_type=F32)


def dot_nt(a, b):
    return lax.dot_general(a, b, (((1,), (1,)), ((), ())), preferred_element_type=F32)


def dot_tn(a, b):
    return lax.dot_general(a, b, (((0,), (0,)), ((), ())), preferred_element_type=F32)


def aligned(row):
    return row if isinstance(row, int) else pl.multiple_of(row, 16)


def wide(mask):
    return jnp.concatenate([mask] * (MID // 128), axis=1)


VM = pl.BlockSpec(memory_space=pltpu.VMEM)
SM = pl.BlockSpec(memory_space=pltpu.SMEM)
HB = pl.BlockSpec(memory_space=pl.ANY)


def call(body, ins, outs, scratch=(), flops=0, moved=0, aliases=None):
    return pl.pallas_call(
        body,
        out_shape=[jax.ShapeDtypeStruct(shape, dtype) for shape, dtype, _ in outs],
        in_specs=[spec for _, spec in ins],
        out_specs=[spec for _, _, spec in outs],
        scratch_shapes=list(scratch),
        input_output_aliases=aliases or {},
        compiler_params=pltpu.CompilerParams(vmem_limit_bytes=58 * 1024 * 1024),
        cost_estimate=pl.CostEstimate(flops=flops, bytes_accessed=moved, transcendentals=0),
    )(*[array for array, _ in ins])


class Device:
    def __init__(self, grid, blocks, members):
        self.g = grid
        self.blocks = blocks
        self.members = members
        self.R = grid.rows


    def sweep(self, cols, make, st=None, sums=()):
        for which in range(3):
            start, count = self.g.seg[which], self.g.size[which] // 16
            for q in range(cols // MID):
                lane = slice(q * MID, (q + 1) * MID)
                work = make(which, q, lane)

                def add(acc, row, work=work):
                    terms = work(aligned(row)) or ()
                    return tuple(a + t[:8] + t[8:] for a, t in zip(acc, terms))

                def trip(i, acc, start=start, add=add):
                    for j in range(UNROLL):
                        acc = add(acc, start + (i * UNROLL + j) * 16)
                    return acc

                acc = tuple(jnp.zeros((8, MID), F32) for _ in sums)
                trips = count // UNROLL
                acc = lax.fori_loop(0, trips, trip, acc)
                for j in range(trips * UNROLL, count):
                    acc = add(acc, start + j * 16)
                for row, a in zip(sums, acc):
                    st[row + which : row + which + 1, lane] = jnp.sum(a, axis=0, keepdims=True)

    def normal(self, c, nrm, which, lane=slice(0, MID)):
        mean, rstd = nrm[which : which + 1, lane], nrm[3 + which : 4 + which, lane]
        return lambda row: (c[pl.ds(row, 16), lane] - mean) * rstd

    def scaled(self, normp, name, q):
        at = NORM_ROW[name] + q
        gain, bias = normp[at : at + 1, :], normp[16 + at : 17 + at, :]
        return lambda xh: gain * xh + bias

    def backed(self, normp, name, q, nrm, sums, which, lane=slice(0, MID)):
        at = NORM_ROW[name] + q
        a, b = sums[which : which + 1, lane], sums[3 + which : 4 + which, lane]
        scale = normp[at : at + 1, :] * nrm[3 + which : 4 + which, lane]
        return lambda dz, xh, m: scale * (dz - m * (a + xh * b))

    def load_start(self, layout, ids, refs, off, rows, dst, sem):
        for ref, (base, places) in zip(refs, layout):
            low, high = max(base, off), min(base + ref.shape[1], off + rows)
            if high <= low:
                continue
            for pos, rel in enumerate(places):
                block = rel ^ ids[0]
                pltpu.make_async_copy(
                    ref.at[pos, pl.ds(low - base, high - low), :],
                    dst.at[pl.ds(pl.multiple_of(block * rows + (low - off), 16), high - low), :],
                    sem,
                ).start()

    def load_wait(self, dst, sem):
        pltpu.make_async_copy(dst, dst, sem).wait()

    def store_start(self, chains, ids, src, rows, split, offs, refs, sems):
        at, lo = 0, 0
        for places_list, take, off in zip(chains, split, offs):
            for places in places_list:
                for pos, rel in enumerate(places):
                    block = rel ^ ids[0]
                    pltpu.make_async_copy(
                        src.at[pl.ds(pl.multiple_of(block * rows + lo, 16), take), :],
                        refs[at].at[pos, pl.ds(off, take), :],
                        sems.at[at],
                    ).start()
                at += 1
            lo += take

    def store_wait(self, refs, sems, spans):
        for which, (ref, (off, size)) in enumerate(zip(refs, spans)):
            view = ref.at[:, pl.ds(off, size), :]
            pltpu.make_async_copy(view, view, sems.at[which]).wait()

    def local_stats(self, c_ref, m_ref, sc, out_ref, at, area, phases=1):
        cols = c_ref.shape[1]
        out_ref[pl.ds(at, 8), :] = jnp.zeros((8, cols), F32)
        def make(which, q, lane):
            start = self.g.seg[which]
            base = c_ref[start : start + 1, lane]

            def work(row):
                m = wide(m_ref[pl.ds(row, 16), :])
                total = square = None
                for phase in range(phases):
                    d = c_ref[pl.ds(aligned(row + phase * self.R), 16), lane] - base
                    v = d * m
                    total = v if total is None else total + v
                    square = v * d if square is None else square + v * d
                return total, square

            return work

        self.sweep(cols, make, out_ref, (at, at + 3))
        for which in range(3):
            held = sc[0, which] * float(area[which])
            base = c_ref[self.g.seg[which] : self.g.seg[which] + 1, :]
            total = out_ref[at + which : at + which + 1, :]
            out_ref[at + which : at + which + 1, :] = total + held * base
            square = out_ref[at + 3 + which : at + 4 + which, :]
            out_ref[at + 3 + which : at + 4 + which, :] = square - total * (total / held)

    def group_norm(self, st_refs, at, sc, area, out_ref):
        cols = out_ref.shape[1]
        out_ref[...] = jnp.zeros(out_ref.shape, F32)
        for which in range(3):
            count = sc[self.members, which] * float(area[which])
            sums = [ref[at + which : at + which + 1, :] for ref in st_refs]
            mean = sum(sums[1:], sums[0]) / count
            spread = jnp.zeros((1, cols), F32)
            for k, ref in enumerate(st_refs):
                held = sc[k, which] * float(area[which])
                apart = sums[k] / held - mean
                spread = spread + (ref[at + 3 + which : at + 4 + which, :] + held * apart * apart)
            out_ref[which : which + 1, :] = mean
            out_ref[3 + which : 4 + which, :] = lax.rsqrt(spread / count + EPSILON)

    def group_sums(self, st_refs, at, sc, area, out_ref):
        out_ref[...] = jnp.zeros(out_ref.shape, F32)
        for which in range(3):
            count = sc[self.members, which] * float(area[which])
            for row in (which, 3 + which):
                rows = [ref[at + row : at + row + 1, :] for ref in st_refs]
                out_ref[row : row + 1, :] = sum(rows[1:], rows[0]) / count

    def shifted(self, hs_ref, dst_ref, col, sign_r, sign_c):
        for which in range(3):
            off = (sign_r * (self.g.sides[which] + 1) + sign_c) * self.g.counts[which]
            for i in range(self.g.size[which] // 16):
                row = self.g.seg[which] + i * 16
                dst_ref[row : row + 16, col : col + MID] = hs_ref[HALO + row + off : HALO + row + off + 16, :].astype(BF)

    def clear_halo(self, hs_ref):
        hs_ref[0:HALO, :] = jnp.zeros((HALO, MID), F32)
        hs_ref[HALO + self.R : 2 * HALO + self.R, :] = jnp.zeros((HALO, MID), F32)

    def area(self, side_scale):
        return [(side_scale * side) ** 2 for side in self.g.sides]


    def prepare(self, spot, lives, pictures):
        R = self.R
        g = self.g
        width = pictures[0].shape[3]
        members = self.members

        def body(spot, la, lb, lc, xa, xb, xc, xp, msk, sc, big):
            x_refs, l_refs = (xa, xb, xc), (la, lb, lc)
            own = []
            for which in range(3):
                per = g.counts[which]
                whole = jnp.zeros((), jnp.int32)
                for k in range(members):
                    first = (spot[0] * members + (spot[1] ^ k)) * per
                    flags = [l_refs[which][first + i] for i in range(per)]
                    held = sum(flags[1:], flags[0])
                    sc[k, which] = held.astype(F32)
                    whole = whole + held
                    if k == 0:
                        own.append(flags)
                sc[members, which] = whole.astype(F32)
            big[...] = jnp.zeros(big.shape, F32)
            msk[...] = jnp.zeros(msk.shape, F32)
            alive = []
            for which in range(3):
                per = g.counts[which]
                slot = lax.broadcasted_iota(jnp.int32, (per, 128), 0)
                mask = jnp.zeros((per, 128), F32)
                for i in range(per):
                    mask = jnp.where(slot == i, own[which][i].astype(F32), mask)
                alive.append(mask)
            for which, line, column, row in g.lines():
                per = g.counts[which]
                msk[row : row + per, :] = alive[which]
                for phase in range(4):
                    odd, second = divmod(phase, 2)
                    base = phase * R + row
                    big[base : base + per, :] = x_refs[which][2 * line + odd, 2 * column + second].astype(F32)

            def cast(i, _):
                row = aligned(i * 16)
                xp[pl.ds(row, 16), :] = big[pl.ds(row, 16), :].astype(BF)
                return 0

            lax.fori_loop(0, 4 * R // 16, cast, 0)

        return call(
            body,
            [(spot, SM)] + [(l, SM) for l in lives] + [(p, VM) for p in pictures],
            [((4 * R, width), BF, VM), ((R, 128), F32, VM), ((members + 1, 3), F32, SM)],
            [pltpu.VMEM((4 * R, width), F32)],
        )

    def conv_one(self, ids, sc, xp, msk, w, off, rows):
        R = self.R
        width = xp.shape[1]
        layout, arrays = w

        def body(ids, sc, xp, msk, *rest):
            refs = rest[: len(arrays)]
            c, st, ws, sem = rest[len(arrays) :]
            self.load_start(layout, ids, refs, off, rows, ws, sem)
            self.load_wait(ws, sem)
            for phase in range(4):
                c[phase * R : (phase + 1) * R, :] = dot_nn(xp[phase * R : (phase + 1) * R, :], ws[...])
            self.local_stats(c, msk, sc, st, 0, self.area(2), 4)

        return call(
            body,
            [(ids, SM), (sc, SM), (xp, VM), (msk, VM)] + [(a, HB) for a in arrays],
            [((4 * R, MID), F32, VM), ((8, MID), F32, VM)],
            [pltpu.VMEM((width, MID), BF), pltpu.SemaphoreType.DMA],
            flops=2 * 4 * R * width * MID,
        )

    @staticmethod
    def tap_two(tap):
        i, j = divmod(tap, 3)
        return (0 if i == 1 else 2) + (0 if j == 1 else 1), (1 if i == 0 else 0), (1 if j == 0 else 0)

    def conv_two(self, ids, sc, c1, sts, normp, msk, w, off, rows, norm_off=None):
        R = self.R
        layout, arrays = w
        nst, nw = len(sts), len(arrays)
        with_norm = norm_off is not None

        def body(ids, sc, c1, msk, *rest):
            st_refs, refs, rest = rest[:nst], rest[nst : nst + nw], rest[nst + nw :]
            if with_norm:
                a1, nrm, c2, st, normp, ws, hs, patches, sem, ns, sem2 = rest
                self.load_start(layout, ids, refs, norm_off, 16, ns, sem2)
            else:
                normp, a1, nrm, c2, st, ws, hs, patches, sem = rest
            self.load_start(layout, ids, refs, off, rows, ws, sem)
            self.group_norm(st_refs, 0, sc, self.area(2), nrm)
            self.clear_halo(hs)
            if with_norm:
                self.load_wait(ns, sem2)
                for b in range(self.blocks):
                    normp[b : b + 1, :] = ns[b * 16 : b * 16 + 16, :].astype(F32)[0:1, :]
            for phase in range(4):

                def make(which, q, lane, phase=phase):
                    xh, put = self.normal(c1, nrm, which), self.scaled(normp, "1", 0)

                    def work(row):
                        at = aligned(row + phase * R)
                        v = silu(put(xh(at))) * wide(msk[pl.ds(row, 16), :])
                        hs[pl.ds(aligned(row + HALO), 16), :] = v
                        a1[pl.ds(at, 16), :] = v.astype(BF)

                    return work

                self.sweep(MID, make)
                for tap in range(9):
                    source, back_r, back_c = self.tap_two(tap)
                    if source == phase:
                        self.shifted(hs, patches, tap * MID, -back_r, -back_c)
            self.load_wait(ws, sem)
            c2[...] = dot_nn(patches[...], ws[...])
            self.local_stats(c2, msk, sc, st, 0, self.area(1))

        ins = [(ids, SM), (sc, SM), (c1, VM), (msk, VM)] + [(s, VM) for s in sts] + [(a, HB) for a in arrays]
        outs = [((4 * R, MID), BF, VM), ((8, MID), F32, VM), ((R, MID), F32, VM), ((8, MID), F32, VM)]
        scratch = [
            pltpu.VMEM((9 * MID, MID), BF),
            pltpu.VMEM((R + 2 * HALO, MID), F32),
            pltpu.VMEM((R, 9 * MID), BF),
            pltpu.SemaphoreType.DMA,
        ]
        if with_norm:
            outs.append(((self.blocks, MID), F32, VM))
            scratch += [pltpu.VMEM((self.blocks * 16, MID), BF), pltpu.SemaphoreType.DMA]
        else:
            ins.append((normp, VM))
        return call(body, ins, outs, scratch, flops=2 * 9 * R * MID * MID)

    def conv_short(self, ids, sc, xp, msk, w, off, rows):
        R = self.R
        layout, arrays = w
        nw = len(arrays)
        out_width = self.blocks * rows if self.blocks > 1 else rows

        def body(ids, sc, xp, msk, *rest):
            refs = rest[:nw]
            c, st, wa, wb, sem = rest[nw:]
            self.load_start(layout, ids, refs, off, rows, wa, sem.at[0])
            self.load_start(layout, ids, refs, off + rows, rows, wb, sem.at[1])
            self.load_wait(wa, sem.at[0])
            self.load_wait(wb, sem.at[1])
            for q in range(out_width // MID):
                lane = slice(q * MID, (q + 1) * MID)
                c[:, lane] = dot_nt(xp[0:R, 0:MID], wa[lane, :]) + dot_nt(xp[0:R, MID : 2 * MID], wb[lane, :])
            self.local_stats(c, msk, sc, st, 0, self.area(1))

        return call(
            body,
            [(ids, SM), (sc, SM), (xp, VM), (msk, VM)] + [(a, HB) for a in arrays],
            [((R, out_width), F32, VM), ((8, out_width), F32, VM)],
            [pltpu.VMEM((out_width, MID), BF), pltpu.VMEM((out_width, MID), BF), pltpu.SemaphoreType.DMA((2,))],
            flops=2 * R * 2 * MID * out_width,
        )

    def conv_expand(self, ids, sc, c, sts, normp, msk, w, off, rows, name, more=None):
        R = self.R
        layout, arrays = w
        nst, nw = len(sts), len(arrays)
        out_width = self.blocks * rows if self.blocks > 1 else rows
        stat_rows = 8 if more is None else 16

        def body(ids, sc, c, normp, msk, *rest):
            st_refs, refs = rest[:nst], rest[nst : nst + nw]
            rest = rest[nst + nw :]
            if more is not None:
                more_ref, rest = rest[0], rest[1:]
            act, nrm, prod, st, ws, sem = rest
            self.load_start(layout, ids, refs, off, rows, ws, sem)
            self.group_norm(st_refs, 0, sc, self.area(1), nrm)

            def make(which, q, lane):
                xh, put = self.normal(c, nrm, which), self.scaled(normp, name, 0)

                def work(row):
                    v = silu(put(xh(row))) * wide(msk[pl.ds(row, 16), :])
                    act[pl.ds(row, 16), :] = v.astype(BF)

                return work

            self.sweep(MID, make)
            self.load_wait(ws, sem)
            for q in range(out_width // MID):
                lane = slice(q * MID, (q + 1) * MID)
                prod[:, lane] = dot_nt(act[...], ws[lane, :])
            self.local_stats(prod, msk, sc, st, 0, self.area(1))
            if more is not None:
                st[8:16, :] = more_ref[...]

        ins = [(ids, SM), (sc, SM), (c, VM), (normp, VM), (msk, VM)] + [(s, VM) for s in sts] + [(a, HB) for a in arrays]
        if more is not None:
            ins.append((more, VM))
        return call(
            body,
            ins,
            [((R, MID), BF, VM), ((8, MID), F32, VM), ((R, out_width), F32, VM), ((stat_rows, out_width), F32, VM)],
            [pltpu.VMEM((out_width, MID), BF), pltpu.SemaphoreType.DMA],
            flops=2 * R * MID * out_width,
        )

    def conv_four(self, ids, sc, c3, cs, sts, normp, msk, w, off, rows):
        R = self.R
        layout, arrays = w
        nst, nw = len(sts), len(arrays)
        out_width = c3.shape[1]

        def body(ids, sc, c3, cs, normp, msk, *rest):
            st_refs, refs = rest[:nst], rest[nst : nst + nw]
            h_far, hb_far, nrm3, nrms, c4, st, ws, h, hb, sem, sems = rest[nst + nw :]
            self.load_start(layout, ids, refs, off, rows, ws, sem)
            self.group_norm(st_refs, 0, sc, self.area(1), nrm3)
            self.group_norm(st_refs, 8, sc, self.area(1), nrms)

            def make(which, q, lane):
                xh3, put3 = self.normal(c3, nrm3, which, lane), self.scaled(normp, "3", q)
                xhs, puts = self.normal(cs, nrms, which, lane), self.scaled(normp, "S", q)

                def work(row):
                    v = silu(put3(xh3(row)) + puts(xhs(row))) * wide(msk[pl.ds(row, 16), :])
                    h[pl.ds(row, 16), lane] = v
                    hb[pl.ds(row, 16), lane] = v.astype(BF)

                return work

            self.sweep(out_width, make)
            out = [pltpu.make_async_copy(h, h_far, sems.at[0]), pltpu.make_async_copy(hb, hb_far, sems.at[1])]
            for copy in out:
                copy.start()
            self.load_wait(ws, sem)
            c4[...] = dot_nn(hb[...], ws[...])
            self.local_stats(c4, msk, sc, st, 0, self.area(1))
            for copy in out:
                copy.wait()

        return call(
            body,
            [(ids, SM), (sc, SM), (c3, VM), (cs, VM), (normp, VM), (msk, VM)]
            + [(s, VM) for s in sts]
            + [(a, HB) for a in arrays],
            [
                ((R, out_width), F32, HB),
                ((R, out_width), BF, HB),
                ((8, out_width), F32, VM),
                ((8, out_width), F32, VM),
                ((R, MID), F32, VM),
                ((8, MID), F32, VM),
            ],
            [
                pltpu.VMEM((out_width, MID), BF),
                pltpu.VMEM((R, out_width), F32),
                pltpu.VMEM((R, out_width), BF),
                pltpu.SemaphoreType.DMA,
                pltpu.SemaphoreType.DMA((2,)),
            ],
            flops=2 * R * MID * out_width,
        )

    def conv_five(self, ids, sc, c4, sts, normp, msk, w, off, rows):
        R = self.R
        layout, arrays = w
        nst, nw = len(sts), len(arrays)

        def body(ids, sc, c4, normp, msk, *rest):
            st_refs, refs = rest[:nst], rest[nst : nst + nw]
            a4, nrm, c5, st, ws, hs, patches, sem = rest[nst + nw :]
            self.load_start(layout, ids, refs, off, rows, ws, sem)
            self.group_norm(st_refs, 0, sc, self.area(1), nrm)
            self.clear_halo(hs)

            def make(which, q, lane):
                xh, put = self.normal(c4, nrm, which), self.scaled(normp, "4", 0)

                def work(row):
                    v = silu(put(xh(row))) * wide(msk[pl.ds(row, 16), :])
                    hs[pl.ds(aligned(row + HALO), 16), :] = v
                    a4[pl.ds(row, 16), :] = v.astype(BF)

                return work

            self.sweep(MID, make)
            for tap in range(9):
                i, j = divmod(tap, 3)
                self.shifted(hs, patches, tap * MID, i - 1, j - 1)
            self.load_wait(ws, sem)
            c5[...] = dot_nn(patches[...], ws[...])
            self.local_stats(c5, msk, sc, st, 0, self.area(1))

        return call(
            body,
            [(ids, SM), (sc, SM), (c4, VM), (normp, VM), (msk, VM)] + [(s, VM) for s in sts] + [(a, HB) for a in arrays],
            [((R, MID), BF, VM), ((8, MID), F32, VM), ((R, MID), F32, VM), ((8, MID), F32, VM)],
            [
                pltpu.VMEM((9 * MID, MID), BF),
                pltpu.VMEM((R + 2 * HALO, MID), F32),
                pltpu.VMEM((R, 9 * MID), BF),
                pltpu.SemaphoreType.DMA,
            ],
            flops=2 * 9 * R * MID * MID,
        )

    def finish(self, sc, c6, h, sts, normp, msk, ups):
        R = self.R
        g = self.g
        nst = len(sts)
        out_width = c6.shape[1]

        def body(sc, c6, h, normp, msk, ua, ub, uc, *rest):
            st_refs = rest[:nst]
            oa, ob, oc, dz, nrm, st, up, res = rest[nst:]
            u_refs, o_refs = (ua, ub, uc), (oa, ob, oc)
            self.group_norm(st_refs, 0, sc, self.area(1), nrm)
            up[...] = jnp.zeros(up.shape, F32)
            st[...] = jnp.zeros(st.shape, F32)
            for which, line, column, row in g.lines():
                up[row : row + g.counts[which], :] = u_refs[which][line, column].astype(F32)

            def make(which, q, lane):
                xh6, put = self.normal(c6, nrm, which, lane), self.scaled(normp, "6", q)

                def work(row):
                    m = wide(msk[pl.ds(row, 16), :])
                    xh = xh6(row)
                    pre = put(xh) + h[pl.ds(row, 16), lane]
                    s = jax.nn.sigmoid(pre)
                    res[pl.ds(row, 16), lane] = m * (pre * s)
                    d = up[pl.ds(row, 16), lane] * m * (s * (1.0 + pre * (1.0 - s)))
                    dz[pl.ds(row, 16), lane] = d
                    return d, d * xh

                return work

            self.sweep(out_width, make, st, (0, 3))
            for which, line, column, row in g.lines():
                o_refs[which][line, column] = res[row : row + g.counts[which], :].astype(BF)

        return call(
            body,
            [(sc, SM), (c6, VM), (h, VM), (normp, VM), (msk, VM)] + [(u, VM) for u in ups] + [(s, VM) for s in sts],
            [(u.shape, BF, VM) for u in ups]
            + [((R, out_width), F32, VM), ((8, out_width), F32, VM), ((8, out_width), F32, VM)],
            [pltpu.VMEM((R, out_width), F32), pltpu.VMEM((R, out_width), F32)],
        )

    def back_six(self, ids, sc, dz, c6, nrm6, sts, normp, msk, c5, nrm5, w, off, rows):
        R = self.R
        layout, arrays = w
        nst, nw = len(sts), len(arrays)
        out_width = c6.shape[1]

        def body(ids, sc, dz, c6, nrm6, normp, msk, c5, nrm5, *rest):
            st_refs, refs = rest[:nst], rest[nst : nst + nw]
            dc, dz5, st, sums, ws, sem = rest[nst + nw :]
            self.load_start(layout, ids, refs, off, rows, ws, sem)
            self.group_sums(st_refs, 0, sc, self.area(1), sums)
            st[...] = jnp.zeros(st.shape, F32)

            def make(which, q, lane):
                xh, back = self.normal(c6, nrm6, which, lane), self.backed(normp, "6", q, nrm6, sums, which, lane)

                def work(row):
                    m = wide(msk[pl.ds(row, 16), :])
                    dc[pl.ds(row, 16), lane] = back(dz[pl.ds(row, 16), lane], xh(row), m).astype(BF)

                return work

            self.sweep(out_width, make)
            self.load_wait(ws, sem)
            dz5[...] = dot_nn(dc[...], ws[...])
            self.through(dz5, c5, nrm5, normp, "5", msk, st)

        return call(
            body,
            [(ids, SM), (sc, SM), (dz, VM), (c6, VM), (nrm6, VM), (normp, VM), (msk, VM), (c5, VM), (nrm5, VM)]
            + [(s, VM) for s in sts]
            + [(a, HB) for a in arrays],
            [((R, out_width), BF, VM), ((R, MID), F32, VM), ((8, MID), F32, VM)],
            [pltpu.VMEM((8, out_width), F32), pltpu.VMEM((out_width, MID), BF), pltpu.SemaphoreType.DMA],
            flops=2 * R * MID * out_width,
        )

    def through(self, dz, c, nrm, normp, name, msk, st, phases=1):
        def make(which, q, lane):
            xhat, put = self.normal(c, nrm, which), self.scaled(normp, name, 0)

            def work(row):
                m = wide(msk[pl.ds(row, 16), :])
                one = two = None
                for phase in range(phases):
                    at = aligned(row + phase * self.R)
                    xh = xhat(at)
                    d = dz[pl.ds(at, 16), :] * slope(put(xh)) * m
                    dz[pl.ds(at, 16), :] = d
                    one = d if one is None else one + d
                    two = d * xh if two is None else two + d * xh
                return one, two

            return work

        self.sweep(MID, make, st, (0, 3))

    def back_five(self, ids, sc, dz5, c5, nrm5, sts, normp, msk, c4, nrm4, w, off, rows):
        R = self.R
        layout, arrays = w
        nst, nw = len(sts), len(arrays)

        def body(ids, sc, dz5, c5, nrm5, normp, msk, c4, nrm4, *rest):
            st_refs, refs = rest[:nst], rest[nst : nst + nw]
            dc, dz4, st, sums, ws, hs, patches, sem = rest[nst + nw :]
            self.load_start(layout, ids, refs, off, rows, ws, sem)
            self.group_sums(st_refs, 0, sc, self.area(1), sums)
            self.clear_halo(hs)
            st[...] = jnp.zeros(st.shape, F32)
            self.own_dc(dz5, c5, nrm5, sums, normp, "5", msk, dc, hs)
            for tap in range(9):
                i, j = divmod(tap, 3)
                self.shifted(hs, patches, tap * MID, 1 - i, 1 - j)
            self.load_wait(ws, sem)
            for tap in range(9):
                part = dot_nt(patches[:, tap * MID : (tap + 1) * MID], ws[tap * MID : (tap + 1) * MID, :])
                if tap == 0:
                    dz4[...] = part
                else:
                    dz4[...] += part
            self.through(dz4, c4, nrm4, normp, "4", msk, st)

        return call(
            body,
            [(ids, SM), (sc, SM), (dz5, VM), (c5, VM), (nrm5, VM), (normp, VM), (msk, VM), (c4, VM), (nrm4, VM)]
            + [(s, VM) for s in sts]
            + [(a, HB) for a in arrays],
            [((R, MID), BF, VM), ((R, MID), F32, VM), ((8, MID), F32, VM)],
            [
                pltpu.VMEM((8, MID), F32),
                pltpu.VMEM((9 * MID, MID), BF),
                pltpu.VMEM((R + 2 * HALO, MID), F32),
                pltpu.VMEM((R, 9 * MID), BF),
                pltpu.SemaphoreType.DMA,
            ],
            flops=2 * 9 * R * MID * MID,
        )

    def own_dc(self, dz, c, nrm, sums, normp, name, msk, dc, hs=None, phases=1):
        def make(which, q, lane):
            xh, back = self.normal(c, nrm, which), self.backed(normp, name, 0, nrm, sums, which)

            def work(row):
                m = wide(msk[pl.ds(row, 16), :])
                for phase in range(phases):
                    at = aligned(row + phase * self.R)
                    v = back(dz[pl.ds(at, 16), :], xh(at), m)
                    dc[pl.ds(at, 16), :] = v.astype(BF)
                    if hs is not None:
                        hs[pl.ds(aligned(row + HALO), 16), :] = v

            return work

        self.sweep(MID, make)

    def back_four(self, ids, sc, dz4, c4, nrm4, sts, normp, msk, dz6, c3, nrm3, cs, nrms, w, off, rows):
        R = self.R
        layout, arrays = w
        nst, nw = len(sts), len(arrays)
        out_width = c3.shape[1]

        def body(ids, sc, dz4, c4, nrm4, normp, msk, dz6_far, c3_far, nrm3, cs_far, nrms, *rest):
            st_refs, refs = rest[:nst], rest[nst : nst + nw]
            dc, dz3, st, sums, ws, dz6, c3, cs, sem, sems = rest[nst + nw :]
            self.load_start(layout, ids, refs, off, rows, ws, sem)
            late = [
                pltpu.make_async_copy(far, held, sems.at[k])
                for k, (far, held) in enumerate(((dz6_far, dz6), (c3_far, c3), (cs_far, cs)))
            ]
            for copy in late:
                copy.start()
            self.group_sums(st_refs, 0, sc, self.area(1), sums)
            st[...] = jnp.zeros(st.shape, F32)
            self.own_dc(dz4, c4, nrm4, sums, normp, "4", msk, dc)
            self.load_wait(ws, sem)
            for q in range(out_width // MID):
                lane = slice(q * MID, (q + 1) * MID)
                dz3[:, lane] = dot_nt(dc[...], ws[lane, :])
            for copy in late:
                copy.wait()

            def make(which, q, lane):
                xhat3, put3 = self.normal(c3, nrm3, which, lane), self.scaled(normp, "3", q)
                xhats, puts = self.normal(cs, nrms, which, lane), self.scaled(normp, "S", q)

                def work(row):
                    xh3, xhs = xhat3(row), xhats(row)
                    d = (dz6[pl.ds(row, 16), lane] + dz3[pl.ds(row, 16), lane]) * slope(put3(xh3) + puts(xhs))
                    d = d * wide(msk[pl.ds(row, 16), :])
                    dz3[pl.ds(row, 16), lane] = d
                    return d, d * xh3, d * xhs

                return work

            self.sweep(out_width, make, st, (0, 3, 11))
            st[8:11, :] = st[0:3, :]

        return call(
            body,
            [(ids, SM), (sc, SM), (dz4, VM), (c4, VM), (nrm4, VM), (normp, VM), (msk, VM)]
            + [(dz6, HB), (c3, HB), (nrm3, VM), (cs, HB), (nrms, VM)]
            + [(s, VM) for s in sts]
            + [(a, HB) for a in arrays],
            [((R, MID), BF, VM), ((R, out_width), F32, VM), ((16, out_width), F32, VM)],
            [pltpu.VMEM((8, MID), F32), pltpu.VMEM((out_width, MID), BF)]
            + [pltpu.VMEM((R, out_width), F32)] * 3
            + [pltpu.SemaphoreType.DMA, pltpu.SemaphoreType.DMA((3,))],
            flops=2 * R * MID * out_width,
        )

    def back_three(self, ids, sc, dz3, c3, nrm3, cs, nrms, sts, normp, msk, c2, nrm2, w, off, rows):
        R = self.R
        layout, arrays = w
        nst, nw = len(sts), len(arrays)
        out_width = c3.shape[1]

        def body(ids, sc, dz3, c3, nrm3, cs, nrms, normp, msk, c2, nrm2, *rest):
            st_refs, refs = rest[:nst], rest[nst : nst + nw]
            dc3_far, dcs_far, dz2, st, sums3, sumss, ws, dc3, dcs, sem, sems = rest[nst + nw :]
            self.load_start(layout, ids, refs, off, rows, ws, sem)
            self.group_sums(st_refs, 0, sc, self.area(1), sums3)
            self.group_sums(st_refs, 8, sc, self.area(1), sumss)
            st[...] = jnp.zeros(st.shape, F32)

            def make(which, q, lane):
                xh3, back3 = self.normal(c3, nrm3, which, lane), self.backed(normp, "3", q, nrm3, sums3, which, lane)
                xhs, backs = self.normal(cs, nrms, which, lane), self.backed(normp, "S", q, nrms, sumss, which, lane)

                def work(row):
                    m = wide(msk[pl.ds(row, 16), :])
                    d = dz3[pl.ds(row, 16), lane]
                    dc3[pl.ds(row, 16), lane] = back3(d, xh3(row), m).astype(BF)
                    dcs[pl.ds(row, 16), lane] = backs(d, xhs(row), m).astype(BF)

                return work

            self.sweep(out_width, make)
            out = [pltpu.make_async_copy(dc3, dc3_far, sems.at[0]), pltpu.make_async_copy(dcs, dcs_far, sems.at[1])]
            for copy in out:
                copy.start()
            self.load_wait(ws, sem)
            dz2[...] = dot_nn(dc3[...], ws[...])
            self.through(dz2, c2, nrm2, normp, "2", msk, st)
            for copy in out:
                copy.wait()

        return call(
            body,
            [(ids, SM), (sc, SM), (dz3, VM), (c3, VM), (nrm3, VM), (cs, VM), (nrms, VM), (normp, VM), (msk, VM)]
            + [(c2, VM), (nrm2, VM)]
            + [(s, VM) for s in sts]
            + [(a, HB) for a in arrays],
            [((R, out_width), BF, HB), ((R, out_width), BF, HB), ((R, MID), F32, VM), ((8, MID), F32, VM)],
            [
                pltpu.VMEM((8, out_width), F32),
                pltpu.VMEM((8, out_width), F32),
                pltpu.VMEM((out_width, MID), BF),
                pltpu.VMEM((R, out_width), BF),
                pltpu.VMEM((R, out_width), BF),
                pltpu.SemaphoreType.DMA,
                pltpu.SemaphoreType.DMA((2,)),
            ],
            flops=2 * R * MID * out_width,
        )

    SHIFTS = ((0, 0), (0, 1), (1, 0), (1, 1))

    def back_two(self, ids, sc, dz2, c2, nrm2, sts, normp, msk, c1, nrm1, w, off, rows):
        R = self.R
        layout, arrays = w
        nst, nw = len(sts), len(arrays)

        def body(ids, sc, dz2, c2, nrm2, normp, msk, c1, nrm1, *rest):
            st_refs, refs = rest[:nst], rest[nst : nst + nw]
            dc, dz1, st, sums, ws, hs, patches, sem = rest[nst + nw :]
            self.load_start(layout, ids, refs, off, rows, ws, sem)
            self.group_sums(st_refs, 0, sc, self.area(1), sums)
            self.clear_halo(hs)
            st[...] = jnp.zeros(st.shape, F32)
            self.own_dc(dz2, c2, nrm2, sums, normp, "2", msk, dc, hs)
            for k, (fwd_r, fwd_c) in enumerate(self.SHIFTS):
                self.shifted(hs, patches, k * MID, fwd_r, fwd_c)
            self.load_wait(ws, sem)
            seen = set()
            for tap in range(9):
                phase, back_r, back_c = self.tap_two(tap)
                k = self.SHIFTS.index((back_r, back_c))
                part = dot_nt(patches[:, k * MID : (k + 1) * MID], ws[tap * MID : (tap + 1) * MID, :])
                if phase in seen:
                    dz1[phase * R : (phase + 1) * R, :] += part
                else:
                    dz1[phase * R : (phase + 1) * R, :] = part
                seen.add(phase)
            self.through(dz1, c1, nrm1, normp, "1", msk, st, 4)

        return call(
            body,
            [(ids, SM), (sc, SM), (dz2, VM), (c2, VM), (nrm2, VM), (normp, VM), (msk, VM), (c1, VM), (nrm1, VM)]
            + [(s, VM) for s in sts]
            + [(a, HB) for a in arrays],
            [((R, MID), BF, VM), ((4 * R, MID), F32, VM), ((8, MID), F32, VM)],
            [
                pltpu.VMEM((8, MID), F32),
                pltpu.VMEM((9 * MID, MID), BF),
                pltpu.VMEM((R + 2 * HALO, MID), F32),
                pltpu.VMEM((R, 4 * MID), BF),
                pltpu.SemaphoreType.DMA,
            ],
            flops=2 * 9 * R * MID * MID,
        )

    def back_one(self, sc, dz1, c1, nrm1, sts, normp, msk):
        R = self.R
        nst = len(sts)

        def body(sc, dz1, c1, nrm1, normp, msk, *rest):
            st_refs = rest[:nst]
            dc, sums = rest[nst:]
            self.group_sums(st_refs, 0, sc, self.area(2), sums)
            self.own_dc(dz1, c1, nrm1, sums, normp, "1", msk, dc, None, 4)

        return call(
            body,
            [(sc, SM), (dz1, VM), (c1, VM), (nrm1, VM), (normp, VM), (msk, VM)] + [(s, VM) for s in sts],
            [((4 * R, MID), BF, VM)],
            [pltpu.VMEM((8, MID), F32)],
        )[0]

    def input_grad(self, ids, dc1, dcs, w1, off1, rows1, ids_s, ws, offs, rowss, pictures):
        R = self.R
        g = self.g
        lay1, arr1 = w1
        lays, arrs = ws
        n1, ns = len(arr1), len(arrs)
        width = pictures[0].shape[3]
        out_width = dcs.shape[1]

        def body(ids, ids_s, dc1, dcs, *rest):
            r1, rs = rest[:n1], rest[n1 : n1 + ns]
            ga, gb, gc, k1, ka, kb, dx, sem = rest[n1 + ns :]
            g_refs = (ga, gb, gc)
            self.load_start(lay1, ids, r1, off1, rows1, k1, sem.at[0])
            self.load_start(lays, ids_s, rs, offs, rowss, ka, sem.at[1])
            self.load_start(lays, ids_s, rs, offs + rowss, rowss, kb, sem.at[2])
            self.load_wait(k1, sem.at[0])
            self.load_wait(ka, sem.at[1])
            self.load_wait(kb, sem.at[2])
            for phase in range(4):
                for q in range(width // MID):
                    lane = slice(q * MID, (q + 1) * MID)
                    part = dot_nt(dc1[phase * R : (phase + 1) * R, :], k1[lane, :])
                    if phase == 0:
                        part = part + dot_nn(dcs[...], (ka, kb)[q][...])
                    dx[phase * R : (phase + 1) * R, lane] = part
            for which, line, column, row in g.lines():
                for phase in range(4):
                    odd, second = divmod(phase, 2)
                    base = phase * R + row
                    g_refs[which][2 * line + odd, 2 * column + second] = dx[base : base + g.counts[which], :].astype(BF)

        return call(
            body,
            [(ids, SM), (ids_s, SM), (dc1, VM), (dcs, VM)] + [(a, HB) for a in arr1] + [(a, HB) for a in arrs],
            [(p.shape, BF, VM) for p in pictures],
            [
                pltpu.VMEM((width, MID), BF),
                pltpu.VMEM((out_width, MID), BF),
                pltpu.VMEM((out_width, MID), BF),
                pltpu.VMEM((4 * R, width), F32),
                pltpu.SemaphoreType.DMA((3,)),
            ],
            flops=2 * (4 * R * width * MID + R * width * out_width),
        )


    def gradient(self, ids, chains, kind, ins, parts, heights, held=None, extra=None):
        fresh = held is None
        arrays, start = ([], [0] * len(chains)) if fresh else held
        outs, spans = [], []
        for c, places_list in enumerate(chains):
            size = sum(split[c] for _, split in parts)
            for places in places_list:
                outs.append(((len(places), heights[c], MID), BF, HB))
                spans.append((start[c], size))
        count, pieces = len(ins), len(outs)

        def body(ids, *rest):
            refs, rest = rest[:count], rest[count + len(arrays) :]
            out_refs, rest = rest[:pieces], rest[pieces:]
            bufs, rest = rest[: len(parts)], rest[len(parts) :]
            sems, tail = rest[0], rest[1:]
            offs = list(start)
            for part, (buf, (rows, split)) in enumerate(zip(bufs, parts)):
                kind(part, refs, buf, tail)
                self.store_start(chains, ids, buf, rows, split, offs, out_refs, sems)
                offs = [o + t for o, t in zip(offs, split)]
            self.store_wait(out_refs, sems, spans)

        tall = [rows * self.blocks if self.blocks > 1 else rows for rows, _ in parts]
        scratch = [pltpu.VMEM((t, MID), BF) for t in tall]
        scratch.append(pltpu.SemaphoreType.DMA((pieces,)))
        scratch.extend(extra or [])
        made = call(
            body,
            [(ids, SM)] + [(a, VM) for a in ins] + [(a, HB) for a in arrays],
            outs,
            scratch,
            flops=2 * self.R * sum(tall) * MID,
            aliases={1 + count + i: i for i in range(len(arrays))},
        )
        ends = [at + sum(split[c] for _, split in parts) for c, at in enumerate(start)]
        return list(made), ends

    def grad_outer(self, ids, chains, pairs, parts, heights, held=None):
        ins = []
        for left, right in pairs:
            ins += [left, right]

        def kind(part, refs, buf, tail):
            left, right = refs[2 * part], refs[2 * part + 1]
            for q in range(left.shape[1] // MID):
                buf[q * MID : (q + 1) * MID, :] = dot_tn(left[:, q * MID : (q + 1) * MID], right[...]).astype(BF)

        return self.gradient(ids, chains, kind, ins, parts, heights, held)

    def grad_short(self, ids, chains, a2, dc3, dcs, xp, parts, heights, held=None):
        R = self.R

        def kind(part, refs, buf, tail):
            a2, dc3, dcs, xp = refs
            left = dc3 if part == 0 else dcs
            for q in range(left.shape[1] // MID):
                cols = left[:, q * MID : (q + 1) * MID]
                right = a2[...] if part == 0 else xp[0:R, (part - 1) * MID : part * MID]
                buf[q * MID : (q + 1) * MID, :] = dot_tn(cols, right).astype(BF)

        return self.gradient(ids, chains, kind, [a2, dc3, dcs, xp], parts, heights, held)

    def grad_taps(self, ids, chains, act, dc, parts, heights, stride, held=None):
        R = self.R

        def kind(part, refs, buf, tail):
            act, dc = refs
            hs, patches = tail
            self.clear_halo(hs)

            for row in range(0, R, 16):
                hs[HALO + row : HALO + row + 16, :] = dc[row : row + 16, :].astype(F32)
            if stride == 1:
                shifts = [(1 - tap // 3, 1 - tap % 3) for tap in range(9)]
            else:
                shifts = list(self.SHIFTS)
            for k, (sr, sc_) in enumerate(shifts):
                self.shifted(hs, patches, k * MID, sr, sc_)
            for tap in range(9):
                if stride == 1:
                    left, k = act[...], tap
                else:
                    phase, back_r, back_c = self.tap_two(tap)
                    left, k = act[phase * R : (phase + 1) * R, :], self.SHIFTS.index((back_r, back_c))
                buf[tap * MID : (tap + 1) * MID, :] = dot_tn(left, patches[:, k * MID : (k + 1) * MID]).astype(BF)

        wide_cols = 9 if stride == 1 else 4
        extra = [pltpu.VMEM((R + 2 * HALO, MID), F32), pltpu.VMEM((R, wide_cols * MID), BF)]
        return self.gradient(ids, chains, kind, [act, dc], parts, heights, held, extra)

    def grad_first(self, ids, chains, xp, dc1, sums, parts, heights):
        def kind(part, refs, buf, tail):
            if part == 0:
                xp, dc1 = refs[0], refs[1]
                for q in range(xp.shape[1] // MID):
                    buf[q * MID : (q + 1) * MID, :] = dot_tn(xp[:, q * MID : (q + 1) * MID], dc1[...]).astype(BF)
            else:
                row = 0
                for first in (3, 0):
                    for name in ("1", "2", "3", "S", "4", "5", "6"):
                        ref = refs[2 + ("1", "2", "3", "4", "5", "6").index("3" if name == "S" else name)]
                        at = first + (8 if name == "S" else 0)
                        total = ref[at : at + 1, :] + ref[at + 1 : at + 2, :] + ref[at + 2 : at + 3, :]
                        for q in range(ref.shape[1] // MID):
                            piece = total[:, q * MID : (q + 1) * MID]
                            buf[row * 16 : row * 16 + 16, :] = jnp.broadcast_to(piece, (16, MID)).astype(BF)
                            row += 1

        return self.gradient(ids, chains, kind, [xp, dc1] + list(sums), parts, heights)


def adam_step(weight, moment_one, moment_two, gradient, step_rate, decay_rate):
    first_new = 0.5 * moment_one + 0.5 * gradient
    second_new = 0.5 * moment_two + 0.5 * gradient * gradient
    correct = 1.0 - 0.5**STEP
    update = first_new / correct / (jnp.sqrt(second_new / correct) + 1e-08) + decay_rate * weight
    return (weight - step_rate * update, first_new, second_new)


BOTH = ("dp", "bn")


def orders(total):
    count = total.bit_length() - 1
    if count == 5:
        return [4, 2, 3, 1, 0], [4, 1, 3, 2, 0], [2, 1, 4, 3, 0]
    return (list(range(count))[::-1],) * 3


class Order:
    def __init__(self, free=False):
        self.last, self.free = None, free

    def hold(self, value):
        if self.last is None:
            return value
        return lax.optimization_barrier((value, self.last))[0]

    def mark(self, value):
        self.last = None if self.free else value


class Gather:
    def __init__(self, seq, swap, buf, order):
        self.seq, self.swap, self.bits = seq, swap, list(order)
        self.held, self.places = buf[None], [0]
        self.go()

    def go(self):
        bit = self.bits.pop(0)
        self.got = self.swap(self.held, bit)
        self.there = [r ^ (1 << bit) for r in self.places]

    def step(self):
        self.held = jnp.concatenate([self.held, self.seq.hold(self.got)])
        self.places = self.places + self.there
        self.seq.mark(self.held)
        self.go()

    def result(self):
        return [self.places, self.there], [self.held, self.got]


class Scatter:
    def __init__(self, seq, swap, pieces, order):
        self.seq, self.swap, self.bits = seq, swap, list(order)
        self.kept = [pieces[0]]
        self.got = swap(pieces[1], self.bits.pop(0))

    @staticmethod
    def places(order):
        kept = [0]
        for bit in reversed(order[1:]):
            kept = kept + [r ^ (1 << bit) for r in kept]
        return [kept, [r ^ (1 << order[0]) for r in kept]]

    def step(self):
        kept = self.kept + [self.seq.hold(self.got)]
        half = kept[0].shape[0] // 2
        sent = sum([k[half:].astype(F32) for k in kept[1:]], kept[0][half:].astype(F32)).astype(BF)
        self.kept = [k[:half] for k in kept]
        self.seq.mark(sent)
        self.got = self.swap(sent, self.bits.pop(0))

    def result(self):
        kept = self.kept + [self.seq.hold(self.got)]
        return sum([k[0].astype(F32) for k in kept[1:]], kept[0][0].astype(F32))


def gentle(total):
    if total == 32:
        return [1, 4, 3, 2, 0], [1, 2, 4, 3, 0]
    return orders(total)[:2]


def backward_orders(total):
    if total == 32:
        return [0, 2, 3, 4, 1], [0, 3, 2, 1, 4], [0, 1, 2, 3, 4], [0, 3, 1, 2, 4]
    return [orders(total)[0][::-1]] * 4


def on_device(*args):
    slots_inside = (1, 2, 0, 3)
    images = [jnp.transpose(args[k], slots_inside) for k in (0, 2, 1)]
    lives = (args[3], args[5], args[4])
    ups = [jnp.transpose(args[k], slots_inside) for k in (6, 8, 7)]
    params, firsts, seconds = args[9:17], args[17:25], args[25:33]
    groups, members = lax.axis_size("dp"), lax.axis_size("bn")
    total = groups * members
    pos_dp, pos_bn = lax.axis_index("dp"), lax.axis_index("bn")
    me = pos_dp * members + pos_bn
    grid = Grid([p.shape[2] for p in images], [u.shape[1] for u in ups])

    seq = Order()
    low = [params[0].astype(BF)]
    seq.mark(low[0])
    low += [seq.hold(p).astype(BF) for p in params[1:]]
    short_t = low[3].T
    shards = {
        "1": low[0],
        "2": low[1],
        "3": low[2].T,
        "S": jnp.concatenate([short_t[:, :MID], short_t[:, MID:]], axis=0),
        "4": low[4],
        "5": low[5],
        "6": low[6].T,
    }
    unit = {"1": 1, "2": 1, "3": 1, "S": 2, "4": 1, "5": 1, "6": 1}
    rows = {k: v.shape[0] // unit[k] for k, v in shards.items()}
    direct = all(r % 16 == 0 for r in rows.values()) and params[7].shape[0] == MID
    blocks = total if direct else 1
    if not direct:
        rows = {k: r * total for k, r in rows.items()}
    dev = Device(grid, blocks, members)

    spot = jnp.stack([pos_dp, pos_bn]).astype(jnp.int32)
    far = jnp.zeros((1,), jnp.int32)
    near = me.reshape(1).astype(jnp.int32) if direct else far

    def offsets(names):
        where, at = {}, 0
        for k in names:
            where[k] = at
            at += rows[k] * unit[k]
        return where, at

    def packed(names, with_norm=False):
        parts = [shards[k] for k in names]
        if with_norm:
            parts.append(jnp.broadcast_to(low[7].reshape(1, MID), (16, MID)))
        return jnp.concatenate(parts, axis=0) if len(parts) > 1 else parts[0]

    def gather(names):
        buf = packed(names)
        full = lax.all_gather(buf, BOTH, axis=0, tiled=True).reshape(total, buf.shape[0], MID)
        if direct:
            return ([(0, list(range(total)))], [full]), offsets(names)[0]
        pieces, spot_row = [], 0
        for k in names:
            for _ in range(unit[k]):
                r = rows[k] // total
                pieces.append(full[:, spot_row : spot_row + r, :].reshape(rows[k], MID))
                spot_row += r
        return ([(0, [0])], [jnp.concatenate(pieces, axis=0)[None]]), offsets(names)[0]

    def swap(array, bit):
        return lax.ppermute(array, BOTH, [(i, i ^ (1 << bit)) for i in range(total)])

    def exchange(stat):
        return [stat] + [
            lax.ppermute(stat, "bn", [(i, i ^ k) for i in range(members)]) for k in range(1, members)
        ]

    first, second, third = orders(total)

    def chains(buf, cuts, seq):
        made, at = [], 0
        for height, order in cuts:
            made.append((at, Gather(seq, swap, buf[at : at + height], order)))
            at += height
        return made

    def steps(made):
        for _, chain in made:
            chain.step()

    def results(made):
        layout, arrays = [], []
        for at, chain in made:
            for places, array in zip(*chain.result()):
                layout.append((at, places))
                arrays.append(array)
        return layout, arrays

    if direct:
        r2 = rows["2"] // 48 * 16
        quiet_x, _ = gentle(total)
        free = Order(True)
        g_one = chains(packed(["1"]), [(rows["1"], first)], free)
        buf2, buf6 = packed(["2"], True), packed(["6"])
        wb, at_b = gather(["3", "S", "4", "5"])
        steps(g_one)
        later = lax.optimization_barrier((buf2, g_one[0][1].held))[0]
        g_two = chains(later, [(r2, first), (r2, second), (rows["2"] - 2 * r2 + 16, third)], free)
        for _ in range(3):
            steps(g_one)
        for _ in range(4):
            steps(g_two)
        xp, msk, sc = dev.prepare(spot, lives, images)
        c1, st1 = dev.conv_one(near, sc, xp, msk, results(g_one), 0, rows["1"])
        seq.mark(st1)
        st1 = exchange(st1)
        g_six = chains(seq.hold(buf6), [(rows["6"], quiet_x)], seq)
        a1, nrm1, c2, st2, normp = dev.conv_two(
            near, sc, c1, st1, None, seq.hold(msk), results(g_two), 0, rows["2"], rows["2"]
        )
        seq.mark(st2)
        st2 = exchange(st2)
        steps(g_six)
        seq.mark((seq.last, *st2[1:]))
        cs, sts = dev.conv_short(far, sc, xp, seq.hold(msk), wb, at_b["S"], rows["S"])
        seq.mark(sts)
        steps(g_six)
        a2, nrm2, c3, st3 = dev.conv_expand(
            far, sc, c2, st2, normp, seq.hold(msk), wb, at_b["3"], rows["3"], "2", sts
        )
        st3 = exchange(st3)
        seq.mark(tuple(st3))
        steps(g_six)
        w1, w2 = results(g_one), results(g_two)
        w3 = w4 = w5 = wb
        at_3 = at_b
    else:
        w1, w2, w4, w5, w6 = [gather([k])[0] for k in ("1", "2", "4", "5", "6")]
        w3, at_3 = gather(["3", "S"])
        xp, msk, sc = dev.prepare(spot, lives, images)
        c1, st1 = dev.conv_one(near, sc, xp, msk, w1, 0, rows["1"])
        normp = lax.all_gather(low[7], BOTH, axis=0, tiled=True).astype(F32).reshape(32, MID)
        a1, nrm1, c2, st2 = dev.conv_two(near, sc, c1, exchange(st1), normp, msk, w2, 0, rows["2"])
        cs, sts = dev.conv_short(far, sc, xp, msk, w3, at_3["S"], rows["S"])
        a2, nrm2, c3, st3 = dev.conv_expand(
            far, sc, c2, exchange(st2), normp, msk, w3, at_3["3"], rows["3"], "2", sts
        )
        st3 = exchange(st3)
        at_b = {"4": 0, "5": 0}
    h, hb, nrm3, nrms, c4, st4 = dev.conv_four(
        far, sc, c3, cs, st3, normp, msk, w4, at_b["4"], rows["4"]
    )
    if direct:
        seq.mark(st4)
        st4 = exchange(st4)
        steps(g_six)
        w6 = results(g_six)
    else:
        st4 = exchange(st4)
    a4, nrm4, c5, st5 = dev.conv_five(far, sc, c4, st4, normp, msk, w5, at_b["5"], rows["5"])
    a5, nrm5, c6, st6 = dev.conv_expand(near, sc, c5, exchange(st5), normp, msk, w6, 0, rows["6"], "5")
    oc, oa, ob, dz6, nrm6, su6 = dev.finish(sc, c6, h, exchange(st6), normp, msk, ups)

    def scatter(piece, heights):
        if not direct:
            parts, spot_row = [], 0
            for height in heights:
                parts.append(piece[0, spot_row : spot_row + height].reshape(total, height // total, MID))
                spot_row += height
            piece = jnp.concatenate(parts, axis=1)
        owned = lax.psum_scatter(piece.reshape(-1, MID), BOTH, scatter_dimension=0, tiled=True)
        return owned.astype(F32)

    def cut(owned, heights):
        parts, spot_row = [], 0
        for height in heights:
            height = height if direct else height // total
            parts.append(owned[spot_row : spot_row + height])
            spot_row += height
        return parts

    whole = [[list(range(total)) if direct else [0]]]
    order_a, order_b, order_two, order_one = backward_orders(total)

    def halves(k):
        if not direct:
            return [rows[k]]
        one = rows[k] // 32 * 16
        return [rows[k] - one, one]

    pair = [order_a, order_b] if direct else [None]
    pair_places = [Scatter.places(order) for order in pair] if direct else whole
    two_places = [Scatter.places(order_two)] if direct else whole
    single_places = [Scatter.places(order_one)] if direct else whole

    def sums(made, orders_used):
        if not direct:
            return []
        return [Scatter(seq, swap, made[0][2 * c : 2 * c + 2], order) for c, order in enumerate(orders_used)]

    def advance(made):
        for chain in made:
            chain.step()

    dc6, dz5, su5 = dev.back_six(
        near, sc, dz6, c6, nrm6, exchange(su6), normp, msk, c5, nrm5, w6, 0, rows["6"]
    )
    seq.mark(su5)
    high = [rows["6"] + rows["5"]]
    g65 = dev.grad_outer(seq.hold(far), whole, [(dc6, a5)], [(rows["6"], [rows["6"]])], high)
    seq.mark(g65[0][0])
    dc5, dz4, su4 = dev.back_five(
        far, sc, dz5, c5, nrm5, exchange(su5), normp, seq.hold(msk), c4, nrm4, w5, at_b["5"], rows["5"]
    )
    seq.mark(su4)
    g65 = dev.grad_taps(seq.hold(far), whole, a4, dc5, [(rows["5"], [rows["5"]])], high, 1, g65)
    seq.mark(g65[0][0])
    hts65 = [rows["6"], rows["5"]]
    owned65 = scatter(g65[0][0], hts65)

    dc4, dz3, su3 = dev.back_four(
        far, sc, dz4, c4, nrm4, exchange(su4), normp, seq.hold(msk), dz6, c3, nrm3, cs, nrms, w4, at_b["4"], rows["4"]
    )
    seq.mark(su3)
    part4, part3 = (rows["4"], halves("4")), (rows["3"], halves("3"))
    mid = [a + 3 * b for a, b in zip(part4[1], part3[1])]
    g43 = dev.grad_outer(seq.hold(near), pair_places, [(hb, dc4)], [part4], mid)
    seq.mark(g43[0][0])
    dc3, dcs, dz2, su2 = dev.back_three(
        far, sc, dz3, c3, nrm3, cs, nrms, exchange(su3), normp, seq.hold(msk), c2, nrm2, w3, at_3["3"], rows["3"]
    )
    seq.mark(su2)
    g43 = dev.grad_short(seq.hold(near), pair_places, a2, dc3, dcs, xp, [part3] * 3, mid, g43)
    seq.mark(g43[0][0])
    s43 = sums(g43, pair)
    dc2, dz1, su1 = dev.back_two(
        near, sc, dz2, c2, nrm2, exchange(su2), normp, seq.hold(msk), c1, nrm1, w2, 0, rows["2"]
    )
    seq.mark(su1)
    advance(s43)
    g2 = dev.grad_taps(seq.hold(near), two_places, a1, dc2, [(rows["2"], [rows["2"]])], [rows["2"]], 2)
    seq.mark(g2[0][0])
    s2 = sums(g2, [order_two])
    dc1 = dev.back_one(sc, dz1, c1, nrm1, exchange(su1), normp, seq.hold(msk))
    seq.mark(dc1)
    advance(s2)
    advance(s43)
    parts = [(rows["1"], [rows["1"]])] + ([(16, [16])] if direct else [])
    g1 = dev.grad_first(
        seq.hold(near), single_places, xp, dc1, (su1, su2, su3, su4, su5, su6), parts, [sum(p for p, _ in parts)]
    )
    seq.mark(g1[0][0])
    s1 = sums(g1, [order_one])
    grads = dev.input_grad(seq.hold(near), dc1, dcs, w1, 0, rows["1"], far, w3, at_3["S"], rows["S"], images)
    seq.mark(grads[0])
    gc_, ga_, gb_ = grads
    if direct:
        advance(s1)
        advance(s43)
        advance(s2)
        advance(s1)
        advance(s43)
        advance(s2)
        advance(s1)
        advance(s2)
        advance(s1)
        got43 = [chain.result() for chain in s43]
        got2 = [chain.result() for chain in s2]
        last = s1[0].result()
    else:
        got43 = [scatter(g43[0][0], [rows["4"]] + [rows["3"]] * 3)]
        got2 = [scatter(g2[0][0], [rows["2"]])]
        last = scatter(g1[0][0], [rows["1"]])
    cuts = [cut(owned, [part4[1][c]] + [part3[1][c]] * 3) for c, owned in enumerate(got43)]
    o4, o3, osa, osb = [jnp.concatenate(p, axis=0) if len(p) > 1 else p[0] for p in zip(*cuts)]
    o2 = jnp.concatenate(got2, axis=0) if len(got2) > 1 else got2[0]
    o6, o5 = cut(owned65, hts65)
    o1 = last[: rows["1"]] if direct else last
    if direct:
        onorm = last[rows["1"]]
    else:

        def three(stat, at):
            return jnp.sum(stat[at : at + 3], axis=0)

        vec = [three(su1, 3), three(su2, 3), three(su3, 3), three(su3, 11), three(su4, 3), three(su5, 3), three(su6, 3)]
        vec += [three(su1, 0), three(su2, 0), three(su3, 0), three(su3, 8), three(su4, 0), three(su5, 0), three(su6, 0)]
        onorm = lax.psum_scatter(jnp.concatenate(vec), BOTH, scatter_dimension=0, tiled=True)
    owned = (o1, o2, o3.T, jnp.concatenate([osa, osb], axis=1).T, o4, o5, o6.T, onorm)
    stepped = []
    for k in range(8):
        rate, decay = (RATE_CONV, DECAY_CONV) if k < 7 else (RATE_NORM, 0.0)
        stepped.extend(adam_step(params[k], firsts[k], seconds[k], owned[k], rate, decay))
    images_out = [jnp.transpose(a, (2, 0, 1, 3)) for a in (oc, oa, ob, gc_, ga_, gb_)]
    order_out = [images_out[k] for k in (0, 2, 1, 3, 5, 4)]
    return (*order_out, *stepped)


def solution(mesh):
    batch = P(BOTH, None, None, None)
    by_row, by_col, flat = P(BOTH, None), P(None, BOTH), P(BOTH)
    weights = (by_row, by_row, by_col, by_col, by_row, by_row, by_col, flat)
    triple = tuple(spec for spec in weights for _ in range(3))
    return jax.shard_map(
        on_device,
        mesh=mesh,
        in_specs=(batch,) * 3 + (P(),) * 3 + (batch,) * 3 + weights * 3,
        out_specs=(batch,) * 6 + triple,
        check_vma=False,
    )
```
